512 devices in a mesh: tiles: 64 (over z, y), depth: 8 (over x, core).
Axes of the slice: x: 4, y: 4, z: 16, core: 2. Of those that a mesh axis runs over, the one named last changes fastest.
Arguments:
- thickness: float32 [16, 64, 128, 128], P('depth', 'tiles'), may hold values from 0.5 to 1.5
- u_layer: float32 [16, 64, 128, 128], P('depth', 'tiles'), may hold values from -4 to 4
- v_layer: float32 [16, 64, 128, 128], P('depth', 'tiles'), may hold values from -4 to 4
- tracers: float32 [6, 16, 64, 128, 128], P(None, 'depth', 'tiles'), may hold values from -6 to 6
- sea_level: float32 [64, 128, 128], P('tiles'), may hold values from -3 to 3
- u_column: float32 [64, 128, 128], P('tiles'), may hold values from -4 to 4
- v_column: float32 [64, 128, 128], P('tiles'), may hold values from -4 to 4
- wet_cells: int32 [64, 128, 128], P('tiles'), may hold values 0 or 1
- levels: int32 [64, 128, 128], P('tiles'), may hold values from 1 to 16
Outputs:
- tracers_new: float32 [6, 16, 64, 128, 128], P(None, 'depth', 'tiles')
- surface_new: float32 [64, 128, 128], P('tiles')
- east_new: float32 [64, 128, 128], P('tiles')
- north_new: float32 [64, 128, 128], P('tiles')
The draws below stay inside these ranges and needn't reach their ends.
All inputs are finite; a program needn't handle non-finite values. No bound on the sum of `wet_cells` on one device may be relied on, other than what follows from the above.
Results may differ from the reference program's by a relative error of at most 0.0003.
Values sent between devices are 32-bit elements; how exact they have to be, the bound alone decides.
A program may use at most 64 MiB of HBM per device.

```python
import jax
import jax.numpy as jnp

NTR = 6
CX = 128
CY = 128
TROWS = 8
NSUB = 8
NT = 64
NZ = 16


def plant(drawn, stream_key, least, top_value):
    shape = drawn.shape
    place = [jax.random.randint(jax.random.fold_in(stream_key, axis), (), 0, shape[axis]) for axis in range(len(shape))]
    drawn = drawn.at[tuple(place)].set(least)
    longest = shape.index(max(shape))
    place[longest] = (place[longest] + 1) % shape[longest]
    return drawn.at[tuple(place)].set(top_value)


def level_of(stream_key, shape, cuts, smallest, top_value):
    def one(position, parts):
        steps = jax.random.uniform(jax.random.fold_in(jax.random.fold_in(stream_key, 6), position), (parts,), jnp.float32, smallest / len(cuts), top_value / len(cuts))
        return jnp.repeat(jnp.exp(steps), shape[position] // parts).reshape((-1,) + (1,) * (len(shape) - position - 1))

    level = one(*cuts[0])
    for cut in cuts[1:]:
        level = level * one(*cut)
    return level


def noise(own_key, shape, width, bound, cuts=(), kind=jnp.bfloat16):
    values = width * jax.random.normal(own_key, shape, jnp.float32)
    if cuts:
        values = values * level_of(own_key, shape, cuts, -0.22, 0.18)
    return jnp.clip(values, -bound, bound).astype(kind)


def setup_inputs(seed: int = 0) -> dict:
    key_of = jax.random.split(jax.random.key(seed), 10)
    return {
        "thickness": jnp.clip(0.5 + 1.0 * jax.random.uniform(key_of[0], (NZ, NT, CY, CX), jnp.float32) ** level_of(key_of[0], (NZ, NT, CY, CX), ((0, 8), (1, 64)), -0.2, 0.2), 0.5, 1.5),
        "u_layer": noise(key_of[1], (NZ, NT, CY, CX), 1.0, 4.0, ((0, 8), (1, 64)), jnp.float32),
        "v_layer": noise(key_of[2], (NZ, NT, CY, CX), 1.0, 4.0, ((0, 8), (1, 64)), jnp.float32),
        "tracers": noise(key_of[3], (NTR, NZ, NT, CY, CX), 1.0, 6.0, ((1, 8), (2, 64)), jnp.float32),
        "sea_level": noise(key_of[4], (NT, CY, CX), 0.5, 3.0, ((0, 64),), jnp.float32),
        "u_column": noise(key_of[5], (NT, CY, CX), 1.0, 4.0, ((0, 64),), jnp.float32),
        "v_column": noise(key_of[6], (NT, CY, CX), 1.0, 4.0, ((0, 64),), jnp.float32),
        "wet_cells": plant((jax.random.randint(key_of[7], (NT, CY, CX), 0, 10) < 9).astype(jnp.int32), jax.random.fold_in(key_of[7], 1), 0, 1),
        "levels": plant(jax.random.randint(key_of[8], (NT, CY, CX), 1, NZ + 1), jax.random.fold_in(key_of[8], 1), 1, NZ).astype(jnp.int32),
    }


gravity = 1.0
substep_time = 0.45
tracer_time = 0.1


def to_grid(array_in):
    leading = array_in.shape[:-3]
    rank_lead = len(leading)
    columns = NT // TROWS
    shaped = array_in.reshape(leading + (columns, TROWS, CY, CX))
    shaped = jnp.moveaxis(shaped, rank_lead, rank_lead + 2)
    return shaped.reshape(leading + (TROWS * CY, columns * CX))


def from_grid(array_in):
    leading = array_in.shape[:-2]
    rank_lead = len(leading)
    columns = NT // TROWS
    shaped = array_in.reshape(leading + (TROWS, CY, columns, CX))
    shaped = jnp.moveaxis(shaped, rank_lead + 2, rank_lead)
    return shaped.reshape(leading + (NT, CY, CX))


def eastward(array_in):
    return jnp.roll(array_in, -1, axis=-1)


def westward(array_in):
    return jnp.roll(array_in, 1, axis=-1)


def northward(array_in):
    return jnp.concatenate([array_in[..., 1:, :], jnp.zeros_like(array_in[..., :1, :])], axis=-2)


def southward(array_in):
    return jnp.concatenate([jnp.zeros_like(array_in[..., :1, :]), array_in[..., :-1, :]], axis=-2)


def reference(thickness, u_layer, v_layer, tracers, sea_level, u_column, v_column, wet_cells, levels):
    layer_depth = to_grid(thickness)
    u_grid = to_grid(u_layer)
    v_grid = to_grid(v_layer)
    wet_grid = to_grid(wet_cells).astype(jnp.float32)
    level_grid = to_grid(levels)
    layer_ids = jnp.arange(NZ, dtype=jnp.int32)[:, None, None]
    active = (layer_ids < level_grid[None]).astype(jnp.float32) * wet_grid[None]
    face_east = 0.5 * (layer_depth + eastward(layer_depth)) * (active * eastward(active))
    face_north = 0.5 * (layer_depth + northward(layer_depth)) * (active * northward(active))
    flux_east = u_grid * face_east
    flux_north = v_grid * face_north
    column_east = jnp.sum(flux_east, axis=0)
    column_north = jnp.sum(flux_north, axis=0)
    depth_east = jnp.sum(face_east, axis=0)
    depth_north = jnp.sum(face_north, axis=0)
    wet_east = wet_grid * eastward(wet_grid)
    wet_north = wet_grid * northward(wet_grid)
    surface = to_grid(sea_level)
    trans_east = to_grid(u_column)
    trans_north = to_grid(v_column)
    coupling = gravity / NZ
    for substep in range(NSUB):
        surface = surface - substep_time * wet_grid * (trans_east - westward(trans_east) + trans_north - southward(trans_north))
        trans_east = wet_east * (trans_east + substep_time * (-coupling * depth_east * (eastward(surface) - surface) + column_east / NZ - trans_east))
        trans_north = wet_north * (trans_north + substep_time * (-coupling * depth_north * (northward(surface) - surface) + column_north / NZ - trans_north))
    final_east = flux_east + face_east * (trans_east - column_east / NZ)[None]
    final_north = flux_north + face_north * (trans_north - column_north / NZ)[None]
    divergence = final_east - westward(final_east) + final_north - southward(final_north)
    suffix = jnp.cumsum(divergence[::-1], axis=0)[::-1]
    lift_bottom = divergence - suffix
    lift_top = jnp.where(layer_ids == 0, 0.0, -suffix)
    tracer_grid = to_grid(tracers)
    tracer_below = jnp.concatenate([tracer_grid[:, 1:], jnp.zeros_like(tracer_grid[:, :1])], axis=1)
    tracer_above = jnp.concatenate([jnp.zeros_like(tracer_grid[:, :1]), tracer_grid[:, :-1]], axis=1)
    vert_bottom = jnp.maximum(lift_bottom, 0.0) * tracer_below + jnp.minimum(lift_bottom, 0.0) * tracer_grid
    vert_top = jnp.maximum(lift_top, 0.0) * tracer_grid + jnp.minimum(lift_top, 0.0) * tracer_above
    side_east = jnp.maximum(final_east, 0.0) * tracer_grid + jnp.minimum(final_east, 0.0) * eastward(tracer_grid)
    side_north = jnp.maximum(final_north, 0.0) * tracer_grid + jnp.minimum(final_north, 0.0) * northward(tracer_grid)
    tendency = -(side_east - westward(side_east) + side_north - southward(side_north)) + vert_bottom - vert_top
    updated = tracer_grid + tracer_time * active * tendency / layer_depth
    return from_grid(updated), from_grid(surface), from_grid(trans_east), from_grid(trans_north)
```

```python
import functools

import jax
import jax.numpy as jnp
from jax import lax
from jax.experimental import pallas as pl
from jax.experimental.pallas import tpu as pltpu
from jax.sharding import PartitionSpec as P

TROWS = 8
NSUB = 8
NTR = 6
ND = 8
CY = 128
CX = 128
RX = CY + 16

tau = 0.45
coupling = 1.0 / 16
tracer_time = 0.1

MESH = pl.DeviceIdType.MESH
F32 = jnp.float32


def roll(x, shift, axis):
    shift = shift % x.shape[axis]
    return x if shift == 0 else pltpu.roll(x, shift, axis)


def lanes(rows, width=CX):
    return lax.broadcasted_iota(jnp.int32, (rows, width), 1)


def rows_of(rows, width=CX):
    return lax.broadcasted_iota(jnp.int32, (rows, width), 0)


def between(x, low, high):
    return (x >= low) & (x < high)


def kernel(
    h_in, u_in, v_in, c_in, sea_in, uc_in, vc_in, wet_in, lev_in,
    c_out, s_out, e_out, n_out,
    h, u, v, c, sea, uc, vc, wet, lev,
    east_pack, west_pack, north_pack, south_pack,
    side_e, side_w, rim_n, rim_s,
    above, below,
    send_buf, recv_buf, total,
    face_e, face_n, u_ext, v_ext,
    surf, te, tn, tw, ae, be, ce, an, bn, cn,
    dep_e, dep_n, col_e, col_n,
    div_send, div_recv, new_c,
    loc_sem, halo_send, halo_recv, vert_send, vert_recv,
    rs_send, rs_recv, ag_send, ag_recv, div_ss, div_rs, out_sem,
):
    me = lax.axis_index("depth")
    tile = lax.axis_index("tiles")
    tx = tile // TROWS
    ty = tile % TROWS
    cols = 8

    def tile_at(dx, dy):
        return ((tx + dx + cols) % cols) * TROWS + (ty + dy + TROWS) % TROWS

    def member(which):
        return {"tiles": tile, "depth": which}

    def beside(dx, dy):
        return {"tiles": tile_at(dx, dy), "depth": me}

    around = [(1, 0), (-1, 0), (0, 1), (0, -1), (1, 1), (-1, 1), (1, -1), (-1, -1)]

    fetches = []
    for i, (src, dst) in enumerate([
        (h_in.at[:, 0], h), (u_in.at[:, 0], u), (v_in.at[:, 0], v), (sea_in.at[0], sea),
        (uc_in.at[0], uc), (vc_in.at[0], vc), (wet_in.at[0], wet), (lev_in.at[0], lev),
        (c_in.at[:, :, 0], c),
    ]):
        copy = pltpu.make_async_copy(src, dst, loc_sem.at[i])
        copy.start()
        fetches.append(copy)

    barrier = pltpu.get_barrier_semaphore()
    for dx, dy in around:
        pl.semaphore_signal(barrier, inc=1, device_id=beside(dx, dy), device_id_type=MESH)
    for k in range(1, ND):
        pl.semaphore_signal(barrier, inc=1, device_id=member((me + k) % ND), device_id_type=MESH)

    for copy in fetches:
        copy.wait()

    lane = lanes(CY)
    row = rows_of(CY)
    count = (wet[...] * lev[...]).astype(F32)
    fields = [h[0], h[1], u[0], u[1], v[0], v[1], count, sea[...], uc[...], vc[...]]
    to_east = jnp.zeros((CY, CX), F32)
    to_west = jnp.zeros((CY, CX), F32)
    for f, x in enumerate(fields):
        turned = roll(x, 8 * f, 1)
        start = (8 * f - 8) % CX
        to_west = jnp.where(between(lane, 8 * f, 8 * f + 8), turned, to_west)
        to_east = jnp.where(between(lane, start, start + 8), turned, to_east)
        south_pack[8 * f : 8 * f + 8] = x[0:8]
        north_pack[8 * f : 8 * f + 8] = x[CY - 8 : CY]
    to_east = jnp.where(between(lane, 72, 80), roll(uc[...], 88, 1), to_east)
    north_pack[80:88] = vc[CY - 16 : CY - 8]
    south_pack[80:88] = vc[0:8]
    for p in range(2 * NTR):
        plane = c[p // 2, p % 2]
        turned = roll(plane, 96 + p, 1)
        to_west = jnp.where(lane == 96 + p, turned, to_west)
        to_east = jnp.where(lane == 95 + p, turned, to_east)
        south_pack[88 + p : 89 + p] = plane[0:1]
        north_pack[88 + p : 89 + p] = plane[CY - 1 : CY]
    for p in range(2 * NTR, 16):
        south_pack[88 + p : 89 + p] = jnp.zeros((1, CX), F32)
        north_pack[88 + p : 89 + p] = jnp.zeros((1, CX), F32)
    east_pack[...] = to_east
    west_pack[...] = to_west

    first = (2 * me).astype(F32)
    count_e = jnp.minimum(count, jnp.where(lane == CX - 1, 0.0, roll(count, -1, 1)))
    count_n = jnp.minimum(count, jnp.where(row == CY - 1, 0.0, roll(count, -1, 0)))
    sums = [None] * 4
    for l in range(2):
        de = jnp.where(first + l < count_e, 0.5 * (h[l] + roll(h[l], -1, 1)), 0.0)
        dn = jnp.where(first + l < count_n, 0.5 * (h[l] + roll(h[l], -1, 0)), 0.0)
        for f, x in enumerate([de, dn, u[l] * de, v[l] * dn]):
            sums[f] = x if l == 0 else sums[f] + x
    for f in range(4):
        for p in range(ND):
            send_buf[p, 16 * f : 16 * f + 16] = sums[f][16 * p : 16 * p + 16]

    pl.semaphore_wait(barrier, len(around) + ND - 1)

    def halo(i, src, dst, dx, dy):
        return pltpu.make_async_remote_copy(
            src_ref=src, dst_ref=dst, send_sem=halo_send.at[i], recv_sem=halo_recv.at[i],
            device_id=beside(dx, dy), device_id_type=MESH,
        )

    halos = [
        halo(0, east_pack, side_w.at[0:CY], 1, 0),
        halo(1, west_pack, side_e.at[0:CY], -1, 0),
        halo(2, north_pack, rim_s, 0, 1),
        halo(3, south_pack, rim_n, 0, -1),
        halo(4, east_pack.at[CY - 8 : CY], side_w.at[CY + 8 : CY + 16], 1, 1),
        halo(5, west_pack.at[CY - 8 : CY], side_e.at[CY + 8 : CY + 16], -1, 1),
        halo(6, east_pack.at[0:8], side_w.at[CY : CY + 8], 1, -1),
        halo(7, west_pack.at[0:8], side_e.at[CY : CY + 8], -1, -1),
    ]
    for copy in halos:
        copy.start()

    def scatter(part, peer, slot):
        low, high = ((0, 64), (64, 88))[part]
        return pltpu.make_async_remote_copy(
            src_ref=send_buf.at[peer, low:high], dst_ref=recv_buf.at[slot, low:high],
            send_sem=rs_send.at[part, peer], recv_sem=rs_recv.at[part, slot],
            device_id=member(peer), device_id_type=MESH,
        )

    peers = [(me + k) % ND for k in range(1, ND)]
    for peer in peers:
        scatter(0, peer, me).start()

    up = pltpu.make_async_remote_copy(
        src_ref=c.at[:, 0], dst_ref=below, send_sem=vert_send.at[0], recv_sem=vert_recv.at[0],
        device_id=member((me + ND - 1) % ND), device_id_type=MESH,
    )
    down = pltpu.make_async_remote_copy(
        src_ref=c.at[:, 1], dst_ref=above, send_sem=vert_send.at[1], recv_sem=vert_recv.at[1],
        device_id=member((me + 1) % ND), device_id_type=MESH,
    )

    @pl.when(me > 0)
    def _():
        up.start()

    @pl.when(me == 0)
    def _():
        above[...] = jnp.zeros_like(above)

    @pl.when(me < ND - 1)
    def _():
        down.start()

    @pl.when(me == ND - 1)
    def _():
        below[...] = jnp.zeros_like(below)

    for copy in halos:
        copy.wait()

    lane_x = lanes(RX)
    row_x = rows_of(RX)
    has_n = ty < TROWS - 1
    has_s = ty > 0
    row_ok = (row_x < CY) | (between(row_x, CY, CY + 8) & has_n) | ((row_x >= CY + 8) & has_s)
    side_ok = row_ok & ((lane_x < 8) | (lane_x >= CX - 8))
    from_e = side_e[...]
    from_w = side_w[...]

    def extended(f, x):
        side = jnp.where(between(lane_x, 8 * f, 8 * f + 8), from_e, from_w)
        side = jnp.where(side_ok, roll(side, -8 * f, 1), 0.0)
        main = jnp.concatenate([x, rim_n[8 * f : 8 * f + 8], rim_s[8 * f : 8 * f + 8]], axis=0)
        main = jnp.where(row_ok, main, 0.0)
        return jnp.concatenate([main, side], axis=1)

    count_x = extended(6, count)
    min_e = jnp.minimum(count_x, roll(count_x, -1, 1))
    min_n = jnp.minimum(count_x, roll(count_x, -1, 0))
    sums = [None] * 4
    for l in range(2):
        h_x = extended(l, h[l])
        u_x = extended(2 + l, u[l])
        v_x = extended(4 + l, v[l])
        de = jnp.where(first + l < min_e, 0.5 * (h_x + roll(h_x, -1, 1)), 0.0)
        dn = jnp.where(first + l < min_n, 0.5 * (h_x + roll(h_x, -1, 0)), 0.0)
        face_e[l] = de
        face_n[l] = dn
        u_ext[l] = u_x
        v_ext[l] = v_x
        for f, x in enumerate([de, dn, u_x * de, v_x * dn]):
            sums[f] = x if l == 0 else sums[f] + x

    packed = jnp.zeros((RX, CX), F32)
    for f in range(4):
        packed = jnp.where(lane_x == 16 * f, roll(sums[f][:, :CX], 1 + 16 * f, 1), packed)
        packed = jnp.where(
            between(lane_x, 16 * f + 1, 16 * f + 16), roll(sums[f][:, CX:], 9 + 16 * f, 1), packed
        )
    half = RX // 2
    folded = jnp.where(lanes(half) < 64, packed[:half], roll(packed[half:], 64, 1))
    blocks = [folded[8 * i : 8 * i + 8] for i in range(9)]
    for f in range(4):
        blocks.append(roll(sums[f][:, :CX], 1, 0)[CY : CY + 8])
    for f in range(4):
        blocks.append(sums[f][CY + 8 : CY + 16, :CX])
    blocks += [jnp.zeros((8, CX), F32)] * (24 - len(blocks))
    for i, block in enumerate(blocks):
        low = 64 + 8 * (i % 3)
        send_buf[i // 3, low : low + 8] = block
    for peer in peers:
        scatter(1, peer, me).start()

    surf[...] = extended(7, sea[...])
    u_col = extended(8, uc[...])
    last = jnp.where(lane_x == CX - 9, roll(from_w, 40, 1), 0.0)
    te[...] = u_col + jnp.concatenate([jnp.zeros((RX, CX), F32), last], axis=1)
    tn[...] = extended(9, vc[...])
    wet_x = jnp.where(count_x > 0.0, 1.0, 0.0)
    tw[...] = tau * wet_x
    wet_e = wet_x * roll(wet_x, -1, 1)
    wet_n = wet_x * roll(wet_x, -1, 0)
    ae[...] = (1.0 - tau) * wet_e
    an[...] = (1.0 - tau) * wet_n

    for peer in peers:
        scatter(0, peer, peer).wait_recv()
        scatter(1, peer, peer).wait_recv()
    mine = send_buf[me]
    for k in range(1, ND):
        mine = mine + recv_buf[(me + k) % ND]
    total[me] = mine

    def gather(peer, slot):
        return pltpu.make_async_remote_copy(
            src_ref=total.at[slot], dst_ref=total.at[slot],
            send_sem=ag_send.at[peer], recv_sem=ag_recv.at[slot],
            device_id=member(peer), device_id_type=MESH,
        )

    for peer in peers:
        gather(peer, me).start()
    for peer in peers:
        gather(peer, peer).wait_recv()

    def block_of(i):
        low = 64 + 8 * (i % 3)
        return total[i // 3, low : low + 8]

    folded = jnp.concatenate([block_of(i) for i in range(9)], axis=0)
    packed = jnp.concatenate([folded, roll(folded, 64, 1)], axis=0)
    for f, ref in enumerate([dep_e, dep_n, col_e, col_n]):
        side = jnp.where((lane_x < 7) | (lane_x >= CX - 8), roll(packed, -(9 + 16 * f), 1), 0.0)
        north = block_of(9 + f)
        main = jnp.concatenate(
            [total[p, 16 * f : 16 * f + 16] for p in range(ND)]
            + [roll(north, -1, 0), block_of(13 + f)],
            axis=0,
        )
        main = jnp.where(row_x == CY - 1, jnp.broadcast_to(north[0:1], (RX, CX)), main)
        main = jnp.where(lane_x == CX - 1, roll(packed, CX - 1 - 16 * f, 1), main)
        ref[...] = jnp.concatenate([main, side], axis=1)
    be[...] = (tau * coupling) * wet_e * dep_e[...]
    bn[...] = (tau * coupling) * wet_n * dep_n[...]
    ce[...] = (tau * coupling) * wet_e * col_e[...]
    cn[...] = (tau * coupling) * wet_n * col_n[...]

    def substep(beyond):
        e = te[...]
        n = tn[...]
        south = roll(n, 1, 0)
        if beyond is not None:
            south = jnp.where(rows_of(RX, 2 * CX) == CY + 8, beyond, south)
        s = surf[...] - tw[...] * (e - roll(e, 1, 1) + n - south)
        surf[...] = s
        te[...] = ae[...] * e - be[...] * (roll(s, -1, 1) - s) + ce[...]
        tn[...] = an[...] * n - bn[...] * (roll(s, -1, 0) - s) + cn[...]

    beyond = jnp.concatenate([rim_s[87:88], jnp.zeros((1, CX), F32)], axis=1)
    substep(jnp.broadcast_to(beyond, (RX, 2 * CX)))

    def more(i, carry):
        substep(None)
        return carry

    lax.fori_loop(1, NSUB, more, 0)

    flat_out = [
        pltpu.make_async_copy(src.at[0:CY, 0:CX], dst.at[0], out_sem.at[i])
        for i, (src, dst) in enumerate([(surf, s_out), (te, e_out), (tn, n_out)])
    ]
    for copy in flat_out:
        copy.start()

    def parts_of(fe, fn):
        return fe[:, :CX], roll(fe, 1, 1)[:, :CX], fn[:CY], roll(fn, 1, 0)[:CY]

    shift_e = te[0:CY] - coupling * col_e[0:CY]
    shift_n = tn[:, 0:CX] - coupling * col_n[:, 0:CX]
    flows = []
    divs = []
    for l in range(2):
        fe, fw, fn, fs = parts_of(
            face_e[l, 0:CY] * (u_ext[l, 0:CY] + shift_e),
            face_n[l, :, 0:CX] * (v_ext[l, :, 0:CX] + shift_n),
        )
        flows.append((fe, fw, fn, fs))
        divs.append(fe - fw + fn - fs)
    here = divs[0] + divs[1]
    div_send[...] = here

    pair = me + 1 - 2 * (me % 2)
    upper = me < ND // 2
    outer = (me < 2) | (me >= ND - 2)
    near = jnp.where(upper, 2, ND - 4)

    def hand(i, slot, peer):
        return pltpu.make_async_remote_copy(
            src_ref=div_send, dst_ref=div_recv.at[slot], send_sem=div_ss.at[i], recv_sem=div_rs.at[slot],
            device_id=member(peer), device_id_type=MESH,
        )

    hand(0, 0, pair).start()

    @pl.when(outer)
    def _():
        hand(1, 1 + me % 2, near).start()
        hand(2, 1 + me % 2, near + 1).start()
        div_recv[1] = jnp.zeros((CY, CX), F32)
        div_recv[2] = jnp.zeros((CY, CX), F32)

    te_, tw_, tn_, ts_ = parts_of(
        col_e[0:CY] + dep_e[0:CY] * shift_e, col_n[:, 0:CX] + dep_n[:, 0:CX] * shift_n
    )
    whole = te_ - tw_ + tn_ - ts_

    gains = []
    for l in range(2):
        gain = jnp.where(first + l < count, tracer_time / h[l], 0.0)
        gains.append(gain)
        fe, fw, fn, fs = flows[l]
        a_e = -gain * jnp.minimum(fe, 0.0)
        a_w = gain * jnp.maximum(fw, 0.0)
        a_n = -gain * jnp.minimum(fn, 0.0)
        a_s = gain * jnp.maximum(fs, 0.0)
        a_c = 1.0 - gain * (
            jnp.maximum(fe, 0.0) - jnp.minimum(fw, 0.0) + jnp.maximum(fn, 0.0) - jnp.minimum(fs, 0.0)
        )
        for m in range(NTR):
            p = 2 * m + l
            x = c[m, l]
            x_e = jnp.where(lane == CX - 1, roll(side_e[0:CY], 31 - p, 1), roll(x, -1, 1))
            x_w = jnp.where(lane == 0, roll(side_w[0:CY], -(95 + p), 1), roll(x, 1, 1))
            x_n = jnp.where(
                row == CY - 1, jnp.broadcast_to(rim_n[88 + p : 89 + p], (CY, CX)), roll(x, -1, 0)
            )
            x_s = jnp.where(row == 0, jnp.broadcast_to(rim_s[88 + p : 89 + p], (CY, CX)), roll(x, 1, 0))
            new_c[m, l] = a_c * x + a_e * x_e + a_w * x_w + a_n * x_n + a_s * x_s

    hand(0, 0, pair).wait_recv()

    @pl.when(jnp.logical_not(outer))
    def _():
        hand(1, 1, pair).wait_recv()
        hand(2, 2, pair).wait_recv()

    partner = div_recv[0]
    far = div_recv[1] + div_recv[2]
    odd = me % 2 == 1
    deeper = jnp.where(
        upper,
        whole - here - far - jnp.where(odd, partner, 0.0),
        far + jnp.where(odd, 0.0, partner),
    )

    @pl.when(me < ND - 1)
    def _():
        up.wait_recv()

    @pl.when(me > 0)
    def _():
        down.wait_recv()

    bottom = -deeper
    middle = -(divs[1] + deeper)
    top = jnp.where(me == 0, 0.0, -(divs[0] + divs[1] + deeper))
    for l in range(2):
        low, high = (middle, top) if l == 0 else (bottom, middle)
        gain = gains[l]
        a_b = gain * jnp.maximum(low, 0.0)
        a_a = -gain * jnp.minimum(high, 0.0)
        a_c = gain * (jnp.minimum(low, 0.0) - jnp.maximum(high, 0.0))
        for m in range(NTR):
            under = c[m, 1] if l == 0 else below[m]
            over = above[m] if l == 0 else c[m, 0]
            new_c[m, l] = new_c[m, l] + a_c * c[m, l] + a_b * under + a_a * over
    store = pltpu.make_async_copy(new_c, c_out.at[:, :, 0], out_sem.at[3])
    store.start()

    for peer in peers:
        scatter(0, peer, me).wait_send()
        scatter(1, peer, me).wait_send()
        gather(peer, me).wait_send()
    hand(0, 0, pair).wait_send()

    @pl.when(outer)
    def _():
        hand(1, 1, near).wait_send()
        hand(2, 2, near).wait_send()

    @pl.when(me > 0)
    def _():
        up.wait_send()

    @pl.when(me < ND - 1)
    def _():
        down.wait_send()

    for copy in flat_out:
        copy.wait()
    store.wait()


def body(thickness, u_layer, v_layer, tracers, sea_level, u_column, v_column, wet_cells, levels):
    any_spec = pl.BlockSpec(memory_space=pl.ANY)
    plane = pltpu.VMEM((CY, CX), F32)
    layers = pltpu.VMEM((2, CY, CX), F32)
    wide = pltpu.VMEM((RX, 2 * CX), F32)
    wide2 = pltpu.VMEM((2, RX, 2 * CX), F32)
    whole_c = pltpu.VMEM((NTR, 2, CY, CX), F32)
    column_c = pltpu.VMEM((NTR, CY, CX), F32)
    side = pltpu.VMEM((RX, CX), F32)
    rim = pltpu.VMEM((104, CX), F32)
    pieces = pltpu.VMEM((ND, 88, CX), F32)
    flat = pltpu.VMEM((CY, CX), jnp.int32)
    dma = pltpu.SemaphoreType.DMA
    return pl.pallas_call(
        kernel,
        out_shape=(
            jax.ShapeDtypeStruct(tracers.shape, F32),
            jax.ShapeDtypeStruct(sea_level.shape, F32),
            jax.ShapeDtypeStruct(sea_level.shape, F32),
            jax.ShapeDtypeStruct(sea_level.shape, F32),
        ),
        in_specs=[any_spec] * 9,
        out_specs=(any_spec,) * 4,
        scratch_shapes=[
            layers, layers, layers, whole_c, plane, plane, plane, flat, flat,
            plane, plane, rim, rim,
            side, side, rim, rim,
            column_c, column_c,
            pieces, pieces, pieces,
            wide2, wide2, wide2, wide2,
            wide, wide, wide, wide, wide, wide, wide, wide, wide, wide,
            wide, wide, wide, wide,
            plane, pltpu.VMEM((3, CY, CX), F32), whole_c,
            dma((9,)), dma((8,)), dma((8,)), dma((2,)), dma((2,)),
            dma((2, ND)), dma((2, ND)), dma((ND,)), dma((ND,)), dma((3,)), dma((3,)), dma((4,)),
        ],
        compiler_params=pltpu.CompilerParams(
            collective_id=0, has_side_effects=True, vmem_limit_bytes=56 * 1024 * 1024
        ),
    )(thickness, u_layer, v_layer, tracers, sea_level, u_column, v_column, wet_cells, levels)


def solution(mesh):
    return jax.shard_map(
        body,
        mesh=mesh,
        in_specs=(
            P("depth", "tiles", None, None),
            P("depth", "tiles", None, None),
            P("depth", "tiles", None, None),
            P(None, "depth", "tiles", None, None),
            P("tiles", None, None),
            P("tiles", None, None),
            P("tiles", None, None),
            P("tiles", None, None),
            P("tiles", None, None),
        ),
        out_specs=(
            P(None, "depth", "tiles", None, None),
            P("tiles", None, None),
            P("tiles", None, None),
            P("tiles", None, None),
        ),
        check_vma=False,
    )
```

```python
import functools

import jax
import jax.numpy as jnp
from jax import lax
from jax.experimental import pallas as pl
from jax.experimental.pallas import tpu as pltpu
from jax.sharding import PartitionSpec as P

TROWS = 8
NSUB = 8
NTR = 6
ND = 8
NE = 4
EB = 5
CY = 128
CX = 128
RX = CY + 32
OWN = 16
END = OWN + CY
LOW = OWN - 8
HIGH = END + 8

tau = 0.45
coupling = 1.0 / 16
tracer_time = 0.1

MESH = pl.DeviceIdType.MESH
F32 = jnp.float32


def roll(x, shift, axis):
    shift = shift % x.shape[axis]
    return x if shift == 0 else pltpu.roll(x, shift, axis)


def lanes(rows, width=CX):
    return lax.broadcasted_iota(jnp.int32, (rows, width), 1)


def rows_of(rows, width=CX):
    return lax.broadcasted_iota(jnp.int32, (rows, width), 0)


def between(x, low, high):
    return (x >= low) & (x < high)


def kernel(
    h_in, u_in, v_in, c_in, sea_in, uc_in, vc_in, wet_in, lev_in,
    part, s_out, e_out, n_out, c, below, above, lift,
    x, state, wet, lev,
    side_pack, side_in, corner_pack, corner_in, sizes,
    edge_c,
    main_send, pair_in, chip_sum, main_in, main_all,
    edge_send, edge_in, edge_all,
    face_e, face_n, local, total,
    tw, ae, an, be, bn, ce, cn,
    outer_send, outer_pair, outer_sum, outer_in, outer_div,
    flow_n, flow_t, prod_n, coef, div_1, whole_div, pair_send, pair_div,
    loc_sem, sent, sent_late, edge_sent, outer_sent, up_sent, down_sent,
    halo_got, pair_got, rs_got, ag_got, forward_got, edge_got, edge_all_got, half_got, outer_got,
    up_got, down_got, div_got,
):
    me = lax.axis_index("depth")
    tile = lax.axis_index("tiles")
    tx = tile // TROWS
    ty = tile % TROWS
    chip = me // 2
    core = me % 2
    other = 1 - core
    partner = 2 * chip + other
    upper = me < ND // 2
    outer = (me < 2) | (me >= ND - 2)
    cols = 8

    def tile_at(dx, dy):
        return ((tx + dx + cols) % cols) * TROWS + (ty + dy + TROWS) % TROWS

    def member(which):
        return {"tiles": tile, "depth": which}

    def beside(dx, dy):
        return {"tiles": tile_at(dx, dy), "depth": me}

    def remote(source, target, send, recv, where):
        return pltpu.make_async_remote_copy(
            src_ref=source, dst_ref=target, send_sem=send, recv_sem=recv,
            device_id=where, device_id_type=MESH,
        )

    around = [(1, 0), (-1, 0), (0, 1), (0, -1), (1, 1), (-1, 1), (1, -1), (-1, -1)]
    rows_own = slice(OWN, END)

    def got(sem, rows):
        remote(sizes.at[0:rows], sizes.at[0:rows], sem, sem, member(partner)).wait_recv()

    def left(sem, rows):
        remote(sizes.at[0:rows], sizes.at[0:rows], sem, sem, member(partner)).wait_send()

    for source, target in [
        (h_in.at[:, 0], x.at[0:2, 0, rows_own]), (wet_in.at[0], wet), (lev_in.at[0], lev),
        (u_in.at[:, 0], x.at[2:4, 0, rows_own]), (v_in.at[:, 0], x.at[4:6, 0, rows_own]),
        (sea_in.at[0], state.at[0, 0, rows_own]), (uc_in.at[0], state.at[1, 0, rows_own]),
        (vc_in.at[0], state.at[2, 0, rows_own]),
    ]:
        pltpu.make_async_copy(source, target, loc_sem.at[0]).start()

    barrier = pltpu.get_barrier_semaphore()
    for dx, dy in around:
        pl.semaphore_signal(barrier, inc=1, device_id=beside(dx, dy), device_id_type=MESH)
    peers = [(me + k) % ND for k in range(1, ND)]
    for peer in peers:
        pl.semaphore_signal(barrier, inc=1, device_id=member(peer), device_id_type=MESH)
    fetch_c = pltpu.make_async_copy(c_in.at[:, :, 0], c.at[:, :, 8 : CY + 8], loc_sem.at[1])
    fetch_c.start()

    fetched = 11 * CY
    pltpu.make_async_copy(sizes.at[0:fetched], sizes.at[0:fetched], loc_sem.at[0]).wait()

    lane8 = lanes(8)
    x[6, 0, rows_own] = (wet[...] * lev[...]).astype(F32)

    def pack_sides(phase, fields, extra=None):
        for i in range(8):
            east = west = jnp.zeros((8, CX), F32)
            for j in range(2):
                low = OWN + 64 * j + 8 * i
                for f, ref in enumerate(fields):
                    turned = roll(ref[low : low + 8], 8 * f + 8 + 64 * j, 1)
                    start = 64 * j + 8 * f
                    west = jnp.where(between(lane8, start + 8, start + 16), turned, west)
                    east = jnp.where(between(lane8, start, start + 8), turned, east)
                if extra is not None:
                    east, west = extra(64 * j + 8 * i, 64 * j, east, west)
            side_pack[phase, 0, 8 * i : 8 * i + 8] = east
            side_pack[phase, 1, 8 * i : 8 * i + 8] = west

    early = [x.at[f, 0] for f in range(7)]
    late = [state.at[f, 0] for f in range(3)]
    pack_sides(0, early)

    for j, low in enumerate((OWN, END - 8)):
        east = west = jnp.zeros((8, CX), F32)
        for f, ref in enumerate(early + late):
            turned = roll(ref[low : low + 8], 8 * f + 8, 1)
            west = jnp.where(between(lane8, 8 * f + 8, 8 * f + 16), turned, west)
            east = jnp.where(between(lane8, 8 * f, 8 * f + 8), turned, east)
        corner_pack[0, j] = east
        corner_pack[1, j] = west

    pl.semaphore_wait(barrier, len(around) + ND - 1)

    def halo(phase, source, target, dx, dy):
        sem = sent if phase == 0 else sent_late
        remote(source, target, sem, halo_got.at[phase], beside(dx, dy)).start()

    halo(0, side_pack.at[0, 0], side_in.at[0, 0], 1, 0)
    halo(0, side_pack.at[0, 1], side_in.at[0, 1], -1, 0)
    halo(0, corner_pack.at[0, 1], corner_in.at[0], 1, 1)
    halo(0, corner_pack.at[1, 1], corner_in.at[1], -1, 1)
    halo(0, corner_pack.at[0, 0], corner_in.at[2], 1, -1)
    halo(0, corner_pack.at[1, 0], corner_in.at[3], -1, -1)
    halo(0, x.at[:, 0, END - 8 : END], x.at[:, 0, LOW:OWN], 0, 1)
    halo(0, x.at[:, 0, OWN : OWN + 8], x.at[:, 0, END:HIGH], 0, -1)

    first = (2 * me).astype(F32)
    lane16 = lanes(16)
    row16 = rows_of(16)

    def next_row(ref, p):
        low = OWN + 16 * p
        if p < ND - 1:
            return ref[low + 1 : low + 17]
        return jnp.where(row16 == 15, 0.0, roll(ref[low : low + 16], -1, 0))

    for p in range(ND):
        low = OWN + 16 * p
        here = slice(low, low + 16)
        count = x[6, 0, here]
        count_e = jnp.minimum(count, jnp.where(lane16 == CX - 1, 0.0, roll(count, -1, 1)))
        count_n = jnp.minimum(count, next_row(x.at[6, 0], p))
        sums = [0.0] * 4
        for l in range(2):
            thick = x[l, 0, here]
            de = jnp.where(first + l < count_e, 0.5 * (thick + roll(thick, -1, 1)), 0.0)
            dn = jnp.where(first + l < count_n, 0.5 * (thick + next_row(x.at[l, 0], p)), 0.0)
            new = [de, dn, x[2 + l, 0, here] * de, x[4 + l, 0, here] * dn]
            sums = [a + b for a, b in zip(sums, new)]
        for f in range(4):
            main_send[p // 2, p % 2, 16 * f : 16 * f + 16] = sums[f]
    remote(main_send.at[:, other], pair_in, sent, pair_got, member(partner)).start()

    fetch_c.wait()
    rows_c = slice(8, CY + 8)

    def send_tracers(i):
        part = slice(2 * i, 2 * i + 2)

        @pl.when(me > 0)
        def _():
            remote(
                c.at[part, 0, rows_c], below.at[part], up_sent, up_got, member((me + ND - 1) % ND)
            ).start()

        @pl.when(me < ND - 1)
        def _():
            remote(
                c.at[part, 1, rows_c], above.at[part], down_sent, down_got, member((me + 1) % ND)
            ).start()

    send_tracers(0)

    def pack_more(low, shift, east, west):
        old = state[1, 0, OWN + low : OWN + low + 8]
        east = jnp.where(between(lane8, shift + 24, shift + 32), roll(old, 40 + shift, 1), east)
        for p in range(2 * NTR):
            plane = c[p // 2, p % 2, 8 + low : 16 + low]
            west = jnp.where(lane8 == shift + 48 + p, roll(plane, shift + 48 + p, 1), west)
            east = jnp.where(lane8 == shift + 49 + p, roll(plane, shift + 50 + p, 1), east)
        return east, west

    pack_sides(1, late, pack_more)

    got(pair_got, 256)
    chips = [(chip + k) % 4 for k in range(1, 4)]
    for q in range(4):
        chip_sum[q] = main_send[q, core] + pair_in[q]
    for q in chips:
        remote(chip_sum.at[q], main_in.at[chip], sent, rs_got, member(2 * q + core)).start()
    send_tracers(1)
    halo(1, side_pack.at[1, 0], side_in.at[1, 0], 1, 0)
    halo(1, side_pack.at[1, 1], side_in.at[1, 1], -1, 0)
    halo(1, state.at[:, 0, END - 16 : END], state.at[:, 0, 0:OWN], 0, 1)
    halo(1, state.at[:, 0, OWN : OWN + 8], state.at[:, 0, END:HIGH], 0, -1)
    halo(1, c.at[:, :, CY : CY + 8], c.at[:, :, 0:8], 0, 1)
    halo(1, c.at[:, :, 8:16], c.at[:, :, CY + 8 : CY + 16], 0, -1)

    @pl.when(me == 0)
    def _():
        above[...] = jnp.zeros_like(above)

    @pl.when(me == ND - 1)
    def _():
        below[...] = jnp.zeros_like(below)

    for ref in (x, state):
        for k in range(2):
            ref[:, k, HIGH:RX] = jnp.zeros((ref.shape[0], RX - HIGH, CX), F32)
    state[2, 1, 0:LOW] = jnp.zeros((LOW, CX), F32)

    has_n = ty < TROWS - 1
    has_s = ty > 0

    def unpack_sides(phase, fields, extra=None):
        side = (lane8 < 8) | (lane8 >= CX - 8)
        for i in range(-1, 17):
            if i < 0:
                west, east, shift, ok = corner_in[0], corner_in[1], 56 * phase, side & has_s
            elif i == 16:
                west, east, shift, ok = corner_in[2], corner_in[3], 56 * phase, side & has_n
            else:
                j = 8 * (i % 8)
                west, east = side_in[phase, 0, j : j + 8], side_in[phase, 1, j : j + 8]
                shift, ok = 64 * (i // 8), side
            low = OWN + 8 * i
            for f, ref in enumerate(fields):
                start = shift + 8 * f + 8
                value = roll(jnp.where(between(lane8, start, start + 8), east, west), -start, 1)
                value = jnp.where(ok, value, 0.0)
                if extra is not None and f == 1 and 0 <= i < 16:
                    value = jnp.where(lane8 == CX - 9, roll(west, 88 - shift, 1), value)
                ref[low : low + 8] = value
            if extra is not None and 0 <= i < 16:
                extra(8 * i, shift, west, east)

    got(halo_got.at[0], 272)
    unpack_sides(0, [x.at[f, 1] for f in range(7)])

    @pl.when(jnp.logical_not(has_s))
    def _():
        x[:, 0, LOW:OWN] = jnp.zeros((7, 8, CX), F32)

    @pl.when(jnp.logical_not(has_n))
    def _():
        x[:, 0, END:HIGH] = jnp.zeros((7, 8, CX), F32)

    def shifted(pair, steps):
        lane = lanes(pair[0].shape[0])
        edge = lane == (0 if steps > 0 else CX - 1)
        main, side = (roll(value, steps, 1) for value in pair)
        return jnp.where(edge, side, main), jnp.where(edge, main, side)

    def both(ref, low, size):
        return ref[0, low : low + size], ref[1, low : low + size]

    step = 24
    for low in range(LOW, HIGH, step):
        here = slice(low, low + step)
        count = both(x.at[6], low, step)
        count_e = shifted(count, -1)
        count_n = both(x.at[6], low + 1, step)
        thick = [both(x.at[l], low, step) for l in range(2)]
        thick_e = [shifted(thick[l], -1) for l in range(2)]
        for k in range(2):
            min_e = jnp.minimum(count[k], count_e[k])
            min_n = jnp.minimum(count[k], count_n[k])
            sums = [0.0] * 4
            for l in range(2):
                north = x[l, k, low + 1 : low + 1 + step]
                de = jnp.where(first + l < min_e, 0.5 * (thick[l][k] + thick_e[l][k]), 0.0)
                dn = jnp.where(first + l < min_n, 0.5 * (thick[l][k] + north), 0.0)
                face_e[l, k, here] = de
                face_n[l, k, here] = dn
                new = [de, dn, x[2 + l, k, here] * de, x[4 + l, k, here] * dn]
                sums = [a + b for a, b in zip(sums, new)]
            for f in range(4):
                local[f, k, here] = sums[f]

    def put_block(i, block):
        edge_send[i // EB, 8 * (i % EB) : 8 * (i % EB) + 8] = block

    for i in range(9):
        block = jnp.zeros((8, CX), F32)
        for j in range(2):
            low = LOW + 72 * j + 8 * i
            for f in range(4):
                start = 64 * j + 16 * f
                block = jnp.where(
                    lane8 == start, roll(local[f, 0, low : low + 8], start + 1, 1), block
                )
                block = jnp.where(
                    between(lane8, start + 1, start + 16),
                    roll(local[f, 1, low : low + 8], start + 9, 1),
                    block,
                )
        put_block(i, block)
    for f in range(4):
        put_block(9 + f, local[f, 0, END - 1 : END + 7])
        put_block(13 + f, local[f, 0, LOW:OWN])
    for i in range(17, NE * EB):
        put_block(i, jnp.zeros((8, CX), F32))

    owner = core == 0

    @pl.when(owner)
    def _():
        for q in chips:
            remote(edge_send.at[q], edge_in.at[me], edge_sent, edge_got, member(2 * q)).start()

    @pl.when(jnp.logical_not(owner))
    def _():
        for q in chips + [chip]:
            remote(edge_send.at[q], edge_in.at[me], edge_sent, edge_got, member(2 * q)).start()

    @pl.when(outer)
    def _():
        for i in range(4):
            low = OWN + 32 * i
            here = slice(low, low + 32)
            flux = both(local.at[2], low, 32)
            value = flux[0] - shifted(flux, 1)[0] + local[3, 0, here] - local[3, 0, low - 1 : low + 31]
            outer_send[i // 2, 32 * (i % 2) : 32 * (i % 2) + 32] = value
        for j in range(2):
            low = OWN + 64 * j
            outer_send[j, 64:128] = local[0, 0, low : low + 64]
            outer_send[j, 128:200] = local[1, 0, low - 8 : low + 64]
            block = jnp.zeros((8, CX), F32)
            for r in range(8):
                turned = roll(local[0, 1, low + 8 * r : low + 8 * r + 8], r + 1, 1)
                block = jnp.where(lane8 == r, turned, block)
            outer_send[j, 200:208] = block
        remote(outer_send.at[other], outer_pair, outer_sent, half_got, member(partner)).start()

    got(rs_got, 192)
    mine = chip_sum[chip]
    for q in chips:
        mine = mine + main_in[q]
    main_all[chip, core] = mine
    piece = main_all.at[chip, core]
    for q in chips:
        remote(piece, piece, sent, ag_got, member(2 * q + core)).start()

    @pl.when(owner)
    def _():
        got(edge_got, 7 * 8 * EB)
        edge = edge_send[chip]
        for peer in peers:
            edge = edge + edge_in[peer]
        edge_all[chip] = edge
        for peer in peers:
            remote(edge_all.at[chip], edge_all.at[chip], edge_sent, edge_all_got, member(peer)).start()

    @pl.when(outer)
    def _():
        got(half_got, 208)
        outer_sum[...] = outer_send[core] + outer_pair[...]
        middle_chip = jnp.where(upper, 2, ND - 4)
        remote(outer_sum, outer_in, outer_sent, outer_got, member(middle_chip + core)).start()

    send_tracers(2)

    got(halo_got.at[1], 392)

    def put_tracers(low, shift, west, east):
        for p in range(2 * NTR):
            value = jnp.where(lane8 <= shift + 48 + p, east, west)
            edge_c[p // 2, p % 2, low : low + 8] = roll(value, 79 - shift - p, 1)

    unpack_sides(1, [state.at[f, 1] for f in range(3)], put_tracers)
    left(sent_late, 392)

    @pl.when(jnp.logical_not(has_s))
    def _():
        state[:, 0, LOW:OWN] = jnp.zeros((3, 8, CX), F32)

    @pl.when(jnp.logical_not(has_n))
    def _():
        state[:, 0, END:HIGH] = jnp.zeros((3, 8, CX), F32)

    for low in range(LOW, HIGH, step):
        here = slice(low, low + step)
        is_wet = [jnp.where(value > 0.0, 1.0, 0.0) for value in both(x.at[6], low, step)]
        wet_e = shifted(is_wet, -1)
        wet_n = [jnp.where(value > 0.0, 1.0, 0.0) for value in both(x.at[6], low + 1, step)]
        for k in range(2):
            tw[k, here] = tau * is_wet[k]
            ae[k, here] = (1.0 - tau) * (is_wet[k] * wet_e[k])
            an[k, here] = (1.0 - tau) * (is_wet[k] * wet_n[k])
            be[k, here] = (tau * coupling) * (is_wet[k] * wet_e[k])
            bn[k, here] = (tau * coupling) * (is_wet[k] * wet_n[k])

    got(ag_got, 192)
    half = main_all.at[:, core]
    remote(half, half, sent, forward_got, member(partner)).start()

    @pl.when(owner)
    def _():
        got(edge_all_got, 3 * 8 * EB)

    @pl.when(jnp.logical_not(owner))
    def _():
        got(edge_all_got, 4 * 8 * EB)

    got(forward_got, 256)

    def block_of(i):
        return edge_all[i // EB, 8 * (i % EB) : 8 * (i % EB) + 8]

    for f in range(4):
        for p in range(ND):
            low = OWN + 16 * p
            total[f, 0, low : low + 16] = main_all[p // 2, p % 2, 16 * f : 16 * f + 16]
        total[f, 0, END - 1 : END + 7] = block_of(9 + f)
        total[f, 0, HIGH - 1 : HIGH] = jnp.zeros((1, CX), F32)
        total[f, 0, LOW:OWN] = block_of(13 + f)
    rim = (lane8 < 7) | (lane8 >= CX - 8)
    for i in range(18):
        block = block_of(i % 9)
        shift = 64 * (i // 9)
        here = slice(LOW + 8 * i, LOW + 8 * i + 8)
        for f in range(4):
            edge = jnp.where(lane8 == CX - 1, roll(block, CX - 1 - 16 * f - shift, 1), total[f, 0, here])
            side = jnp.where(rim, roll(block, -(9 + 16 * f + shift), 1), 0.0)
            total[f, 0, here] = edge
            total[f, 1, here] = side
            for k, value in enumerate((edge, side)):
                if f == 2:
                    ce[k, here] = be[k, here] * value
                if f == 3:
                    cn[k, here] = bn[k, here] * value
        for k in range(2):
            be[k, here] = be[k, here] * total[0, k, here]
            bn[k, here] = bn[k, here] * total[1, k, here]

    def substep(i, carry):
        def rise(low):
            here = slice(low, low + step)
            east = both(state.at[1], low, step)
            west = shifted(east, 1)
            north = both(state.at[2], low, step)
            south = both(state.at[2], low - 1, step)
            level = []
            for k in range(2):
                value = state[0, k, here] - tw[k, here] * (east[k] - west[k] + north[k] - south[k])
                state[0, k, here] = value
                level.append(value)
            return level, east, north

        def move(low, level, east, north):
            here = slice(low, low + step)
            level_e = shifted(level, -1)
            level_n = both(state.at[0], low + 1, step)
            for k in range(2):
                state[1, k, here] = ae[k, here] * east[k] - be[k, here] * (level_e[k] - level[k]) + ce[k, here]
                state[2, k, here] = an[k, here] * north[k] - bn[k, here] * (level_n[k] - level[k]) + cn[k, here]

        held = rise(LOW)
        for low in range(LOW, HIGH, step):
            coming = rise(low + step) if low + step < HIGH else None
            move(low, *held)
            held = coming
        return carry

    lax.fori_loop(0, NSUB, substep, 0)

    flow_rows = [(OWN - 8, 8)] + [(OWN + 32 * i, 32) for i in range(4)]
    for low, size in flow_rows:
        here = slice(low, low + size)
        shift_n = state[2, 0, here] - coupling * total[3, 0, here]
        for l in range(2):
            flow_n[l, here] = face_n[l, 0, here] * (x[4 + l, 0, here] + shift_n)
        flow_t[here] = total[3, 0, here] + total[1, 0, here] * shift_n
        prod_n[here] = shift_n

    for i in range(4):
        low = OWN + 32 * i
        here = slice(low, low + 32)
        mine = slice(32 * i, 32 * i + 32)
        shift_e = [state[1, k, here] - coupling * total[2, k, here] for k in range(2)]
        flow = [total[2, k, here] + total[0, k, here] * shift_e[k] for k in range(2)]
        whole_div[mine] = flow[0] - shifted(flow, 1)[0] + flow_t[here] - flow_t[low - 1 : low + 31]
        count = x[6, 0, here]
        divs = []
        for l in range(2):
            flow = [face_e[l, k, here] * (x[2 + l, k, here] + shift_e[k]) for k in range(2)]
            fe = flow[0]
            fw = shifted(flow, 1)[0]
            fn = flow_n[l, here]
            fs = flow_n[l, low - 1 : low + 31]
            divs.append(fe - fw + fn - fs)
            gain = jnp.where(first + l < count, tracer_time / x[l, 0, here], 0.0)
            plus_e, minus_w = jnp.maximum(fe, 0.0), jnp.minimum(fw, 0.0)
            plus_n, minus_s = jnp.maximum(fn, 0.0), jnp.minimum(fs, 0.0)
            coef[l, 0, mine] = gain * (plus_e - fe)
            coef[l, 1, mine] = gain * (fw - minus_w)
            coef[l, 2, mine] = gain * (plus_n - fn)
            coef[l, 3, mine] = gain * (fs - minus_s)
            coef[l, 4, mine] = 1.0 - gain * (plus_e - minus_w + plus_n - minus_s)
            coef[l, 5, mine] = gain
        div_1[mine] = divs[1]
        pair_send[mine] = divs[0] + divs[1]

    @pl.when(jnp.logical_not(outer))
    def _():
        got(outer_got, 208)
        base = pl.multiple_of(OWN + 64 * core, 8)
        here = pl.ds(base, 64)
        shift_e = [state[1, k, here] - coupling * total[2, k, here] for k in range(2)]
        flow = outer_in[64:128] * shift_e[0]
        block = outer_in[200:208]
        column = jnp.concatenate([roll(block, -r, 1) for r in range(8)], axis=0)
        west = jnp.where(lanes(64) == 0, column * roll(shift_e[1], 1, 1), roll(flow, 1, 1))
        flow_t[0:72] = outer_in[128:200] * prod_n[pl.ds(pl.multiple_of(base - 8, 8), 72)]
        value = outer_in[0:64] + flow - west + flow_t[8:72] - flow_t[7:71]
        outer_div[core] = value
        pair_send[CY : CY + 64] = value

    remote(pair_send, pair_div, sent, div_got, member(partner)).start()

    s_out[0] = state[0, 0, rows_own]
    e_out[0] = state[1, 0, rows_own]
    n_out[0] = state[2, 0, rows_own]

    lane32 = lanes(32)
    for l in range(2):
        for i in range(4):
            mine = slice(32 * i, 32 * i + 32)
            low = 8 + 32 * i
            a_e, a_w, a_n, a_s, a_c = (coef[l, j, mine] for j in range(5))
            for m in range(NTR):
                value = c[m, l, low : low + 32]
                edge = edge_c[m, l, mine]
                value_e = jnp.where(lane32 == CX - 1, edge, roll(value, -1, 1))
                value_w = jnp.where(lane32 == 0, edge, roll(value, 1, 1))
                part[m, l, mine] = (
                    a_c * value
                    + a_e * value_e
                    + a_w * value_w
                    + a_n * c[m, l, low + 1 : low + 33]
                    + a_s * c[m, l, low - 1 : low + 31]
                )

    left(sent, 1360)

    @pl.when(owner)
    def _():
        left(edge_sent, 10 * 8 * EB)

    @pl.when(jnp.logical_not(owner))
    def _():
        left(edge_sent, 4 * 8 * EB)

    @pl.when(outer)
    def _():
        left(outer_sent, 416)

    got(div_got, 192)

    @pl.when(jnp.logical_not(outer))
    def _():
        outer_div[other] = pair_div[CY : CY + 64]

    @pl.when(outer)
    def _():
        outer_div[...] = jnp.zeros_like(outer_div)

    odd = core == 1
    for i in range(4):
        mine = slice(32 * i, 32 * i + 32)
        beyond = outer_div[i // 2, 32 * (i % 2) : 32 * (i % 2) + 32]
        near = pair_div[mine]
        here = pair_send[mine]
        deeper = jnp.where(
            upper,
            whole_div[mine] - here - beyond - jnp.where(odd, near, 0.0),
            beyond + jnp.where(odd, 0.0, near),
        )
        bottom = -deeper
        middle = -(div_1[mine] + deeper)
        top = jnp.where(me == 0, 0.0, -(here + deeper))
        for l in range(2):
            under_flow, over_flow = (middle, top) if l == 0 else (bottom, middle)
            gain = coef[l, 5, mine]
            lift[l, 0, mine] = gain * (jnp.minimum(under_flow, 0.0) - jnp.maximum(over_flow, 0.0))
            lift[l, 1, mine] = gain * jnp.maximum(under_flow, 0.0)
            lift[l, 2, mine] = -gain * jnp.minimum(over_flow, 0.0)

    @pl.when(me < ND - 1)
    def _():
        got(up_got, NTR * CY)
        left(down_sent, NTR * CY)

    @pl.when(me > 0)
    def _():
        got(down_got, NTR * CY)
        left(up_sent, NTR * CY)


def store(part, s_ref, e_ref, n_ref, c, below, above, lift, c_out, s_out, e_out, n_out, new_c, sem):
    copies = [
        pltpu.make_async_copy(source, target, sem.at[NTR + i])
        for i, (source, target) in enumerate([(s_ref, s_out), (e_ref, e_out), (n_ref, n_out)])
    ]
    for copy in copies:
        copy.start()
    for pair in range(0, NTR, 2):
        for l in range(2):
            for i in range(4):
                mine = slice(32 * i, 32 * i + 32)
                low = 8 + 32 * i
                a_c, a_b, a_a = (lift[l, j, mine] for j in range(3))
                for m in (pair, pair + 1):
                    under = c[m, 1, low : low + 32] if l == 0 else below[m, mine]
                    over = above[m, mine] if l == 0 else c[m, 0, low : low + 32]
                    new_c[m, l, mine] = (
                        part[m, l, mine] + a_c * c[m, l, low : low + 32] + a_b * under + a_a * over
                    )
        for m in (pair, pair + 1):
            copy = pltpu.make_async_copy(new_c.at[m], c_out.at[m, :, 0], sem.at[m])
            copy.start()
            copies.append(copy)
    for copy in copies:
        copy.wait()


def body(thickness, u_layer, v_layer, tracers, sea_level, u_column, v_column, wet_cells, levels):
    any_spec = pl.BlockSpec(memory_space=pl.ANY)
    near_spec = pl.BlockSpec(memory_space=pltpu.VMEM)

    def vmem(*shape):
        return pltpu.VMEM(shape, F32)

    plane = vmem(CY, CX)
    wide = vmem(2, RX, CX)
    wide2 = vmem(2, 2, RX, CX)
    column_c = vmem(NTR, CY, CX)
    flat = pltpu.VMEM((CY, CX), jnp.int32)
    quarter = vmem(4, 64, CX)
    halves = vmem(4, 2, 64, CX)
    edges = vmem(NE, 8 * EB, CX)
    dma = pltpu.SemaphoreType.DMA
    shapes = [tracers.shape] + [sea_level.shape] * 3
    results = pl.pallas_call(
        kernel,
        out_shape=(
            vmem(NTR, 2, CY, CX), *(pltpu.VMEM(shape, F32) for shape in shapes[1:]),
            vmem(NTR, 2, CY + 16, CX), column_c, column_c, vmem(2, 3, CY, CX),
        ),
        in_specs=[pl.BlockSpec(memory_space=pltpu.HBM)] * 9,
        out_specs=(near_spec,) * 8,
        scratch_shapes=[
            vmem(7, 2, RX, CX), vmem(3, 2, RX, CX), flat, flat,
            vmem(2, 2, 64, CX), vmem(2, 2, 64, CX), vmem(2, 2, 8, CX), vmem(4, 8, CX), vmem(11 * CY, CX),
            vmem(NTR, 2, CY, CX),
            halves, quarter, quarter, quarter, halves,
            edges, vmem(ND, 8 * EB, CX), edges,
            wide2, wide2, vmem(4, 2, RX, CX), vmem(4, 2, RX, CX),
            wide, wide, wide, wide, wide, wide, wide,
            vmem(2, 208, CX), vmem(208, CX), vmem(208, CX), vmem(208, CX), vmem(2, 64, CX),
            vmem(2, RX, CX), vmem(RX, CX), vmem(RX, CX), vmem(2, 6, CY, CX),
            plane, plane, vmem(CY + 64, CX), vmem(CY + 64, CX),
            dma((2,)), dma, dma, dma, dma, dma, dma,
            dma((2,)), dma, dma, dma, dma, dma, dma, dma, dma,
            dma, dma, dma,
        ],
        compiler_params=pltpu.CompilerParams(
            collective_id=0, has_side_effects=True, vmem_limit_bytes=48 * 1024 * 1024
        ),
    )(*[
        pltpu.with_memory_space_constraint(x, pltpu.HBM)
        for x in (thickness, u_layer, v_layer, tracers, sea_level, u_column, v_column, wet_cells, levels)
    ])
    return pl.pallas_call(
        store,
        out_shape=tuple(jax.ShapeDtypeStruct(shape, F32) for shape in shapes),
        in_specs=[near_spec] * 8,
        out_specs=(any_spec,) * 4,
        scratch_shapes=[vmem(NTR, 2, CY, CX), dma((NTR + 3,))],
    )(*[pltpu.with_memory_space_constraint(x, pltpu.VMEM) for x in results])


def solution(mesh):
    return jax.shard_map(
        body,
        mesh=mesh,
        in_specs=(
            P("depth", "tiles", None, None),
            P("depth", "tiles", None, None),
            P("depth", "tiles", None, None),
            P(None, "depth", "tiles", None, None),
            P("tiles", None, None),
            P("tiles", None, None),
            P("tiles", None, None),
            P("tiles", None, None),
            P("tiles", None, None),
        ),
        out_specs=(
            P(None, "depth", "tiles", None, None),
            P("tiles", None, None),
            P("tiles", None, None),
            P("tiles", None, None),
        ),
        check_vma=False,
    )
```

```python
import functools

import jax
import jax.numpy as jnp
from jax import lax
from jax.experimental import pallas as pl
from jax.experimental.pallas import tpu as pltpu
from jax.sharding import PartitionSpec as P

TROWS = 8
NSUB = 8
NTR = 6
ND = 8
NE = 4
EB = 5
CY = 128
CX = 128
RX = CY + 32
OWN = 16
END = OWN + CY
LOW = OWN - 8
HIGH = END + 8

tau = 0.45
coupling = 1.0 / 16
tracer_time = 0.1

MESH = pl.DeviceIdType.MESH
F32 = jnp.float32


def roll(x, shift, axis):
    shift = shift % x.shape[axis]
    return x if shift == 0 else pltpu.roll(x, shift, axis)


def lanes(rows, width=CX):
    return lax.broadcasted_iota(jnp.int32, (rows, width), 1)


def rows_of(rows, width=CX):
    return lax.broadcasted_iota(jnp.int32, (rows, width), 0)


def between(x, low, high):
    return (x >= low) & (x < high)


def kernel(
    h_in, u_in, v_in, c_in, sea_in, uc_in, vc_in, wet_in, lev_in,
    part, s_out, e_out, n_out, c, below, above, lift,
    x, state, wet, lev,
    side_pack, side_in, corner_pack, corner_in, sizes,
    edge_c,
    main_send, pair_in, chip_sum, main_in, main_all,
    edge_send, edge_in, edge_all,
    face_e, face_n, local, total,
    tw, ae, an, be, bn, ce, cn,
    outer_send, outer_pair, outer_sum, outer_in, outer_div,
    flow_n, flow_t, prod_n, coef, div_1, whole_div, pair_send, pair_div,
    loc_sem, sent, sent_late, edge_sent, outer_sent, up_sent, down_sent,
    halo_got, pair_got, rs_got, ag_got, forward_got, edge_got, edge_all_got, half_got, outer_got,
    up_got, down_got, div_got,
):
    me = lax.axis_index("depth")
    tile = lax.axis_index("tiles")
    tx = tile // TROWS
    ty = tile % TROWS
    chip = me // 2
    core = me % 2
    other = 1 - core
    partner = 2 * chip + other
    upper = me < ND // 2
    outer = (me < 2) | (me >= ND - 2)
    cols = 8

    def tile_at(dx, dy):
        return ((tx + dx + cols) % cols) * TROWS + (ty + dy + TROWS) % TROWS

    def member(which):
        return {"tiles": tile, "depth": which}

    def beside(dx, dy):
        return {"tiles": tile_at(dx, dy), "depth": me}

    def remote(source, target, send, recv, where):
        return pltpu.make_async_remote_copy(
            src_ref=source, dst_ref=target, send_sem=send, recv_sem=recv,
            device_id=where, device_id_type=MESH,
        )

    around = [(1, 0), (-1, 0), (0, 1), (0, -1), (1, 1), (-1, 1), (1, -1), (-1, -1)]
    rows_own = slice(OWN, END)

    def got(sem, rows):
        remote(sizes.at[0:rows], sizes.at[0:rows], sem, sem, member(partner)).wait_recv()

    def left(sem, rows):
        remote(sizes.at[0:rows], sizes.at[0:rows], sem, sem, member(partner)).wait_send()

    def fetch(source, target):
        pltpu.make_async_copy(source, target, loc_sem.at[0]).start()

    fetch(h_in.at[:, 0], x.at[0:2, 0, rows_own])
    fetch(wet_in.at[0], wet)
    fetch(lev_in.at[0], lev)
    fetch(u_in.at[:, 0], x.at[2:4, 0, rows_own])
    fetch(v_in.at[:, 0], x.at[4:6, 0, rows_own])
    barrier = pltpu.get_barrier_semaphore()
    for dx, dy in around:
        pl.semaphore_signal(barrier, inc=1, device_id=beside(dx, dy), device_id_type=MESH)
    fetch(sea_in.at[0], state.at[0, 0, rows_own])
    fetch(uc_in.at[0], state.at[1, 0, rows_own])
    fetch(vc_in.at[0], state.at[2, 0, rows_own])
    peers = [(me + k) % ND for k in range(1, ND)]
    for peer in peers:
        pl.semaphore_signal(barrier, inc=1, device_id=member(peer), device_id_type=MESH)
    fetch_c = pltpu.make_async_copy(c_in.at[:, :, 0], c.at[:, :, 8 : CY + 8], loc_sem.at[1])
    fetch_c.start()

    fetched = 11 * CY
    pltpu.make_async_copy(sizes.at[0:fetched], sizes.at[0:fetched], loc_sem.at[0]).wait()

    lane8 = lanes(8)
    x[6, 0, rows_own] = (wet[...] * lev[...]).astype(F32)

    def pack_sides(phase, fields, extra=None):
        for i in range(8):
            east = west = jnp.zeros((8, CX), F32)
            for j in range(2):
                low = OWN + 64 * j + 8 * i
                for f, ref in enumerate(fields):
                    turned = roll(ref[low : low + 8], 8 * f + 8 + 64 * j, 1)
                    start = 64 * j + 8 * f
                    west = jnp.where(between(lane8, start + 8, start + 16), turned, west)
                    east = jnp.where(between(lane8, start, start + 8), turned, east)
                if extra is not None:
                    east, west = extra(64 * j + 8 * i, 64 * j, east, west)
            side_pack[phase, 0, 8 * i : 8 * i + 8] = east
            side_pack[phase, 1, 8 * i : 8 * i + 8] = west

    early = [x.at[f, 0] for f in range(7)]
    late = [state.at[f, 0] for f in range(3)]
    pack_sides(0, early)

    for j, low in enumerate((OWN, END - 8)):
        east = west = jnp.zeros((8, CX), F32)
        for f, ref in enumerate(early + late):
            turned = roll(ref[low : low + 8], 8 * f + 8, 1)
            west = jnp.where(between(lane8, 8 * f + 8, 8 * f + 16), turned, west)
            east = jnp.where(between(lane8, 8 * f, 8 * f + 8), turned, east)
        corner_pack[0, j] = east
        corner_pack[1, j] = west

    pl.semaphore_wait(barrier, len(around) + ND - 1)

    def halo(phase, source, target, dx, dy):
        sem = sent if phase == 0 else sent_late
        remote(source, target, sem, halo_got.at[phase], beside(dx, dy)).start()

    halo(0, side_pack.at[0, 0], side_in.at[0, 0], 1, 0)
    halo(0, side_pack.at[0, 1], side_in.at[0, 1], -1, 0)
    halo(0, corner_pack.at[0, 1], corner_in.at[0], 1, 1)
    halo(0, corner_pack.at[1, 1], corner_in.at[1], -1, 1)
    halo(0, corner_pack.at[0, 0], corner_in.at[2], 1, -1)
    halo(0, corner_pack.at[1, 0], corner_in.at[3], -1, -1)
    halo(0, x.at[:, 0, END - 8 : END], x.at[:, 0, LOW:OWN], 0, 1)
    halo(0, x.at[:, 0, OWN : OWN + 8], x.at[:, 0, END:HIGH], 0, -1)

    first = (2 * me).astype(F32)
    lane16 = lanes(16)
    row16 = rows_of(16)

    def next_row(ref, p):
        low = OWN + 16 * p
        if p < ND - 1:
            return ref[low + 1 : low + 17]
        return jnp.where(row16 == 15, 0.0, roll(ref[low : low + 16], -1, 0))

    for p in range(ND):
        low = OWN + 16 * p
        here = slice(low, low + 16)
        count = x[6, 0, here]
        count_e = jnp.minimum(count, jnp.where(lane16 == CX - 1, 0.0, roll(count, -1, 1)))
        count_n = jnp.minimum(count, next_row(x.at[6, 0], p))
        sums = [0.0] * 4
        for l in range(2):
            thick = x[l, 0, here]
            de = jnp.where(first + l < count_e, 0.5 * (thick + roll(thick, -1, 1)), 0.0)
            dn = jnp.where(first + l < count_n, 0.5 * (thick + next_row(x.at[l, 0], p)), 0.0)
            new = [de, dn, x[2 + l, 0, here] * de, x[4 + l, 0, here] * dn]
            sums = [a + b for a, b in zip(sums, new)]
        for f in range(4):
            main_send[p // 2, p % 2, 16 * f : 16 * f + 16] = sums[f]
    remote(main_send.at[:, other], pair_in, sent, pair_got, member(partner)).start()

    fetch_c.wait()
    rows_c = slice(8, CY + 8)

    def send_tracers(i):
        part = slice(0, 2) if i == 0 else slice(2, NTR)

        @pl.when(me > 0)
        def _():
            remote(
                c.at[part, 0, rows_c], below.at[part], up_sent, up_got, member((me + ND - 1) % ND)
            ).start()

        @pl.when(me < ND - 1)
        def _():
            remote(
                c.at[part, 1, rows_c], above.at[part], down_sent, down_got, member((me + 1) % ND)
            ).start()

    send_tracers(0)

    got(pair_got, 256)
    chips = [(chip + k) % 4 for k in range(1, 4)]
    for q in range(4):
        chip_sum[q] = main_send[q, core] + pair_in[q]
    for q in chips:
        remote(chip_sum.at[q], main_in.at[chip], sent, rs_got, member(2 * q + core)).start()

    def pack_more(low, shift, east, west):
        old = state[1, 0, OWN + low : OWN + low + 8]
        east = jnp.where(between(lane8, shift + 24, shift + 32), roll(old, 40 + shift, 1), east)
        for p in range(2 * NTR):
            plane = c[p // 2, p % 2, 8 + low : 16 + low]
            west = jnp.where(lane8 == shift + 48 + p, roll(plane, shift + 48 + p, 1), west)
            east = jnp.where(lane8 == shift + 49 + p, roll(plane, shift + 50 + p, 1), east)
        return east, west

    pack_sides(1, late, pack_more)

    halo(1, side_pack.at[1, 0], side_in.at[1, 0], 1, 0)
    halo(1, side_pack.at[1, 1], side_in.at[1, 1], -1, 0)
    halo(1, state.at[:, 0, END - 16 : END], state.at[:, 0, 0:OWN], 0, 1)
    halo(1, state.at[:, 0, OWN : OWN + 8], state.at[:, 0, END:HIGH], 0, -1)
    halo(1, c.at[:, :, CY : CY + 8], c.at[:, :, 0:8], 0, 1)
    halo(1, c.at[:, :, 8:16], c.at[:, :, CY + 8 : CY + 16], 0, -1)

    @pl.when(me == 0)
    def _():
        above[...] = jnp.zeros_like(above)

    @pl.when(me == ND - 1)
    def _():
        below[...] = jnp.zeros_like(below)

    for ref in (x, state):
        for k in range(2):
            ref[:, k, HIGH:RX] = jnp.zeros((ref.shape[0], RX - HIGH, CX), F32)
    state[2, 1, 0:LOW] = jnp.zeros((LOW, CX), F32)

    has_n = ty < TROWS - 1
    has_s = ty > 0

    def unpack_sides(phase, fields, extra=None):
        side = (lane8 < 8) | (lane8 >= CX - 8)
        for i in range(-1, 17):
            if i < 0:
                west, east, shift, ok = corner_in[0], corner_in[1], 56 * phase, side & has_s
            elif i == 16:
                west, east, shift, ok = corner_in[2], corner_in[3], 56 * phase, side & has_n
            else:
                j = 8 * (i % 8)
                west, east = side_in[phase, 0, j : j + 8], side_in[phase, 1, j : j + 8]
                shift, ok = 64 * (i // 8), side
            low = OWN + 8 * i
            for f, ref in enumerate(fields):
                start = shift + 8 * f + 8
                value = roll(jnp.where(between(lane8, start, start + 8), east, west), -start, 1)
                value = jnp.where(ok, value, 0.0)
                if extra is not None and f == 1 and 0 <= i < 16:
                    value = jnp.where(lane8 == CX - 9, roll(west, 88 - shift, 1), value)
                ref[low : low + 8] = value
            if extra is not None and 0 <= i < 16:
                extra(8 * i, shift, west, east)

    got(halo_got.at[0], 272)
    unpack_sides(0, [x.at[f, 1] for f in range(7)])

    @pl.when(jnp.logical_not(has_s))
    def _():
        x[:, 0, LOW:OWN] = jnp.zeros((7, 8, CX), F32)

    @pl.when(jnp.logical_not(has_n))
    def _():
        x[:, 0, END:HIGH] = jnp.zeros((7, 8, CX), F32)

    def shifted(pair, steps):
        lane = lanes(pair[0].shape[0])
        edge = lane == (0 if steps > 0 else CX - 1)
        main, side = (roll(value, steps, 1) for value in pair)
        return jnp.where(edge, side, main), jnp.where(edge, main, side)

    def both(ref, low, size):
        return ref[0, low : low + size], ref[1, low : low + size]

    step = 24
    for low in range(LOW, HIGH, step):
        here = slice(low, low + step)
        count = both(x.at[6], low, step)
        count_e = shifted(count, -1)
        count_n = both(x.at[6], low + 1, step)
        thick = [both(x.at[l], low, step) for l in range(2)]
        thick_e = [shifted(thick[l], -1) for l in range(2)]
        for k in range(2):
            min_e = jnp.minimum(count[k], count_e[k])
            min_n = jnp.minimum(count[k], count_n[k])
            sums = [0.0] * 4
            for l in range(2):
                north = x[l, k, low + 1 : low + 1 + step]
                de = jnp.where(first + l < min_e, 0.5 * (thick[l][k] + thick_e[l][k]), 0.0)
                dn = jnp.where(first + l < min_n, 0.5 * (thick[l][k] + north), 0.0)
                face_e[l, k, here] = de
                face_n[l, k, here] = dn
                new = [de, dn, x[2 + l, k, here] * de, x[4 + l, k, here] * dn]
                sums = [a + b for a, b in zip(sums, new)]
            for f in range(4):
                local[f, k, here] = sums[f]

    def put_block(i, block):
        edge_send[i // EB, 8 * (i % EB) : 8 * (i % EB) + 8] = block

    for i in range(9):
        block = jnp.zeros((8, CX), F32)
        for j in range(2):
            low = LOW + 72 * j + 8 * i
            for f in range(4):
                start = 64 * j + 16 * f
                block = jnp.where(
                    lane8 == start, roll(local[f, 0, low : low + 8], start + 1, 1), block
                )
                block = jnp.where(
                    between(lane8, start + 1, start + 16),
                    roll(local[f, 1, low : low + 8], start + 9, 1),
                    block,
                )
        put_block(i, block)
    for f in range(4):
        put_block(9 + f, local[f, 0, END - 1 : END + 7])
        put_block(13 + f, local[f, 0, LOW:OWN])
    for i in range(17, NE * EB):
        put_block(i, jnp.zeros((8, CX), F32))

    owner = core == 0

    @pl.when(owner)
    def _():
        for q in chips:
            remote(edge_send.at[q], edge_in.at[me], edge_sent, edge_got, member(2 * q)).start()

    @pl.when(jnp.logical_not(owner))
    def _():
        for q in chips + [chip]:
            remote(edge_send.at[q], edge_in.at[me], edge_sent, edge_got, member(2 * q)).start()

    @pl.when(outer)
    def _():
        for i in range(4):
            low = OWN + 32 * i
            here = slice(low, low + 32)
            flux = both(local.at[2], low, 32)
            value = flux[0] - shifted(flux, 1)[0] + local[3, 0, here] - local[3, 0, low - 1 : low + 31]
            outer_send[i // 2, 32 * (i % 2) : 32 * (i % 2) + 32] = value
        for j in range(2):
            low = OWN + 64 * j
            outer_send[j, 64:128] = local[0, 0, low : low + 64]
            outer_send[j, 128:200] = local[1, 0, low - 8 : low + 64]
            block = jnp.zeros((8, CX), F32)
            for r in range(8):
                turned = roll(local[0, 1, low + 8 * r : low + 8 * r + 8], r + 1, 1)
                block = jnp.where(lane8 == r, turned, block)
            outer_send[j, 200:208] = block
        remote(outer_send.at[other], outer_pair, outer_sent, half_got, member(partner)).start()

    got(rs_got, 192)
    mine = chip_sum[chip]
    for q in chips:
        mine = mine + main_in[q]
    main_all[chip, core] = mine
    piece = main_all.at[chip, core]
    for q in chips:
        remote(piece, piece, sent, ag_got, member(2 * q + core)).start()

    @pl.when(owner)
    def _():
        got(edge_got, 7 * 8 * EB)
        edge = edge_send[chip]
        for peer in peers:
            edge = edge + edge_in[peer]
        edge_all[chip] = edge
        for peer in peers:
            remote(edge_all.at[chip], edge_all.at[chip], edge_sent, edge_all_got, member(peer)).start()

    @pl.when(outer)
    def _():
        got(half_got, 208)
        outer_sum[...] = outer_send[core] + outer_pair[...]
        middle_chip = jnp.where(upper, 2, ND - 4)
        remote(outer_sum, outer_in, outer_sent, outer_got, member(middle_chip + core)).start()

    send_tracers(1)

    got(halo_got.at[1], 392)

    def put_tracers(low, shift, west, east):
        for p in range(2 * NTR):
            value = jnp.where(lane8 <= shift + 48 + p, east, west)
            edge_c[p // 2, p % 2, low : low + 8] = roll(value, 79 - shift - p, 1)

    unpack_sides(1, [state.at[f, 1] for f in range(3)], put_tracers)
    left(sent_late, 392)

    @pl.when(jnp.logical_not(has_s))
    def _():
        state[:, 0, LOW:OWN] = jnp.zeros((3, 8, CX), F32)

    @pl.when(jnp.logical_not(has_n))
    def _():
        state[:, 0, END:HIGH] = jnp.zeros((3, 8, CX), F32)

    for low in range(LOW, HIGH, step):
        here = slice(low, low + step)
        is_wet = [jnp.where(value > 0.0, 1.0, 0.0) for value in both(x.at[6], low, step)]
        wet_e = shifted(is_wet, -1)
        wet_n = [jnp.where(value > 0.0, 1.0, 0.0) for value in both(x.at[6], low + 1, step)]
        for k in range(2):
            tw[k, here] = tau * is_wet[k]
            ae[k, here] = (1.0 - tau) * (is_wet[k] * wet_e[k])
            an[k, here] = (1.0 - tau) * (is_wet[k] * wet_n[k])
            be[k, here] = (tau * coupling) * (is_wet[k] * wet_e[k])
            bn[k, here] = (tau * coupling) * (is_wet[k] * wet_n[k])

    got(ag_got, 192)
    half = main_all.at[:, core]
    remote(half, half, sent, forward_got, member(partner)).start()

    @pl.when(owner)
    def _():
        got(edge_all_got, 3 * 8 * EB)

    @pl.when(jnp.logical_not(owner))
    def _():
        got(edge_all_got, 4 * 8 * EB)

    got(forward_got, 256)

    def block_of(i):
        return edge_all[i // EB, 8 * (i % EB) : 8 * (i % EB) + 8]

    for f in range(4):
        for p in range(ND):
            low = OWN + 16 * p
            total[f, 0, low : low + 16] = main_all[p // 2, p % 2, 16 * f : 16 * f + 16]
        total[f, 0, END - 1 : END + 7] = block_of(9 + f)
        total[f, 0, HIGH - 1 : HIGH] = jnp.zeros((1, CX), F32)
        total[f, 0, LOW:OWN] = block_of(13 + f)
    rim = (lane8 < 7) | (lane8 >= CX - 8)
    for i in range(18):
        block = block_of(i % 9)
        shift = 64 * (i // 9)
        here = slice(LOW + 8 * i, LOW + 8 * i + 8)
        for f in range(4):
            edge = jnp.where(lane8 == CX - 1, roll(block, CX - 1 - 16 * f - shift, 1), total[f, 0, here])
            side = jnp.where(rim, roll(block, -(9 + 16 * f + shift), 1), 0.0)
            total[f, 0, here] = edge
            total[f, 1, here] = side
            for k, value in enumerate((edge, side)):
                if f == 2:
                    ce[k, here] = be[k, here] * value
                if f == 3:
                    cn[k, here] = bn[k, here] * value
        for k in range(2):
            be[k, here] = be[k, here] * total[0, k, here]
            bn[k, here] = bn[k, here] * total[1, k, here]

    def substep(i, carry):
        def rise(low):
            here = slice(low, low + step)
            east = both(state.at[1], low, step)
            west = shifted(east, 1)
            north = both(state.at[2], low, step)
            south = both(state.at[2], low - 1, step)
            level = []
            for k in range(2):
                value = state[0, k, here] - tw[k, here] * (east[k] - west[k] + north[k] - south[k])
                state[0, k, here] = value
                level.append(value)
            return level, east, north

        def move(low, level, east, north):
            here = slice(low, low + step)
            level_e = shifted(level, -1)
            level_n = both(state.at[0], low + 1, step)
            for k in range(2):
                state[1, k, here] = ae[k, here] * east[k] - be[k, here] * (level_e[k] - level[k]) + ce[k, here]
                state[2, k, here] = an[k, here] * north[k] - bn[k, here] * (level_n[k] - level[k]) + cn[k, here]

        held = rise(LOW)
        for low in range(LOW, HIGH, step):
            coming = rise(low + step) if low + step < HIGH else None
            move(low, *held)
            held = coming
        return carry

    lax.fori_loop(0, NSUB, substep, 0)

    flow_rows = [(OWN - 8, 8)] + [(OWN + 32 * i, 32) for i in range(4)]
    for low, size in flow_rows:
        here = slice(low, low + size)
        shift_n = state[2, 0, here] - coupling * total[3, 0, here]
        for l in range(2):
            flow_n[l, here] = face_n[l, 0, here] * (x[4 + l, 0, here] + shift_n)
        flow_t[here] = total[3, 0, here] + total[1, 0, here] * shift_n
        prod_n[here] = shift_n

    for i in range(4):
        low = OWN + 32 * i
        here = slice(low, low + 32)
        mine = slice(32 * i, 32 * i + 32)
        shift_e = [state[1, k, here] - coupling * total[2, k, here] for k in range(2)]
        flow = [total[2, k, here] + total[0, k, here] * shift_e[k] for k in range(2)]
        whole_div[mine] = flow[0] - shifted(flow, 1)[0] + flow_t[here] - flow_t[low - 1 : low + 31]
        count = x[6, 0, here]
        divs = []
        for l in range(2):
            flow = [face_e[l, k, here] * (x[2 + l, k, here] + shift_e[k]) for k in range(2)]
            fe = flow[0]
            fw = shifted(flow, 1)[0]
            fn = flow_n[l, here]
            fs = flow_n[l, low - 1 : low + 31]
            divs.append(fe - fw + fn - fs)
            gain = jnp.where(first + l < count, tracer_time / x[l, 0, here], 0.0)
            plus_e, minus_w = jnp.maximum(fe, 0.0), jnp.minimum(fw, 0.0)
            plus_n, minus_s = jnp.maximum(fn, 0.0), jnp.minimum(fs, 0.0)
            coef[l, 0, mine] = gain * (plus_e - fe)
            coef[l, 1, mine] = gain * (fw - minus_w)
            coef[l, 2, mine] = gain * (plus_n - fn)
            coef[l, 3, mine] = gain * (fs - minus_s)
            coef[l, 4, mine] = 1.0 - gain * (plus_e - minus_w + plus_n - minus_s)
            coef[l, 5, mine] = gain
        div_1[mine] = divs[1]
        pair_send[mine] = divs[0] + divs[1]

    @pl.when(jnp.logical_not(outer))
    def _():
        got(outer_got, 208)
        base = pl.multiple_of(OWN + 64 * core, 8)
        here = pl.ds(base, 64)
        shift_e = [state[1, k, here] - coupling * total[2, k, here] for k in range(2)]
        flow = outer_in[64:128] * shift_e[0]
        block = outer_in[200:208]
        column = jnp.concatenate([roll(block, -r, 1) for r in range(8)], axis=0)
        west = jnp.where(lanes(64) == 0, column * roll(shift_e[1], 1, 1), roll(flow, 1, 1))
        flow_t[0:72] = outer_in[128:200] * prod_n[pl.ds(pl.multiple_of(base - 8, 8), 72)]
        value = outer_in[0:64] + flow - west + flow_t[8:72] - flow_t[7:71]
        outer_div[core] = value
        pair_send[CY : CY + 64] = value

    remote(pair_send, pair_div, sent, div_got, member(partner)).start()

    s_out[0] = state[0, 0, rows_own]
    e_out[0] = state[1, 0, rows_own]
    n_out[0] = state[2, 0, rows_own]

    lane32 = lanes(32)
    for l in range(2):
        for i in range(4):
            mine = slice(32 * i, 32 * i + 32)
            low = 8 + 32 * i
            a_e, a_w, a_n, a_s, a_c = (coef[l, j, mine] for j in range(5))
            for m in range(NTR):
                value = c[m, l, low : low + 32]
                edge = edge_c[m, l, mine]
                value_e = jnp.where(lane32 == CX - 1, edge, roll(value, -1, 1))
                value_w = jnp.where(lane32 == 0, edge, roll(value, 1, 1))
                part[m, l, mine] = (
                    a_c * value
                    + a_e * value_e
                    + a_w * value_w
                    + a_n * c[m, l, low + 1 : low + 33]
                    + a_s * c[m, l, low - 1 : low + 31]
                )

    left(sent, 1360)

    @pl.when(owner)
    def _():
        left(edge_sent, 10 * 8 * EB)

    @pl.when(jnp.logical_not(owner))
    def _():
        left(edge_sent, 4 * 8 * EB)

    @pl.when(outer)
    def _():
        left(outer_sent, 416)

    got(div_got, 192)

    @pl.when(jnp.logical_not(outer))
    def _():
        outer_div[other] = pair_div[CY : CY + 64]

    @pl.when(outer)
    def _():
        outer_div[...] = jnp.zeros_like(outer_div)

    odd = core == 1
    for i in range(4):
        mine = slice(32 * i, 32 * i + 32)
        beyond = outer_div[i // 2, 32 * (i % 2) : 32 * (i % 2) + 32]
        near = pair_div[mine]
        here = pair_send[mine]
        deeper = jnp.where(
            upper,
            whole_div[mine] - here - beyond - jnp.where(odd, near, 0.0),
            beyond + jnp.where(odd, 0.0, near),
        )
        bottom = -deeper
        middle = -(div_1[mine] + deeper)
        top = jnp.where(me == 0, 0.0, -(here + deeper))
        for l in range(2):
            under_flow, over_flow = (middle, top) if l == 0 else (bottom, middle)
            gain = coef[l, 5, mine]
            lift[l, 0, mine] = gain * (jnp.minimum(under_flow, 0.0) - jnp.maximum(over_flow, 0.0))
            lift[l, 1, mine] = gain * jnp.maximum(under_flow, 0.0)
            lift[l, 2, mine] = -gain * jnp.minimum(over_flow, 0.0)

    @pl.when(me < ND - 1)
    def _():
        got(up_got, NTR * CY)
        left(down_sent, NTR * CY)

    @pl.when(me > 0)
    def _():
        got(down_got, NTR * CY)
        left(up_sent, NTR * CY)


def store(part, s_ref, e_ref, n_ref, c, below, above, lift, c_out, s_out, e_out, n_out, new_c, sem):
    copies = [
        pltpu.make_async_copy(source, target, sem.at[NTR + i])
        for i, (source, target) in enumerate([(s_ref, s_out), (e_ref, e_out), (n_ref, n_out)])
    ]
    for copy in copies:
        copy.start()
    for pair in range(0, NTR, 2):
        for l in range(2):
            for i in range(4):
                mine = slice(32 * i, 32 * i + 32)
                low = 8 + 32 * i
                a_c, a_b, a_a = (lift[l, j, mine] for j in range(3))
                for m in (pair, pair + 1):
                    under = c[m, 1, low : low + 32] if l == 0 else below[m, mine]
                    over = above[m, mine] if l == 0 else c[m, 0, low : low + 32]
                    new_c[m, l, mine] = (
                        part[m, l, mine] + a_c * c[m, l, low : low + 32] + a_b * under + a_a * over
                    )
        for m in (pair, pair + 1):
            copy = pltpu.make_async_copy(new_c.at[m], c_out.at[m, :, 0], sem.at[m])
            copy.start()
            copies.append(copy)
    for copy in copies:
        copy.wait()


def body(thickness, u_layer, v_layer, tracers, sea_level, u_column, v_column, wet_cells, levels):
    any_spec = pl.BlockSpec(memory_space=pl.ANY)
    near_spec = pl.BlockSpec(memory_space=pltpu.VMEM)

    def vmem(*shape):
        return pltpu.VMEM(shape, F32)

    plane = vmem(CY, CX)
    wide = vmem(2, RX, CX)
    wide2 = vmem(2, 2, RX, CX)
    column_c = vmem(NTR, CY, CX)
    flat = pltpu.VMEM((CY, CX), jnp.int32)
    quarter = vmem(4, 64, CX)
    halves = vmem(4, 2, 64, CX)
    edges = vmem(NE, 8 * EB, CX)
    dma = pltpu.SemaphoreType.DMA
    shapes = [tracers.shape] + [sea_level.shape] * 3
    results = pl.pallas_call(
        kernel,
        out_shape=(
            vmem(NTR, 2, CY, CX), *(pltpu.VMEM(shape, F32) for shape in shapes[1:]),
            vmem(NTR, 2, CY + 16, CX), column_c, column_c, vmem(2, 3, CY, CX),
        ),
        in_specs=[pl.BlockSpec(memory_space=pltpu.HBM)] * 9,
        out_specs=(near_spec,) * 8,
        scratch_shapes=[
            vmem(7, 2, RX, CX), vmem(3, 2, RX, CX), flat, flat,
            vmem(2, 2, 64, CX), vmem(2, 2, 64, CX), vmem(2, 2, 8, CX), vmem(4, 8, CX), vmem(11 * CY, CX),
            vmem(NTR, 2, CY, CX),
            halves, quarter, quarter, quarter, halves,
            edges, vmem(ND, 8 * EB, CX), edges,
            wide2, wide2, vmem(4, 2, RX, CX), vmem(4, 2, RX, CX),
            wide, wide, wide, wide, wide, wide, wide,
            vmem(2, 208, CX), vmem(208, CX), vmem(208, CX), vmem(208, CX), vmem(2, 64, CX),
            vmem(2, RX, CX), vmem(RX, CX), vmem(RX, CX), vmem(2, 6, CY, CX),
            plane, plane, vmem(CY + 64, CX), vmem(CY + 64, CX),
            dma((2,)), dma, dma, dma, dma, dma, dma,
            dma((2,)), dma, dma, dma, dma, dma, dma, dma, dma,
            dma, dma, dma,
        ],
        compiler_params=pltpu.CompilerParams(
            collective_id=0, has_side_effects=True, vmem_limit_bytes=48 * 1024 * 1024
        ),
    )(*[
        pltpu.with_memory_space_constraint(x, pltpu.HBM)
        for x in (thickness, u_layer, v_layer, tracers, sea_level, u_column, v_column, wet_cells, levels)
    ])
    return pl.pallas_call(
        store,
        out_shape=tuple(jax.ShapeDtypeStruct(shape, F32) for shape in shapes),
        in_specs=[near_spec] * 8,
        out_specs=(any_spec,) * 4,
        scratch_shapes=[vmem(NTR, 2, CY, CX), dma((NTR + 3,))],
    )(*[pltpu.with_memory_space_constraint(x, pltpu.VMEM) for x in results])


def solution(mesh):
    return jax.shard_map(
        body,
        mesh=mesh,
        in_specs=(
            P("depth", "tiles", None, None),
            P("depth", "tiles", None, None),
            P("depth", "tiles", None, None),
            P(None, "depth", "tiles", None, None),
            P("tiles", None, None),
            P("tiles", None, None),
            P("tiles", None, None),
            P("tiles", None, None),
            P("tiles", None, None),
        ),
        out_specs=(
            P(None, "depth", "tiles", None, None),
            P("tiles", None, None),
            P("tiles", None, None),
            P("tiles", None, None),
        ),
        check_vma=False,
    )
```

```python
import functools

import jax
import jax.numpy as jnp
from jax import lax
from jax.experimental import pallas as pl
from jax.experimental.pallas import tpu as pltpu
from jax.sharding import PartitionSpec as P

TROWS = 8
NSUB = 8
NTR = 6
ND = 8
NE = 4
EB = 5
CY = 128
CX = 128
RX = CY + 32
OWN = 16
END = OWN + CY
LOW = OWN - 8
HIGH = END + 8

tau = 0.45
coupling = 1.0 / 16
tracer_time = 0.1

MESH = pl.DeviceIdType.MESH
F32 = jnp.float32


def roll(x, shift, axis):
    shift = shift % x.shape[axis]
    return x if shift == 0 else pltpu.roll(x, shift, axis)


def lanes(rows, width=CX):
    return lax.broadcasted_iota(jnp.int32, (rows, width), 1)


def rows_of(rows, width=CX):
    return lax.broadcasted_iota(jnp.int32, (rows, width), 0)


def between(x, low, high):
    return (x >= low) & (x < high)


def kernel(
    h_in, u_in, v_in, c_in, sea_in, uc_in, vc_in, wet_in, lev_in,
    part, s_out, e_out, n_out, c, below, above, lift,
    x, state, wet, lev,
    side_pack, side_in, corner_pack, corner_in, sizes,
    edge_c,
    main_send, pair_in, chip_sum, main_in, main_all,
    edge_send, edge_in, edge_all,
    face_e, face_n, local, total,
    tw, ae, an, be, bn, ce, cn, wet_e_all, wet_n_all, state_b,
    outer_send, outer_pair, outer_sum, outer_in, outer_div,
    flow_n, flow_t, flow_w, flow_e, prod_n, coef, div_1, whole_div, pair_send, pair_div,
    loc_sem, sent, sent_late, edge_sent, outer_sent, up_sent, down_sent,
    halo_got, pair_got, rs_got, ag_got, forward_got, edge_got, edge_all_got, half_got, outer_got,
    up_got, down_got, div_got,
):
    me = lax.axis_index("depth")
    tile = lax.axis_index("tiles")
    tx = tile // TROWS
    ty = tile % TROWS
    chip = me // 2
    core = me % 2
    other = 1 - core
    partner = 2 * chip + other
    upper = me < ND // 2
    outer = (me < 2) | (me >= ND - 2)
    cols = 8

    def tile_at(dx, dy):
        return ((tx + dx + cols) % cols) * TROWS + (ty + dy + TROWS) % TROWS

    def member(which):
        return {"tiles": tile, "depth": which}

    def beside(dx, dy):
        return {"tiles": tile_at(dx, dy), "depth": me}

    def remote(source, target, send, recv, where):
        return pltpu.make_async_remote_copy(
            src_ref=source, dst_ref=target, send_sem=send, recv_sem=recv,
            device_id=where, device_id_type=MESH,
        )

    around = [(1, 0), (-1, 0), (0, 1), (0, -1), (1, 1), (-1, 1), (1, -1), (-1, -1)]
    rows_own = slice(OWN, END)

    def got(sem, rows):
        remote(sizes.at[0:rows], sizes.at[0:rows], sem, sem, member(partner)).wait_recv()

    def left(sem, rows):
        remote(sizes.at[0:rows], sizes.at[0:rows], sem, sem, member(partner)).wait_send()

    def fetch(source, target):
        pltpu.make_async_copy(source, target, loc_sem.at[0]).start()

    barrier = pltpu.get_barrier_semaphore()
    for dx, dy in around:
        pl.semaphore_signal(barrier, inc=1, device_id=beside(dx, dy), device_id_type=MESH)
    fetch(h_in.at[:, 0], x.at[0:2, 0, rows_own])
    fetch(wet_in.at[0], wet)
    fetch(lev_in.at[0], lev)
    fetch(u_in.at[:, 0], x.at[2:4, 0, rows_own])
    fetch(v_in.at[:, 0], x.at[4:6, 0, rows_own])
    fetch(sea_in.at[0], state.at[0, 0, rows_own])
    fetch(uc_in.at[0], state.at[1, 0, rows_own])
    fetch(vc_in.at[0], state.at[2, 0, rows_own])
    peers = [(me + k) % ND for k in range(1, ND)]
    for peer in peers:
        pl.semaphore_signal(barrier, inc=1, device_id=member(peer), device_id_type=MESH)
    fetch_c = pltpu.make_async_copy(c_in.at[:, :, 0], c.at[:, :, 8 : CY + 8], loc_sem.at[1])
    fetch_c.start()

    fetched = 11 * CY
    pltpu.make_async_copy(sizes.at[0:fetched], sizes.at[0:fetched], loc_sem.at[0]).wait()

    lane8 = lanes(8)
    x[6, 0, rows_own] = (wet[...] * lev[...]).astype(F32)

    def pack_sides(phase, fields, extra=None):
        for i in range(8):
            east = west = jnp.zeros((8, CX), F32)
            for j in range(2):
                low = OWN + 64 * j + 8 * i
                for f, ref in enumerate(fields):
                    turned = roll(ref[low : low + 8], 8 * f + 8 + 64 * j, 1)
                    start = 64 * j + 8 * f
                    west = jnp.where(between(lane8, start + 8, start + 16), turned, west)
                    east = jnp.where(between(lane8, start, start + 8), turned, east)
                if extra is not None:
                    east, west = extra(64 * j + 8 * i, 64 * j, east, west)
            side_pack[phase, 0, 8 * i : 8 * i + 8] = east
            side_pack[phase, 1, 8 * i : 8 * i + 8] = west

    early = [x.at[f, 0] for f in range(7)]
    late = [state.at[f, 0] for f in range(3)]
    pack_sides(0, early)

    for j, low in enumerate((OWN, END - 8)):
        east = west = jnp.zeros((8, CX), F32)
        for f, ref in enumerate(early + late):
            turned = roll(ref[low : low + 8], 8 * f + 8, 1)
            west = jnp.where(between(lane8, 8 * f + 8, 8 * f + 16), turned, west)
            east = jnp.where(between(lane8, 8 * f, 8 * f + 8), turned, east)
        corner_pack[0, j] = east
        corner_pack[1, j] = west

    pl.semaphore_wait(barrier, len(around) + ND - 1)

    def halo(phase, source, target, dx, dy):
        sem = sent if phase == 0 else sent_late
        remote(source, target, sem, halo_got.at[phase], beside(dx, dy)).start()

    halo(0, side_pack.at[0, 0], side_in.at[0, 0], 1, 0)
    halo(0, side_pack.at[0, 1], side_in.at[0, 1], -1, 0)
    halo(0, corner_pack.at[0, 1], corner_in.at[0], 1, 1)
    halo(0, corner_pack.at[1, 1], corner_in.at[1], -1, 1)
    halo(0, corner_pack.at[0, 0], corner_in.at[2], 1, -1)
    halo(0, corner_pack.at[1, 0], corner_in.at[3], -1, -1)
    halo(0, x.at[:, 0, END - 8 : END], x.at[:, 0, LOW:OWN], 0, 1)
    halo(0, x.at[:, 0, OWN : OWN + 8], x.at[:, 0, END:HIGH], 0, -1)

    first = (2 * me).astype(F32)
    lane16 = lanes(16)
    row16 = rows_of(16)

    def next_row(ref, p):
        low = OWN + 16 * p
        if p < ND - 1:
            return ref[low + 1 : low + 17]
        return jnp.where(row16 == 15, 0.0, roll(ref[low : low + 16], -1, 0))

    for p in range(ND):
        low = OWN + 16 * p
        here = slice(low, low + 16)
        count = x[6, 0, here]
        count_e = jnp.minimum(count, jnp.where(lane16 == CX - 1, 0.0, roll(count, -1, 1)))
        count_n = jnp.minimum(count, next_row(x.at[6, 0], p))
        sums = [0.0] * 4
        for l in range(2):
            thick = x[l, 0, here]
            de = jnp.where(first + l < count_e, 0.5 * (thick + roll(thick, -1, 1)), 0.0)
            dn = jnp.where(first + l < count_n, 0.5 * (thick + next_row(x.at[l, 0], p)), 0.0)
            new = [de, dn, x[2 + l, 0, here] * de, x[4 + l, 0, here] * dn]
            sums = [a + b for a, b in zip(sums, new)]
        for f in range(4):
            main_send[p // 2, p % 2, 16 * f : 16 * f + 16] = sums[f]
    remote(main_send.at[:, other], pair_in, sent, pair_got, member(partner)).start()

    fetch_c.wait()
    rows_c = slice(8, CY + 8)

    def send_tracers(i):
        part = slice(0, 2) if i == 0 else slice(2, NTR)

        @pl.when(me > 0)
        def _():
            remote(
                c.at[part, 0, rows_c], below.at[part], up_sent, up_got, member((me + ND - 1) % ND)
            ).start()

        @pl.when(me < ND - 1)
        def _():
            remote(
                c.at[part, 1, rows_c], above.at[part], down_sent, down_got, member((me + 1) % ND)
            ).start()

    send_tracers(0)

    got(pair_got, 256)
    chips = [(chip + k) % 4 for k in range(1, 4)]
    for q in range(4):
        chip_sum[q] = main_send[q, core] + pair_in[q]
    for q in chips:
        remote(chip_sum.at[q], main_in.at[chip], sent, rs_got, member(2 * q + core)).start()

    def pack_more(low, shift, east, west):
        old = state[1, 0, OWN + low : OWN + low + 8]
        east = jnp.where(between(lane8, shift + 24, shift + 32), roll(old, 40 + shift, 1), east)
        for p in range(2 * NTR):
            plane = c[p // 2, p % 2, 8 + low : 16 + low]
            west = jnp.where(lane8 == shift + 48 + p, roll(plane, shift + 48 + p, 1), west)
            east = jnp.where(lane8 == shift + 49 + p, roll(plane, shift + 50 + p, 1), east)
        return east, west

    pack_sides(1, late, pack_more)

    halo(1, side_pack.at[1, 0], side_in.at[1, 0], 1, 0)
    halo(1, side_pack.at[1, 1], side_in.at[1, 1], -1, 0)
    halo(1, state.at[:, 0, END - 16 : END], state.at[:, 0, 0:OWN], 0, 1)
    halo(1, state.at[:, 0, OWN : OWN + 8], state.at[:, 0, END:HIGH], 0, -1)
    halo(1, c.at[:, :, CY : CY + 8], c.at[:, :, 0:8], 0, 1)
    halo(1, c.at[:, :, 8:16], c.at[:, :, CY + 8 : CY + 16], 0, -1)

    @pl.when(me == 0)
    def _():
        above[...] = jnp.zeros_like(above)

    @pl.when(me == ND - 1)
    def _():
        below[...] = jnp.zeros_like(below)

    for ref in (x, state):
        for k in range(2):
            ref[:, k, HIGH:RX] = jnp.zeros((ref.shape[0], RX - HIGH, CX), F32)
    state[2, 1, 0:LOW] = jnp.zeros((LOW, CX), F32)
    state_b[2, :, 0:LOW] = jnp.zeros((2, LOW, CX), F32)

    has_n = ty < TROWS - 1
    has_s = ty > 0

    def unpack_sides(phase, fields, extra=None):
        side = (lane8 < 8) | (lane8 >= CX - 8)
        for i in range(-1, 17):
            if i < 0:
                west, east, shift, ok = corner_in[0], corner_in[1], 56 * phase, side & has_s
            elif i == 16:
                west, east, shift, ok = corner_in[2], corner_in[3], 56 * phase, side & has_n
            else:
                j = 8 * (i % 8)
                west, east = side_in[phase, 0, j : j + 8], side_in[phase, 1, j : j + 8]
                shift, ok = 64 * (i // 8), side
            low = OWN + 8 * i
            for f, ref in enumerate(fields):
                start = shift + 8 * f + 8
                value = roll(jnp.where(between(lane8, start, start + 8), east, west), -start, 1)
                value = jnp.where(ok, value, 0.0)
                if extra is not None and f == 1 and 0 <= i < 16:
                    value = jnp.where(lane8 == CX - 9, roll(west, 88 - shift, 1), value)
                ref[low : low + 8] = value
            if extra is not None and 0 <= i < 16:
                extra(8 * i, shift, west, east)

    got(halo_got.at[0], 272)
    unpack_sides(0, [x.at[f, 1] for f in range(7)])

    @pl.when(jnp.logical_not(has_s))
    def _():
        x[:, 0, LOW:OWN] = jnp.zeros((7, 8, CX), F32)

    @pl.when(jnp.logical_not(has_n))
    def _():
        x[:, 0, END:HIGH] = jnp.zeros((7, 8, CX), F32)

    def shifted(pair, steps):
        lane = lanes(pair[0].shape[0])
        edge = lane == (0 if steps > 0 else CX - 1)
        main, side = (roll(value, steps, 1) for value in pair)
        return jnp.where(edge, side, main), jnp.where(edge, main, side)

    def both(ref, low, size):
        return ref[0, low : low + size], ref[1, low : low + size]

    step = 24
    for low in range(LOW, HIGH, step):
        here = slice(low, low + step)
        count = both(x.at[6], low, step)
        count_e = shifted(count, -1)
        count_n = both(x.at[6], low + 1, step)
        thick = [both(x.at[l], low, step) for l in range(2)]
        thick_e = [shifted(thick[l], -1) for l in range(2)]
        for k in range(2):
            min_e = jnp.minimum(count[k], count_e[k])
            min_n = jnp.minimum(count[k], count_n[k])
            sums = [0.0] * 4
            for l in range(2):
                north = x[l, k, low + 1 : low + 1 + step]
                de = jnp.where(first + l < min_e, 0.5 * (thick[l][k] + thick_e[l][k]), 0.0)
                dn = jnp.where(first + l < min_n, 0.5 * (thick[l][k] + north), 0.0)
                face_e[l, k, here] = de
                face_n[l, k, here] = dn
                new = [de, dn, x[2 + l, k, here] * de, x[4 + l, k, here] * dn]
                sums = [a + b for a, b in zip(sums, new)]
            for f in range(4):
                local[f, k, here] = sums[f]

    def put_block(i, block):
        edge_send[i // EB, 8 * (i % EB) : 8 * (i % EB) + 8] = block

    for i in range(9):
        block = jnp.zeros((8, CX), F32)
        for j in range(2):
            low = LOW + 72 * j + 8 * i
            for f in range(4):
                start = 64 * j + 16 * f
                block = jnp.where(
                    lane8 == start, roll(local[f, 0, low : low + 8], start + 1, 1), block
                )
                block = jnp.where(
                    between(lane8, start + 1, start + 16),
                    roll(local[f, 1, low : low + 8], start + 9, 1),
                    block,
                )
        put_block(i, block)
    for f in range(4):
        put_block(9 + f, local[f, 0, END - 1 : END + 7])
        put_block(13 + f, local[f, 0, LOW:OWN])
    for i in range(17, NE * EB):
        put_block(i, jnp.zeros((8, CX), F32))

    owner = core == 0

    @pl.when(owner)
    def _():
        for q in chips:
            remote(edge_send.at[q], edge_in.at[me], edge_sent, edge_got, member(2 * q)).start()

    @pl.when(jnp.logical_not(owner))
    def _():
        for q in chips + [chip]:
            remote(edge_send.at[q], edge_in.at[me], edge_sent, edge_got, member(2 * q)).start()

    got(rs_got, 192)
    mine = chip_sum[chip]
    for q in chips:
        mine = mine + main_in[q]
    main_all[chip, core] = mine
    piece = main_all.at[chip, core]
    for q in chips:
        remote(piece, piece, sent, ag_got, member(2 * q + core)).start()

    @pl.when(outer)
    def _():
        for i in range(4):
            low = OWN + 32 * i
            here = slice(low, low + 32)
            flux = both(local.at[2], low, 32)
            value = flux[0] - shifted(flux, 1)[0] + local[3, 0, here] - local[3, 0, low - 1 : low + 31]
            outer_send[i // 2, 32 * (i % 2) : 32 * (i % 2) + 32] = value
        for j in range(2):
            low = OWN + 64 * j
            outer_send[j, 64:128] = local[0, 0, low : low + 64]
            outer_send[j, 128:200] = local[1, 0, low - 8 : low + 64]
            block = jnp.zeros((8, CX), F32)
            for r in range(8):
                turned = roll(local[0, 1, low + 8 * r : low + 8 * r + 8], r + 1, 1)
                block = jnp.where(lane8 == r, turned, block)
            outer_send[j, 200:208] = block
        remote(outer_send.at[other], outer_pair, outer_sent, half_got, member(partner)).start()

    @pl.when(owner)
    def _():
        got(edge_got, 7 * 8 * EB)
        edge = edge_send[chip]
        for peer in peers:
            edge = edge + edge_in[peer]
        edge_all[chip] = edge
        for peer in peers:
            remote(edge_all.at[chip], edge_all.at[chip], edge_sent, edge_all_got, member(peer)).start()

    @pl.when(outer)
    def _():
        got(half_got, 208)
        outer_sum[...] = outer_send[core] + outer_pair[...]
        middle_chip = jnp.where(upper, 2, ND - 4)
        remote(outer_sum, outer_in, outer_sent, outer_got, member(middle_chip + core)).start()

    send_tracers(1)

    got(halo_got.at[1], 392)

    def put_tracers(low, shift, west, east):
        for p in range(2 * NTR):
            value = jnp.where(lane8 <= shift + 48 + p, east, west)
            edge_c[p // 2, p % 2, low : low + 8] = roll(value, 79 - shift - p, 1)

    unpack_sides(1, [state.at[f, 1] for f in range(3)], put_tracers)
    left(sent_late, 392)

    @pl.when(jnp.logical_not(has_s))
    def _():
        state[:, 0, LOW:OWN] = jnp.zeros((3, 8, CX), F32)

    @pl.when(jnp.logical_not(has_n))
    def _():
        state[:, 0, END:HIGH] = jnp.zeros((3, 8, CX), F32)

    for low in range(LOW, HIGH, step):
        here = slice(low, low + step)
        is_wet = [jnp.where(value > 0.0, 1.0, 0.0) for value in both(x.at[6], low, step)]
        wet_e = shifted(is_wet, -1)
        wet_n = [jnp.where(value > 0.0, 1.0, 0.0) for value in both(x.at[6], low + 1, step)]
        for k in range(2):
            tw[k, here] = tau * is_wet[k]
            ae[k, here] = (1.0 - tau) * (is_wet[k] * wet_e[k])
            an[k, here] = (1.0 - tau) * (is_wet[k] * wet_n[k])
            wet_e_all[k, here] = (tau * coupling) * (is_wet[k] * wet_e[k])
            wet_n_all[k, here] = (tau * coupling) * (is_wet[k] * wet_n[k])

    got(ag_got, 192)
    half = main_all.at[:, core]
    remote(half, half, sent, forward_got, member(partner)).start()

    @pl.when(owner)
    def _():
        got(edge_all_got, 3 * 8 * EB)

    @pl.when(jnp.logical_not(owner))
    def _():
        got(edge_all_got, 4 * 8 * EB)

    got(forward_got, 256)

    def block_of(i):
        return edge_all[i // EB, 8 * (i % EB) : 8 * (i % EB) + 8]

    rim = (lane8 < 7) | (lane8 >= CX - 8)
    last_lane = lane8 == CX - 1
    row8 = rows_of(8)
    for i in range(18):
        block = block_of(i % 9)
        shift = 64 * (i // 9)
        here = slice(LOW + 8 * i, LOW + 8 * i + 8)
        sums = []
        for f in range(4):
            if i == 0:
                main = block_of(13 + f)
            elif i == 17:
                main = jnp.where(row8 == 7, 0.0, roll(block_of(9 + f), -1, 0))
            else:
                p, part_low = (i - 1) // 2, 16 * f + 8 * ((i - 1) % 2)
                main = main_all[p // 2, p % 2, part_low : part_low + 8]
                if i == 16:
                    main = jnp.where(row8 == 7, jnp.broadcast_to(block_of(9 + f)[0:1], (8, CX)), main)
            main = jnp.where(last_lane, roll(block, CX - 1 - 16 * f - shift, 1), main)
            side = jnp.where(rim, roll(block, -(9 + 16 * f + shift), 1), 0.0)
            total[f, 0, here] = main
            total[f, 1, here] = side
            sums.append((main, side))
        for k in range(2):
            east, north = wet_e_all[k, here], wet_n_all[k, here]
            be[k, here] = east * sums[0][k]
            bn[k, here] = north * sums[1][k]
            ce[k, here] = east * sums[2][k]
            cn[k, here] = north * sums[3][k]

    def substep(old, new):
        bottom_row = rows_of(step) == step - 1

        def rise(low):
            here = slice(low, low + step)
            east = both(old.at[1], low, step)
            west = shifted(east, 1)
            north = both(old.at[2], low, step)
            south = both(old.at[2], low - 1, step)
            level = []
            for k in range(2):
                value = old[0, k, here] - tw[k, here] * (east[k] - west[k] + north[k] - south[k])
                new[0, k, here] = value
                level.append(value)
            return level, east, north

        def move(low, held, beyond):
            here = slice(low, low + step)
            level, east, north = held
            level_e = shifted(level, -1)
            for k in range(2):
                level_n = roll(level[k], -1, 0)
                if beyond is not None:
                    first_row = jnp.broadcast_to(beyond[0][k][0:1], (step, CX))
                    level_n = jnp.where(bottom_row, first_row, level_n)
                new[1, k, here] = ae[k, here] * east[k] - be[k, here] * (level_e[k] - level[k]) + ce[k, here]
                new[2, k, here] = an[k, here] * north[k] - bn[k, here] * (level_n - level[k]) + cn[k, here]

        held = rise(LOW)
        for low in range(LOW, HIGH, step):
            coming = rise(low + step) if low + step < HIGH else None
            move(low, held, coming)
            held = coming

    def two(i, carry):
        substep(state, state_b)
        substep(state_b, state)
        return carry

    lax.fori_loop(0, NSUB // 2, two, 0)

    flow_rows = [(OWN - 8, 8)] + [(OWN + 32 * i, 32) for i in range(4)]
    for low, size in flow_rows:
        here = slice(low, low + size)
        shift_n = state[2, 0, here] - coupling * total[3, 0, here]
        for l in range(2):
            flow_n[l, here] = face_n[l, 0, here] * (x[4 + l, 0, here] + shift_n)
        prod_n[here] = shift_n

    for i in range(4):
        low = OWN + 32 * i
        here = slice(low, low + 32)
        mine = slice(32 * i, 32 * i + 32)
        shift_e = [state[1, k, here] - coupling * total[2, k, here] for k in range(2)]
        divs = []
        for l in range(2):
            flow = [face_e[l, k, here] * (x[2 + l, k, here] + shift_e[k]) for k in range(2)]
            west = shifted(flow, 1)[0]
            flow_e[l, 0, mine] = flow[0]
            flow_e[l, 1, mine] = west
            divs.append(flow[0] - west + flow_n[l, here] - flow_n[l, low - 1 : low + 31])
        div_1[mine] = divs[1]
        pair_send[mine] = divs[0] + divs[1]

    @pl.when(jnp.logical_not(outer))
    def _():
        got(outer_got, 208)
        base = pl.multiple_of(OWN + 64 * core, 8)
        here = pl.ds(base, 64)
        shift_e = [state[1, k, here] - coupling * total[2, k, here] for k in range(2)]
        flow = outer_in[64:128] * shift_e[0]
        block = outer_in[200:208]
        column = jnp.concatenate([roll(block, -r, 1) for r in range(8)], axis=0)
        west = jnp.where(lanes(64) == 0, column * roll(shift_e[1], 1, 1), roll(flow, 1, 1))
        flow_t[0:72] = outer_in[128:200] * prod_n[pl.ds(pl.multiple_of(base - 8, 8), 72)]
        value = outer_in[0:64] + flow - west + flow_t[8:72] - flow_t[7:71]
        outer_div[core] = value
        pair_send[CY : CY + 64] = value

    remote(pair_send, pair_div, sent, div_got, member(partner)).start()

    for low, size in flow_rows:
        here = slice(low, low + size)
        flow_w[here] = total[3, 0, here] + total[1, 0, here] * prod_n[here]

    for i in range(4):
        low = OWN + 32 * i
        here = slice(low, low + 32)
        mine = slice(32 * i, 32 * i + 32)
        shift_e = [state[1, k, here] - coupling * total[2, k, here] for k in range(2)]
        flow = [total[2, k, here] + total[0, k, here] * shift_e[k] for k in range(2)]
        whole_div[mine] = flow[0] - shifted(flow, 1)[0] + flow_w[here] - flow_w[low - 1 : low + 31]
        count = x[6, 0, here]
        for l in range(2):
            fe, fw = flow_e[l, 0, mine], flow_e[l, 1, mine]
            fn, fs = flow_n[l, here], flow_n[l, low - 1 : low + 31]
            gain = jnp.where(first + l < count, tracer_time / x[l, 0, here], 0.0)
            plus_e, minus_w = jnp.maximum(fe, 0.0), jnp.minimum(fw, 0.0)
            plus_n, minus_s = jnp.maximum(fn, 0.0), jnp.minimum(fs, 0.0)
            coef[l, 0, mine] = gain * (plus_e - fe)
            coef[l, 1, mine] = gain * (fw - minus_w)
            coef[l, 2, mine] = gain * (plus_n - fn)
            coef[l, 3, mine] = gain * (fs - minus_s)
            coef[l, 4, mine] = 1.0 - gain * (plus_e - minus_w + plus_n - minus_s)
            coef[l, 5, mine] = gain

    s_out[0] = state[0, 0, rows_own]
    e_out[0] = state[1, 0, rows_own]
    n_out[0] = state[2, 0, rows_own]

    lane32 = lanes(32)
    for l in range(2):
        for i in range(4):
            mine = slice(32 * i, 32 * i + 32)
            low = 8 + 32 * i
            a_e, a_w, a_n, a_s, a_c = (coef[l, j, mine] for j in range(5))
            for m in range(NTR):
                value = c[m, l, low : low + 32]
                edge = edge_c[m, l, mine]
                value_e = jnp.where(lane32 == CX - 1, edge, roll(value, -1, 1))
                value_w = jnp.where(lane32 == 0, edge, roll(value, 1, 1))
                part[m, l, mine] = (
                    a_c * value
                    + a_e * value_e
                    + a_w * value_w
                    + a_n * c[m, l, low + 1 : low + 33]
                    + a_s * c[m, l, low - 1 : low + 31]
                )

    left(sent, 1360)

    @pl.when(owner)
    def _():
        left(edge_sent, 10 * 8 * EB)

    @pl.when(jnp.logical_not(owner))
    def _():
        left(edge_sent, 4 * 8 * EB)

    @pl.when(outer)
    def _():
        left(outer_sent, 416)

    got(div_got, 192)

    @pl.when(jnp.logical_not(outer))
    def _():
        outer_div[other] = pair_div[CY : CY + 64]

    @pl.when(outer)
    def _():
        outer_div[...] = jnp.zeros_like(outer_div)

    odd = core == 1
    for i in range(4):
        mine = slice(32 * i, 32 * i + 32)
        beyond = outer_div[i // 2, 32 * (i % 2) : 32 * (i % 2) + 32]
        near = pair_div[mine]
        here = pair_send[mine]
        deeper = jnp.where(
            upper,
            whole_div[mine] - here - beyond - jnp.where(odd, near, 0.0),
            beyond + jnp.where(odd, 0.0, near),
        )
        bottom = -deeper
        middle = -(div_1[mine] + deeper)
        top = jnp.where(me == 0, 0.0, -(here + deeper))
        for l in range(2):
            under_flow, over_flow = (middle, top) if l == 0 else (bottom, middle)
            gain = coef[l, 5, mine]
            lift[l, 0, mine] = gain * (jnp.minimum(under_flow, 0.0) - jnp.maximum(over_flow, 0.0))
            lift[l, 1, mine] = gain * jnp.maximum(under_flow, 0.0)
            lift[l, 2, mine] = -gain * jnp.minimum(over_flow, 0.0)

    @pl.when(me < ND - 1)
    def _():
        got(up_got, NTR * CY)
        left(down_sent, NTR * CY)

    @pl.when(me > 0)
    def _():
        got(down_got, NTR * CY)
        left(up_sent, NTR * CY)


def store(part, s_ref, e_ref, n_ref, c, below, above, lift, c_out, s_out, e_out, n_out, new_c, sem):
    copies = [
        pltpu.make_async_copy(source, target, sem.at[NTR + i])
        for i, (source, target) in enumerate([(s_ref, s_out), (e_ref, e_out), (n_ref, n_out)])
    ]
    for copy in copies:
        copy.start()
    for pair in range(0, NTR, 2):
        for l in range(2):
            for i in range(4):
                mine = slice(32 * i, 32 * i + 32)
                low = 8 + 32 * i
                a_c, a_b, a_a = (lift[l, j, mine] for j in range(3))
                for m in (pair, pair + 1):
                    under = c[m, 1, low : low + 32] if l == 0 else below[m, mine]
                    over = above[m, mine] if l == 0 else c[m, 0, low : low + 32]
                    new_c[m, l, mine] = (
                        part[m, l, mine] + a_c * c[m, l, low : low + 32] + a_b * under + a_a * over
                    )
        for m in (pair, pair + 1):
            copy = pltpu.make_async_copy(new_c.at[m], c_out.at[m, :, 0], sem.at[m])
            copy.start()
            copies.append(copy)
    for copy in copies:
        copy.wait()


def body(thickness, u_layer, v_layer, tracers, sea_level, u_column, v_column, wet_cells, levels):
    any_spec = pl.BlockSpec(memory_space=pl.ANY)
    near_spec = pl.BlockSpec(memory_space=pltpu.VMEM)

    def vmem(*shape):
        return pltpu.VMEM(shape, F32)

    plane = vmem(CY, CX)
    wide = vmem(2, RX, CX)
    wide2 = vmem(2, 2, RX, CX)
    column_c = vmem(NTR, CY, CX)
    flat = pltpu.VMEM((CY, CX), jnp.int32)
    quarter = vmem(4, 64, CX)
    halves = vmem(4, 2, 64, CX)
    edges = vmem(NE, 8 * EB, CX)
    dma = pltpu.SemaphoreType.DMA
    shapes = [tracers.shape] + [sea_level.shape] * 3
    results = pl.pallas_call(
        kernel,
        out_shape=(
            vmem(NTR, 2, CY, CX), *(pltpu.VMEM(shape, F32) for shape in shapes[1:]),
            vmem(NTR, 2, CY + 16, CX), column_c, column_c, vmem(2, 3, CY, CX),
        ),
        in_specs=[pl.BlockSpec(memory_space=pltpu.HBM)] * 9,
        out_specs=(near_spec,) * 8,
        scratch_shapes=[
            vmem(7, 2, RX, CX), vmem(3, 2, RX, CX), flat, flat,
            vmem(2, 2, 64, CX), vmem(2, 2, 64, CX), vmem(2, 2, 8, CX), vmem(4, 8, CX), vmem(11 * CY, CX),
            vmem(NTR, 2, CY, CX),
            halves, quarter, quarter, quarter, halves,
            edges, vmem(ND, 8 * EB, CX), edges,
            wide2, wide2, vmem(4, 2, RX, CX), vmem(4, 2, RX, CX),
            wide, wide, wide, wide, wide, wide, wide, wide, wide, vmem(3, 2, RX, CX),
            vmem(2, 208, CX), vmem(208, CX), vmem(208, CX), vmem(208, CX), vmem(2, 64, CX),
            vmem(2, RX, CX), vmem(RX, CX), vmem(RX, CX), vmem(2, 2, CY, CX), vmem(RX, CX), vmem(2, 6, CY, CX),
            plane, plane, vmem(CY + 64, CX), vmem(CY + 64, CX),
            dma((2,)), dma, dma, dma, dma, dma, dma,
            dma((2,)), dma, dma, dma, dma, dma, dma, dma, dma,
            dma, dma, dma,
        ],
        compiler_params=pltpu.CompilerParams(
            collective_id=0, has_side_effects=True, vmem_limit_bytes=48 * 1024 * 1024
        ),
    )(*[
        pltpu.with_memory_space_constraint(x, pltpu.HBM)
        for x in (thickness, u_layer, v_layer, tracers, sea_level, u_column, v_column, wet_cells, levels)
    ])
    return pl.pallas_call(
        store,
        out_shape=tuple(jax.ShapeDtypeStruct(shape, F32) for shape in shapes),
        in_specs=[near_spec] * 8,
        out_specs=(any_spec,) * 4,
        scratch_shapes=[vmem(NTR, 2, CY, CX), dma((NTR + 3,))],
    )(*[pltpu.with_memory_space_constraint(x, pltpu.VMEM) for x in results])


def solution(mesh):
    return jax.shard_map(
        body,
        mesh=mesh,
        in_specs=(
            P("depth", "tiles", None, None),
            P("depth", "tiles", None, None),
            P("depth", "tiles", None, None),
            P(None, "depth", "tiles", None, None),
            P("tiles", None, None),
            P("tiles", None, None),
            P("tiles", None, None),
            P("tiles", None, None),
            P("tiles", None, None),
        ),
        out_specs=(
            P(None, "depth", "tiles", None, None),
            P("tiles", None, None),
            P("tiles", None, None),
            P("tiles", None, None),
        ),
        check_vma=False,
    )
```

```python
import functools

import jax
import jax.numpy as jnp
from jax import lax
from jax.experimental import pallas as pl
from jax.experimental.pallas import tpu as pltpu
from jax.sharding import PartitionSpec as P

TROWS = 8
NSUB = 8
NTR = 6
ND = 8
NE = 4
EB = 5
CY = 128
CX = 128
RX = CY + 32
OWN = 16
END = OWN + CY
LOW = OWN - 8
HIGH = END + 8

tau = 0.45
coupling = 1.0 / 16
tracer_time = 0.1

MESH = pl.DeviceIdType.MESH
F32 = jnp.float32


def roll(x, shift, axis):
    shift = shift % x.shape[axis]
    return x if shift == 0 else pltpu.roll(x, shift, axis)


def lanes(rows, width=CX):
    return lax.broadcasted_iota(jnp.int32, (rows, width), 1)


def rows_of(rows, width=CX):
    return lax.broadcasted_iota(jnp.int32, (rows, width), 0)


def between(x, low, high):
    return (x >= low) & (x < high)


def kernel(
    h_in, u_in, v_in, c_in, sea_in, uc_in, vc_in, wet_in, lev_in,
    part, s_out, e_out, n_out, c, below, above, lift,
    x, state, wet, lev,
    side_pack, side_in, corner_pack, corner_in, sizes,
    edge_c,
    main_send, pair_in, chip_sum, main_in, main_all,
    edge_send, edge_in, edge_all,
    face_e, face_n, local, total,
    tw, ae, an, be, bn, ce, cn, wet_e_all, wet_n_all, state_b,
    outer_send, outer_pair, outer_sum, outer_in, outer_div,
    flow_n, flow_t, flow_w, flow_e, prod_n, coef, div_1, whole_div, pair_send, pair_div,
    loc_sem, sent, sent_late, edge_sent, outer_sent, up_sent, down_sent,
    halo_got, pair_got, rs_got, ag_got, forward_got, edge_got, edge_all_got, half_got, outer_got,
    up_got, down_got, div_got,
):
    me = lax.axis_index("depth")
    tile = lax.axis_index("tiles")
    tx = tile // TROWS
    ty = tile % TROWS
    chip = me // 2
    core = me % 2
    other = 1 - core
    partner = 2 * chip + other
    upper = me < ND // 2
    outer = (me < 2) | (me >= ND - 2)
    cols = 8

    def tile_at(dx, dy):
        return ((tx + dx + cols) % cols) * TROWS + (ty + dy + TROWS) % TROWS

    def member(which):
        return {"tiles": tile, "depth": which}

    def beside(dx, dy):
        return {"tiles": tile_at(dx, dy), "depth": me}

    def remote(source, target, send, recv, where):
        return pltpu.make_async_remote_copy(
            src_ref=source, dst_ref=target, send_sem=send, recv_sem=recv,
            device_id=where, device_id_type=MESH,
        )

    has_n = ty < TROWS - 1
    has_s = ty > 0
    inner = has_n & has_s

    rows_own = slice(OWN, END)

    def got(sem, rows):
        remote(sizes.at[0:rows], sizes.at[0:rows], sem, sem, member(partner)).wait_recv()

    def left(sem, rows):
        remote(sizes.at[0:rows], sizes.at[0:rows], sem, sem, member(partner)).wait_send()

    def fetch(source, target):
        pltpu.make_async_copy(source, target, loc_sem.at[0]).start()

    barrier = pltpu.get_barrier_semaphore()

    def greet(dy):
        for dx in (1, -1) if dy == 0 else (0, 1, -1):
            pl.semaphore_signal(barrier, inc=1, device_id=beside(dx, dy), device_id_type=MESH)

    greet(0)

    @pl.when(has_n)
    def _():
        greet(1)

    @pl.when(has_s)
    def _():
        greet(-1)

    fetch(h_in.at[:, 0], x.at[0:2, 0, rows_own])
    fetch(wet_in.at[0], wet)
    fetch(lev_in.at[0], lev)
    fetch(u_in.at[:, 0], x.at[2:4, 0, rows_own])
    fetch(v_in.at[:, 0], x.at[4:6, 0, rows_own])
    fetch(sea_in.at[0], state.at[0, 0, rows_own])
    fetch(uc_in.at[0], state.at[1, 0, rows_own])
    fetch(vc_in.at[0], state.at[2, 0, rows_own])
    peers = [(me + k) % ND for k in range(1, ND)]
    for peer in peers:
        pl.semaphore_signal(barrier, inc=1, device_id=member(peer), device_id_type=MESH)
    fetch_c = pltpu.make_async_copy(c_in.at[:, :, 0], c.at[:, :, 8 : CY + 8], loc_sem.at[1])
    fetch_c.start()

    fetched = 11 * CY
    pltpu.make_async_copy(sizes.at[0:fetched], sizes.at[0:fetched], loc_sem.at[0]).wait()

    lane8 = lanes(8)
    x[6, 0, rows_own] = (wet[...] * lev[...]).astype(F32)

    def pack_sides(phase, fields, extra=None):
        for i in range(8):
            east = west = jnp.zeros((8, CX), F32)
            for j in range(2):
                low = OWN + 64 * j + 8 * i
                for f, ref in enumerate(fields):
                    turned = roll(ref[low : low + 8], 8 * f + 8 + 64 * j, 1)
                    start = 64 * j + 8 * f
                    west = jnp.where(between(lane8, start + 8, start + 16), turned, west)
                    east = jnp.where(between(lane8, start, start + 8), turned, east)
                if extra is not None:
                    east, west = extra(64 * j + 8 * i, 64 * j, east, west)
            side_pack[phase, 0, 8 * i : 8 * i + 8] = east
            side_pack[phase, 1, 8 * i : 8 * i + 8] = west

    early = [x.at[f, 0] for f in range(7)]
    late = [state.at[f, 0] for f in range(3)]
    pack_sides(0, early)

    for j, low in enumerate((OWN, END - 8)):
        east = west = jnp.zeros((8, CX), F32)
        for f, ref in enumerate(early + late):
            turned = roll(ref[low : low + 8], 8 * f + 8, 1)
            west = jnp.where(between(lane8, 8 * f + 8, 8 * f + 16), turned, west)
            east = jnp.where(between(lane8, 8 * f, 8 * f + 8), turned, east)
        corner_pack[0, j] = east
        corner_pack[1, j] = west

    @pl.when(inner)
    def _():
        pl.semaphore_wait(barrier, 8 + ND - 1)

    @pl.when(jnp.logical_not(inner))
    def _():
        pl.semaphore_wait(barrier, 5 + ND - 1)

    def halo(phase, source, target, dx, dy):
        sem = sent if phase == 0 else sent_late
        remote(source, target, sem, halo_got.at[phase], beside(dx, dy)).start()

    halo(0, side_pack.at[0, 0], side_in.at[0, 0], 1, 0)
    halo(0, side_pack.at[0, 1], side_in.at[0, 1], -1, 0)

    @pl.when(has_n)
    def _():
        halo(0, corner_pack.at[0, 1], corner_in.at[0], 1, 1)
        halo(0, corner_pack.at[1, 1], corner_in.at[1], -1, 1)
        halo(0, x.at[:, 0, END - 8 : END], x.at[:, 0, LOW:OWN], 0, 1)

    @pl.when(has_s)
    def _():
        halo(0, corner_pack.at[0, 0], corner_in.at[2], 1, -1)
        halo(0, corner_pack.at[1, 0], corner_in.at[3], -1, -1)
        halo(0, x.at[:, 0, OWN : OWN + 8], x.at[:, 0, END:HIGH], 0, -1)

    first = (2 * me).astype(F32)
    lane16 = lanes(16)
    row16 = rows_of(16)

    def next_row(ref, p):
        low = OWN + 16 * p
        if p < ND - 1:
            return ref[low + 1 : low + 17]
        return jnp.where(row16 == 15, 0.0, roll(ref[low : low + 16], -1, 0))

    for p in range(ND):
        low = OWN + 16 * p
        here = slice(low, low + 16)
        count = x[6, 0, here]
        count_e = jnp.minimum(count, jnp.where(lane16 == CX - 1, 0.0, roll(count, -1, 1)))
        count_n = jnp.minimum(count, next_row(x.at[6, 0], p))
        sums = [0.0] * 4
        for l in range(2):
            thick = x[l, 0, here]
            de = jnp.where(first + l < count_e, 0.5 * (thick + roll(thick, -1, 1)), 0.0)
            dn = jnp.where(first + l < count_n, 0.5 * (thick + next_row(x.at[l, 0], p)), 0.0)
            new = [de, dn, x[2 + l, 0, here] * de, x[4 + l, 0, here] * dn]
            sums = [a + b for a, b in zip(sums, new)]
        for f in range(4):
            main_send[p // 2, p % 2, 16 * f : 16 * f + 16] = sums[f]
    remote(main_send.at[:, other], pair_in, sent, pair_got, member(partner)).start()

    fetch_c.wait()
    rows_c = slice(8, CY + 8)

    def send_tracers(i):
        part = slice(0, 2) if i == 0 else slice(2, NTR)

        @pl.when(me > 0)
        def _():
            remote(
                c.at[part, 0, rows_c], below.at[part], up_sent, up_got, member((me + ND - 1) % ND)
            ).start()

        @pl.when(me < ND - 1)
        def _():
            remote(
                c.at[part, 1, rows_c], above.at[part], down_sent, down_got, member((me + 1) % ND)
            ).start()

    send_tracers(0)

    got(pair_got, 256)
    chips = [(chip + k) % 4 for k in range(1, 4)]
    for q in range(4):
        chip_sum[q] = main_send[q, core] + pair_in[q]
    for q in chips:
        remote(chip_sum.at[q], main_in.at[chip], sent, rs_got, member(2 * q + core)).start()

    def pack_more(low, shift, east, west):
        old = state[1, 0, OWN + low : OWN + low + 8]
        east = jnp.where(between(lane8, shift + 24, shift + 32), roll(old, 40 + shift, 1), east)
        for p in range(2 * NTR):
            plane = c[p // 2, p % 2, 8 + low : 16 + low]
            west = jnp.where(lane8 == shift + 48 + p, roll(plane, shift + 48 + p, 1), west)
            east = jnp.where(lane8 == shift + 49 + p, roll(plane, shift + 50 + p, 1), east)
        return east, west

    pack_sides(1, late, pack_more)

    halo(1, side_pack.at[1, 0], side_in.at[1, 0], 1, 0)
    halo(1, side_pack.at[1, 1], side_in.at[1, 1], -1, 0)

    @pl.when(has_n)
    def _():
        halo(1, state.at[:, 0, END - 16 : END], state.at[:, 0, 0:OWN], 0, 1)
        halo(1, c.at[:, :, CY : CY + 8], c.at[:, :, 0:8], 0, 1)

    @pl.when(has_s)
    def _():
        halo(1, state.at[:, 0, OWN : OWN + 8], state.at[:, 0, END:HIGH], 0, -1)
        halo(1, c.at[:, :, 8:16], c.at[:, :, CY + 8 : CY + 16], 0, -1)

    @pl.when(me == 0)
    def _():
        above[...] = jnp.zeros_like(above)

    @pl.when(me == ND - 1)
    def _():
        below[...] = jnp.zeros_like(below)

    for ref in (x, state):
        for k in range(2):
            ref[:, k, HIGH:RX] = jnp.zeros((ref.shape[0], RX - HIGH, CX), F32)
    state[2, 1, 0:LOW] = jnp.zeros((LOW, CX), F32)
    state_b[2, :, 0:LOW] = jnp.zeros((2, LOW, CX), F32)

    def unpack_sides(phase, fields, extra=None):
        side = (lane8 < 8) | (lane8 >= CX - 8)
        for i in range(-1, 17):
            if i < 0:
                west, east, shift, ok = corner_in[0], corner_in[1], 56 * phase, side & has_s
            elif i == 16:
                west, east, shift, ok = corner_in[2], corner_in[3], 56 * phase, side & has_n
            else:
                j = 8 * (i % 8)
                west, east = side_in[phase, 0, j : j + 8], side_in[phase, 1, j : j + 8]
                shift, ok = 64 * (i // 8), side
            low = OWN + 8 * i
            for f, ref in enumerate(fields):
                start = shift + 8 * f + 8
                value = roll(jnp.where(between(lane8, start, start + 8), east, west), -start, 1)
                value = jnp.where(ok, value, 0.0)
                if extra is not None and f == 1 and 0 <= i < 16:
                    value = jnp.where(lane8 == CX - 9, roll(west, 88 - shift, 1), value)
                ref[low : low + 8] = value
            if extra is not None and 0 <= i < 16:
                extra(8 * i, shift, west, east)

    @pl.when(inner)
    def _():
        got(halo_got.at[0], 272)

    @pl.when(jnp.logical_not(inner))
    def _():
        got(halo_got.at[0], 200)

    unpack_sides(0, [x.at[f, 1] for f in range(7)])

    @pl.when(jnp.logical_not(has_s))
    def _():
        x[:, 0, LOW:OWN] = jnp.zeros((7, 8, CX), F32)

    @pl.when(jnp.logical_not(has_n))
    def _():
        x[:, 0, END:HIGH] = jnp.zeros((7, 8, CX), F32)

    def shifted(pair, steps):
        lane = lanes(pair[0].shape[0])
        edge = lane == (0 if steps > 0 else CX - 1)
        main, side = (roll(value, steps, 1) for value in pair)
        return jnp.where(edge, side, main), jnp.where(edge, main, side)

    def both(ref, low, size):
        return ref[0, low : low + size], ref[1, low : low + size]

    step = 24
    for low in range(LOW, HIGH, step):
        here = slice(low, low + step)
        count = both(x.at[6], low, step)
        count_e = shifted(count, -1)
        count_n = both(x.at[6], low + 1, step)
        thick = [both(x.at[l], low, step) for l in range(2)]
        thick_e = [shifted(thick[l], -1) for l in range(2)]
        for k in range(2):
            min_e = jnp.minimum(count[k], count_e[k])
            min_n = jnp.minimum(count[k], count_n[k])
            sums = [0.0] * 4
            for l in range(2):
                north = x[l, k, low + 1 : low + 1 + step]
                de = jnp.where(first + l < min_e, 0.5 * (thick[l][k] + thick_e[l][k]), 0.0)
                dn = jnp.where(first + l < min_n, 0.5 * (thick[l][k] + north), 0.0)
                face_e[l, k, here] = de
                face_n[l, k, here] = dn
                new = [de, dn, x[2 + l, k, here] * de, x[4 + l, k, here] * dn]
                sums = [a + b for a, b in zip(sums, new)]
            for f in range(4):
                local[f, k, here] = sums[f]

    def put_block(i, block):
        edge_send[i // EB, 8 * (i % EB) : 8 * (i % EB) + 8] = block

    for i in range(9):
        block = jnp.zeros((8, CX), F32)
        for j in range(2):
            low = LOW + 72 * j + 8 * i
            for f in range(4):
                start = 64 * j + 16 * f
                block = jnp.where(
                    lane8 == start, roll(local[f, 0, low : low + 8], start + 1, 1), block
                )
                block = jnp.where(
                    between(lane8, start + 1, start + 16),
                    roll(local[f, 1, low : low + 8], start + 9, 1),
                    block,
                )
        put_block(i, block)
    for f in range(4):
        put_block(9 + f, local[f, 0, END - 1 : END + 7])
        put_block(13 + f, local[f, 0, LOW:OWN])
    for i in range(17, NE * EB):
        put_block(i, jnp.zeros((8, CX), F32))

    owner = core == 0

    @pl.when(owner)
    def _():
        for q in chips:
            remote(edge_send.at[q], edge_in.at[me], edge_sent, edge_got, member(2 * q)).start()

    @pl.when(jnp.logical_not(owner))
    def _():
        for q in chips + [chip]:
            remote(edge_send.at[q], edge_in.at[me], edge_sent, edge_got, member(2 * q)).start()

    got(rs_got, 192)
    mine = chip_sum[chip]
    for q in chips:
        mine = mine + main_in[q]
    main_all[chip, core] = mine
    piece = main_all.at[chip, core]
    for q in chips:
        remote(piece, piece, sent, ag_got, member(2 * q + core)).start()

    @pl.when(outer)
    def _():
        for i in range(4):
            low = OWN + 32 * i
            here = slice(low, low + 32)
            flux = both(local.at[2], low, 32)
            value = flux[0] - shifted(flux, 1)[0] + local[3, 0, here] - local[3, 0, low - 1 : low + 31]
            outer_send[i // 2, 32 * (i % 2) : 32 * (i % 2) + 32] = value
        for j in range(2):
            low = OWN + 64 * j
            outer_send[j, 64:128] = local[0, 0, low : low + 64]
            outer_send[j, 128:200] = local[1, 0, low - 8 : low + 64]
            block = jnp.zeros((8, CX), F32)
            for r in range(8):
                turned = roll(local[0, 1, low + 8 * r : low + 8 * r + 8], r + 1, 1)
                block = jnp.where(lane8 == r, turned, block)
            outer_send[j, 200:208] = block
        remote(outer_send, outer_pair, outer_sent, half_got, member(partner)).start()

    @pl.when(owner)
    def _():
        got(edge_got, 7 * 8 * EB)
        edge = edge_send[chip]
        for peer in peers:
            edge = edge + edge_in[peer]
        edge_all[chip] = edge
        for peer in peers:
            remote(edge_all.at[chip], edge_all.at[chip], edge_sent, edge_all_got, member(peer)).start()

    @pl.when(outer)
    def _():
        got(half_got, 416)
        outer_sum[...] = outer_send[core] + outer_pair[core]
        middle_chip = jnp.where(upper, 2, ND - 4)
        remote(outer_sum, outer_in, outer_sent, outer_got, member(middle_chip + core)).start()

    send_tracers(1)

    @pl.when(inner)
    def _():
        got(halo_got.at[1], 392)
        left(sent_late, 392)

    @pl.when(jnp.logical_not(has_s))
    def _():
        got(halo_got.at[1], 248)
        left(sent_late, 272)

    @pl.when(jnp.logical_not(has_n))
    def _():
        got(halo_got.at[1], 272)
        left(sent_late, 248)


    def put_tracers(low, shift, west, east):
        for p in range(2 * NTR):
            value = jnp.where(lane8 <= shift + 48 + p, east, west)
            edge_c[p // 2, p % 2, low : low + 8] = roll(value, 79 - shift - p, 1)

    unpack_sides(1, [state.at[f, 1] for f in range(3)], put_tracers)

    @pl.when(jnp.logical_not(has_s))
    def _():
        state[:, 0, 0:OWN] = jnp.zeros((3, OWN, CX), F32)
        c[:, :, 0:8] = jnp.zeros((NTR, 2, 8, CX), F32)

    @pl.when(jnp.logical_not(has_n))
    def _():
        state[:, 0, END:HIGH] = jnp.zeros((3, 8, CX), F32)
        c[:, :, CY + 8 : CY + 16] = jnp.zeros((NTR, 2, 8, CX), F32)

    for low in range(LOW, HIGH, step):
        here = slice(low, low + step)
        is_wet = [jnp.where(value > 0.0, 1.0, 0.0) for value in both(x.at[6], low, step)]
        wet_e = shifted(is_wet, -1)
        wet_n = [jnp.where(value > 0.0, 1.0, 0.0) for value in both(x.at[6], low + 1, step)]
        for k in range(2):
            tw[k, here] = tau * is_wet[k]
            ae[k, here] = (1.0 - tau) * (is_wet[k] * wet_e[k])
            an[k, here] = (1.0 - tau) * (is_wet[k] * wet_n[k])
            wet_e_all[k, here] = (tau * coupling) * (is_wet[k] * wet_e[k])
            wet_n_all[k, here] = (tau * coupling) * (is_wet[k] * wet_n[k])

    got(ag_got, 192)
    half = main_all.at[:, core]
    remote(half, half, sent, forward_got, member(partner)).start()

    @pl.when(owner)
    def _():
        got(edge_all_got, 3 * 8 * EB)

    @pl.when(jnp.logical_not(owner))
    def _():
        got(edge_all_got, 4 * 8 * EB)

    got(forward_got, 256)

    def block_of(i):
        return edge_all[i // EB, 8 * (i % EB) : 8 * (i % EB) + 8]

    rim = (lane8 < 7) | (lane8 >= CX - 8)
    last_lane = lane8 == CX - 1
    row8 = rows_of(8)
    for i in range(18):
        block = block_of(i % 9)
        shift = 64 * (i // 9)
        here = slice(LOW + 8 * i, LOW + 8 * i + 8)
        sums = []
        for f in range(4):
            if i == 0:
                main = block_of(13 + f)
            elif i == 17:
                main = jnp.where(row8 == 7, 0.0, roll(block_of(9 + f), -1, 0))
            else:
                p, part_low = (i - 1) // 2, 16 * f + 8 * ((i - 1) % 2)
                main = main_all[p // 2, p % 2, part_low : part_low + 8]
                if i == 16:
                    main = jnp.where(row8 == 7, jnp.broadcast_to(block_of(9 + f)[0:1], (8, CX)), main)
            main = jnp.where(last_lane, roll(block, CX - 1 - 16 * f - shift, 1), main)
            side = jnp.where(rim, roll(block, -(9 + 16 * f + shift), 1), 0.0)
            total[f, 0, here] = main
            total[f, 1, here] = side
            sums.append((main, side))
        for k in range(2):
            east, north = wet_e_all[k, here], wet_n_all[k, here]
            be[k, here] = east * sums[0][k]
            bn[k, here] = north * sums[1][k]
            ce[k, here] = east * sums[2][k]
            cn[k, here] = north * sums[3][k]

    def substep(old, new):
        bottom_row = rows_of(step) == step - 1

        def rise(low):
            here = slice(low, low + step)
            east = both(old.at[1], low, step)
            west = shifted(east, 1)
            north = both(old.at[2], low, step)
            south = both(old.at[2], low - 1, step)
            level = []
            for k in range(2):
                value = old[0, k, here] - tw[k, here] * (east[k] - west[k] + north[k] - south[k])
                new[0, k, here] = value
                level.append(value)
            return level, east, north

        def move(low, held, beyond):
            here = slice(low, low + step)
            level, east, north = held
            level_e = shifted(level, -1)
            for k in range(2):
                level_n = roll(level[k], -1, 0)
                if beyond is not None:
                    first_row = jnp.broadcast_to(beyond[0][k][0:1], (step, CX))
                    level_n = jnp.where(bottom_row, first_row, level_n)
                new[1, k, here] = ae[k, here] * east[k] - be[k, here] * (level_e[k] - level[k]) + ce[k, here]
                new[2, k, here] = an[k, here] * north[k] - bn[k, here] * (level_n - level[k]) + cn[k, here]

        held = rise(LOW)
        for low in range(LOW, HIGH, step):
            coming = rise(low + step) if low + step < HIGH else None
            move(low, held, coming)
            held = coming

    def two(i, carry):
        substep(state, state_b)
        substep(state_b, state)
        return carry

    lax.fori_loop(0, NSUB // 2, two, 0)

    flow_rows = [(OWN - 8, 8)] + [(OWN + 32 * i, 32) for i in range(4)]
    for low, size in flow_rows:
        here = slice(low, low + size)
        shift_n = state[2, 0, here] - coupling * total[3, 0, here]
        for l in range(2):
            flow_n[l, here] = face_n[l, 0, here] * (x[4 + l, 0, here] + shift_n)
        prod_n[here] = shift_n

    for i in range(4):
        low = OWN + 32 * i
        here = slice(low, low + 32)
        mine = slice(32 * i, 32 * i + 32)
        shift_e = [state[1, k, here] - coupling * total[2, k, here] for k in range(2)]
        divs = []
        for l in range(2):
            flow = [face_e[l, k, here] * (x[2 + l, k, here] + shift_e[k]) for k in range(2)]
            west = shifted(flow, 1)[0]
            flow_e[l, 0, mine] = flow[0]
            flow_e[l, 1, mine] = west
            divs.append(flow[0] - west + flow_n[l, here] - flow_n[l, low - 1 : low + 31])
        div_1[mine] = divs[1]
        pair_send[mine] = divs[0] + divs[1]

    def divergence_of(parts, base):
        here = pl.ds(base, 64)
        shift_e = [state[1, k, here] - coupling * total[2, k, here] for k in range(2)]
        flow = parts[64:128] * shift_e[0]
        block = parts[200:208]
        column = jnp.concatenate([roll(block, -r, 1) for r in range(8)], axis=0)
        west = jnp.where(lanes(64) == 0, column * roll(shift_e[1], 1, 1), roll(flow, 1, 1))
        flow_t[0:72] = parts[128:200] * prod_n[pl.ds(base - 8, 72)]
        return parts[0:64] + flow - west + flow_t[8:72] - flow_t[7:71]

    @pl.when(jnp.logical_not(outer))
    def _():
        got(outer_got, 208)
        value = divergence_of(outer_in, pl.multiple_of(OWN + 64 * core, 8))
        outer_div[core] = value
        pair_send[CY : CY + 64] = value
        remote(pair_send, pair_div, sent, div_got, member(partner)).start()

    @pl.when(outer)
    def _():
        for j in range(2):
            pair_div[64 * j : 64 * j + 64] = divergence_of(outer_pair.at[j], OWN + 64 * j)
        outer_div[...] = jnp.zeros_like(outer_div)

    for low, size in flow_rows:
        here = slice(low, low + size)
        flow_w[here] = total[3, 0, here] + total[1, 0, here] * prod_n[here]

    for i in range(4):
        low = OWN + 32 * i
        here = slice(low, low + 32)
        mine = slice(32 * i, 32 * i + 32)
        shift_e = [state[1, k, here] - coupling * total[2, k, here] for k in range(2)]
        flow = [total[2, k, here] + total[0, k, here] * shift_e[k] for k in range(2)]
        whole_div[mine] = flow[0] - shifted(flow, 1)[0] + flow_w[here] - flow_w[low - 1 : low + 31]
        count = x[6, 0, here]
        for l in range(2):
            fe, fw = flow_e[l, 0, mine], flow_e[l, 1, mine]
            fn, fs = flow_n[l, here], flow_n[l, low - 1 : low + 31]
            gain = jnp.where(first + l < count, tracer_time / x[l, 0, here], 0.0)
            plus_e, minus_w = jnp.maximum(fe, 0.0), jnp.minimum(fw, 0.0)
            plus_n, minus_s = jnp.maximum(fn, 0.0), jnp.minimum(fs, 0.0)
            coef[l, 0, mine] = gain * (plus_e - fe)
            coef[l, 1, mine] = gain * (fw - minus_w)
            coef[l, 2, mine] = gain * (plus_n - fn)
            coef[l, 3, mine] = gain * (fs - minus_s)
            coef[l, 4, mine] = 1.0 - gain * (plus_e - minus_w + plus_n - minus_s)
            coef[l, 5, mine] = gain

    s_out[0] = state[0, 0, rows_own]
    e_out[0] = state[1, 0, rows_own]
    n_out[0] = state[2, 0, rows_own]

    lane32 = lanes(32)
    for l in range(2):
        for i in range(4):
            mine = slice(32 * i, 32 * i + 32)
            low = 8 + 32 * i
            a_e, a_w, a_n, a_s, a_c = (coef[l, j, mine] for j in range(5))
            for m in range(NTR):
                value = c[m, l, low : low + 32]
                edge = edge_c[m, l, mine]
                value_e = jnp.where(lane32 == CX - 1, edge, roll(value, -1, 1))
                value_w = jnp.where(lane32 == 0, edge, roll(value, 1, 1))
                part[m, l, mine] = (
                    a_c * value
                    + a_e * value_e
                    + a_w * value_w
                    + a_n * c[m, l, low + 1 : low + 33]
                    + a_s * c[m, l, low - 1 : low + 31]
                )

    halos_sent = [(inner, 272), (jnp.logical_not(inner), 200)]
    for where, rows in halos_sent:
        @pl.when(where & outer)
        def _(rows=rows):
            left(sent, rows + 896)

        @pl.when(where & jnp.logical_not(outer))
        def _(rows=rows):
            left(sent, rows + 1088)

    @pl.when(owner)
    def _():
        left(edge_sent, 10 * 8 * EB)

    @pl.when(jnp.logical_not(owner))
    def _():
        left(edge_sent, 4 * 8 * EB)

    @pl.when(outer)
    def _():
        left(outer_sent, 624)

    @pl.when(jnp.logical_not(outer))
    def _():
        got(div_got, 192)
        outer_div[other] = pair_div[CY : CY + 64]

    odd = core == 1
    for i in range(4):
        mine = slice(32 * i, 32 * i + 32)
        beyond = outer_div[i // 2, 32 * (i % 2) : 32 * (i % 2) + 32]
        near = pair_div[mine]
        here = pair_send[mine]
        deeper = jnp.where(
            upper,
            whole_div[mine] - here - beyond - jnp.where(odd, near, 0.0),
            beyond + jnp.where(odd, 0.0, near),
        )
        bottom = -deeper
        middle = -(div_1[mine] + deeper)
        top = jnp.where(me == 0, 0.0, -(here + deeper))
        for l in range(2):
            under_flow, over_flow = (middle, top) if l == 0 else (bottom, middle)
            gain = coef[l, 5, mine]
            lift[l, 0, mine] = gain * (jnp.minimum(under_flow, 0.0) - jnp.maximum(over_flow, 0.0))
            lift[l, 1, mine] = gain * jnp.maximum(under_flow, 0.0)
            lift[l, 2, mine] = -gain * jnp.minimum(over_flow, 0.0)

    @pl.when(me < ND - 1)
    def _():
        got(up_got, NTR * CY)
        left(down_sent, NTR * CY)

    @pl.when(me > 0)
    def _():
        got(down_got, NTR * CY)
        left(up_sent, NTR * CY)


def store(part, s_ref, e_ref, n_ref, c, below, above, lift, c_out, s_out, e_out, n_out, new_c, sem):
    copies = [
        pltpu.make_async_copy(source, target, sem.at[NTR + i])
        for i, (source, target) in enumerate([(s_ref, s_out), (e_ref, e_out), (n_ref, n_out)])
    ]
    for copy in copies:
        copy.start()
    for pair in range(0, NTR, 2):
        for l in range(2):
            for i in range(4):
                mine = slice(32 * i, 32 * i + 32)
                low = 8 + 32 * i
                a_c, a_b, a_a = (lift[l, j, mine] for j in range(3))
                for m in (pair, pair + 1):
                    under = c[m, 1, low : low + 32] if l == 0 else below[m, mine]
                    over = above[m, mine] if l == 0 else c[m, 0, low : low + 32]
                    new_c[m, l, mine] = (
                        part[m, l, mine] + a_c * c[m, l, low : low + 32] + a_b * under + a_a * over
                    )
        for m in (pair, pair + 1):
            copy = pltpu.make_async_copy(new_c.at[m], c_out.at[m, :, 0], sem.at[m])
            copy.start()
            copies.append(copy)
    for copy in copies:
        copy.wait()


def body(thickness, u_layer, v_layer, tracers, sea_level, u_column, v_column, wet_cells, levels):
    any_spec = pl.BlockSpec(memory_space=pl.ANY)
    near_spec = pl.BlockSpec(memory_space=pltpu.VMEM)

    def vmem(*shape):
        return pltpu.VMEM(shape, F32)

    plane = vmem(CY, CX)
    wide = vmem(2, RX, CX)
    wide2 = vmem(2, 2, RX, CX)
    column_c = vmem(NTR, CY, CX)
    flat = pltpu.VMEM((CY, CX), jnp.int32)
    quarter = vmem(4, 64, CX)
    halves = vmem(4, 2, 64, CX)
    edges = vmem(NE, 8 * EB, CX)
    dma = pltpu.SemaphoreType.DMA
    shapes = [tracers.shape] + [sea_level.shape] * 3
    results = pl.pallas_call(
        kernel,
        out_shape=(
            vmem(NTR, 2, CY, CX), *(pltpu.VMEM(shape, F32) for shape in shapes[1:]),
            vmem(NTR, 2, CY + 16, CX), column_c, column_c, vmem(2, 3, CY, CX),
        ),
        in_specs=[pl.BlockSpec(memory_space=pltpu.HBM)] * 9,
        out_specs=(near_spec,) * 8,
        scratch_shapes=[
            vmem(7, 2, RX, CX), vmem(3, 2, RX, CX), flat, flat,
            vmem(2, 2, 64, CX), vmem(2, 2, 64, CX), vmem(2, 2, 8, CX), vmem(4, 8, CX), vmem(11 * CY, CX),
            vmem(NTR, 2, CY, CX),
            halves, quarter, quarter, quarter, halves,
            edges, vmem(ND, 8 * EB, CX), edges,
            wide2, wide2, vmem(4, 2, RX, CX), vmem(4, 2, RX, CX),
            wide, wide, wide, wide, wide, wide, wide, wide, wide, vmem(3, 2, RX, CX),
            vmem(2, 208, CX), vmem(2, 208, CX), vmem(208, CX), vmem(208, CX), vmem(2, 64, CX),
            vmem(2, RX, CX), vmem(RX, CX), vmem(RX, CX), vmem(2, 2, CY, CX), vmem(RX, CX), vmem(2, 6, CY, CX),
            plane, plane, vmem(CY + 64, CX), vmem(CY + 64, CX),
            dma((2,)), dma, dma, dma, dma, dma, dma,
            dma((2,)), dma, dma, dma, dma, dma, dma, dma, dma,
            dma, dma, dma,
        ],
        compiler_params=pltpu.CompilerParams(
            collective_id=0, has_side_effects=True, vmem_limit_bytes=48 * 1024 * 1024
        ),
    )(*[
        pltpu.with_memory_space_constraint(x, pltpu.HBM)
        for x in (thickness, u_layer, v_layer, tracers, sea_level, u_column, v_column, wet_cells, levels)
    ])
    return pl.pallas_call(
        store,
        out_shape=tuple(jax.ShapeDtypeStruct(shape, F32) for shape in shapes),
        in_specs=[near_spec] * 8,
        out_specs=(any_spec,) * 4,
        scratch_shapes=[vmem(NTR, 2, CY, CX), dma((NTR + 3,))],
    )(*[pltpu.with_memory_space_constraint(x, pltpu.VMEM) for x in results])


def solution(mesh):
    return jax.shard_map(
        body,
        mesh=mesh,
        in_specs=(
            P("depth", "tiles", None, None),
            P("depth", "tiles", None, None),
            P("depth", "tiles", None, None),
            P(None, "depth", "tiles", None, None),
            P("tiles", None, None),
            P("tiles", None, None),
            P("tiles", None, None),
            P("tiles", None, None),
            P("tiles", None, None),
        ),
        out_specs=(
            P(None, "depth", "tiles", None, None),
            P("tiles", None, None),
            P("tiles", None, None),
            P("tiles", None, None),
        ),
        check_vma=False,
    )
```

```python
import functools

import jax
import jax.numpy as jnp
from jax import lax
from jax.experimental import pallas as pl
from jax.experimental.pallas import tpu as pltpu
from jax.sharding import PartitionSpec as P

TROWS = 8
NSUB = 8
NTR = 6
ND = 8
NE = 4
EB = 5
CY = 128
CX = 128
RX = CY + 32
OWN = 16
END = OWN + CY
LOW = OWN - 8
HIGH = END + 8

tau = 0.45
coupling = 1.0 / 16
tracer_time = 0.1

MESH = pl.DeviceIdType.MESH
F32 = jnp.float32


def roll(x, shift, axis):
    shift = shift % x.shape[axis]
    return x if shift == 0 else pltpu.roll(x, shift, axis)


def lanes(rows, width=CX):
    return lax.broadcasted_iota(jnp.int32, (rows, width), 1)


def rows_of(rows, width=CX):
    return lax.broadcasted_iota(jnp.int32, (rows, width), 0)


def between(x, low, high):
    return (x >= low) & (x < high)


def kernel(
    h_in, u_in, v_in, c_in, sea_in, uc_in, vc_in, wet_in, lev_in,
    part, s_out, e_out, n_out, c, below, above, lift,
    x, state, wet, lev,
    side_pack, side_in, corner_pack, corner_in, sizes,
    edge_c,
    main_send, main_in, main_all,
    edge_send, edge_in, edge_all,
    face_e, face_n, local, total,
    tw, ae, an, be, bn, ce, cn, wet_e_all, wet_n_all, state_b,
    outer_send, outer_pair, outer_sum, outer_in, outer_div,
    flow_n, flow_t, flow_w, flow_e, prod_n, coef, div_1, whole_div, pair_send, pair_div,
    loc_sem, sent, sent_late, edge_sent, outer_sent, up_sent, down_sent,
    halo_got, rs_got, ag_got, forward_got, edge_got, edge_all_got, half_got, outer_got,
    up_got, down_got, div_got,
):
    me = lax.axis_index("depth")
    tile = lax.axis_index("tiles")
    tx = tile // TROWS
    ty = tile % TROWS
    chip = me // 2
    core = me % 2
    other = 1 - core
    partner = 2 * chip + other
    upper = me < ND // 2
    outer = (me < 2) | (me >= ND - 2)
    cols = 8

    def tile_at(dx, dy):
        return ((tx + dx + cols) % cols) * TROWS + (ty + dy + TROWS) % TROWS

    def member(which):
        return {"tiles": tile, "depth": which}

    def beside(dx, dy):
        return {"tiles": tile_at(dx, dy), "depth": me}

    def remote(source, target, send, recv, where):
        return pltpu.make_async_remote_copy(
            src_ref=source, dst_ref=target, send_sem=send, recv_sem=recv,
            device_id=where, device_id_type=MESH,
        )

    has_n = ty < TROWS - 1
    has_s = ty > 0
    inner = has_n & has_s

    rows_own = slice(OWN, END)

    def got(sem, rows):
        remote(sizes.at[0:rows], sizes.at[0:rows], sem, sem, member(partner)).wait_recv()

    def left(sem, rows):
        remote(sizes.at[0:rows], sizes.at[0:rows], sem, sem, member(partner)).wait_send()

    def fetch(source, target):
        pltpu.make_async_copy(source, target, loc_sem.at[0]).start()

    barrier = pltpu.get_barrier_semaphore()

    def greet(dy):
        for dx in (1, -1) if dy == 0 else (0, 1, -1):
            pl.semaphore_signal(barrier, inc=1, device_id=beside(dx, dy), device_id_type=MESH)

    greet(0)

    @pl.when(has_n)
    def _():
        greet(1)

    @pl.when(has_s)
    def _():
        greet(-1)

    fetch(h_in.at[:, 0], x.at[0:2, 0, rows_own])
    fetch(wet_in.at[0], wet)
    fetch(lev_in.at[0], lev)
    fetch(u_in.at[:, 0], x.at[2:4, 0, rows_own])
    fetch(v_in.at[:, 0], x.at[4:6, 0, rows_own])
    fetch(sea_in.at[0], state.at[0, 0, rows_own])
    fetch(uc_in.at[0], state.at[1, 0, rows_own])
    fetch(vc_in.at[0], state.at[2, 0, rows_own])
    peers = [(me + k) % ND for k in range(1, ND)]
    for peer in peers:
        pl.semaphore_signal(barrier, inc=1, device_id=member(peer), device_id_type=MESH)
    fetch_c = pltpu.make_async_copy(c_in.at[:, :, 0], c.at[:, :, 8 : CY + 8], loc_sem.at[1])
    fetch_c.start()

    fetched = 11 * CY
    pltpu.make_async_copy(sizes.at[0:fetched], sizes.at[0:fetched], loc_sem.at[0]).wait()

    lane8 = lanes(8)
    x[6, 0, rows_own] = (wet[...] * lev[...]).astype(F32)

    def pack_sides(phase, fields, extra=None):
        for i in range(8):
            east = west = jnp.zeros((8, CX), F32)
            for j in range(2):
                low = OWN + 64 * j + 8 * i
                for f, ref in enumerate(fields):
                    turned = roll(ref[low : low + 8], 8 * f + 8 + 64 * j, 1)
                    start = 64 * j + 8 * f
                    west = jnp.where(between(lane8, start + 8, start + 16), turned, west)
                    east = jnp.where(between(lane8, start, start + 8), turned, east)
                if extra is not None:
                    east, west = extra(64 * j + 8 * i, 64 * j, east, west)
            side_pack[phase, 0, 8 * i : 8 * i + 8] = east
            side_pack[phase, 1, 8 * i : 8 * i + 8] = west

    early = [x.at[f, 0] for f in range(7)]
    late = [state.at[f, 0] for f in range(3)]
    pack_sides(0, early)

    for j, low in enumerate((OWN, END - 8)):
        east = west = jnp.zeros((8, CX), F32)
        for f, ref in enumerate(early + late):
            turned = roll(ref[low : low + 8], 8 * f + 8, 1)
            west = jnp.where(between(lane8, 8 * f + 8, 8 * f + 16), turned, west)
            east = jnp.where(between(lane8, 8 * f, 8 * f + 8), turned, east)
        corner_pack[0, j] = east
        corner_pack[1, j] = west

    first = (2 * me).astype(F32)
    lane16 = lanes(16)
    row16 = rows_of(16)

    def next_row(ref, p):
        low = OWN + 16 * p
        if p < ND - 1:
            return ref[low + 1 : low + 17]
        return jnp.where(row16 == 15, 0.0, roll(ref[low : low + 16], -1, 0))

    for p in range(ND):
        low = OWN + 16 * p
        here = slice(low, low + 16)
        count = x[6, 0, here]
        count_e = jnp.minimum(count, jnp.where(lane16 == CX - 1, 0.0, roll(count, -1, 1)))
        count_n = jnp.minimum(count, next_row(x.at[6, 0], p))
        sums = [0.0] * 4
        for l in range(2):
            thick = x[l, 0, here]
            de = jnp.where(first + l < count_e, 0.5 * (thick + roll(thick, -1, 1)), 0.0)
            dn = jnp.where(first + l < count_n, 0.5 * (thick + next_row(x.at[l, 0], p)), 0.0)
            new = [de, dn, x[2 + l, 0, here] * de, x[4 + l, 0, here] * dn]
            sums = [a + b for a, b in zip(sums, new)]
        for f in range(4):
            main_send[p, 16 * f : 16 * f + 16] = sums[f]
    @pl.when(inner)
    def _():
        pl.semaphore_wait(barrier, 8 + ND - 1)

    @pl.when(jnp.logical_not(inner))
    def _():
        pl.semaphore_wait(barrier, 5 + ND - 1)

    def halo(phase, source, target, dx, dy):
        sem = sent if phase == 0 else sent_late
        remote(source, target, sem, halo_got.at[phase], beside(dx, dy)).start()

    halo(0, side_pack.at[0, 0], side_in.at[0, 0], 1, 0)
    halo(0, side_pack.at[0, 1], side_in.at[0, 1], -1, 0)

    @pl.when(has_n)
    def _():
        halo(0, corner_pack.at[0, 1], corner_in.at[0], 1, 1)
        halo(0, corner_pack.at[1, 1], corner_in.at[1], -1, 1)
        halo(0, x.at[:, 0, END - 8 : END], x.at[:, 0, LOW:OWN], 0, 1)

    @pl.when(has_s)
    def _():
        halo(0, corner_pack.at[0, 0], corner_in.at[2], 1, -1)
        halo(0, corner_pack.at[1, 0], corner_in.at[3], -1, -1)
        halo(0, x.at[:, 0, OWN : OWN + 8], x.at[:, 0, END:HIGH], 0, -1)

    far_first = [(me + k) % ND for k in (4, 5, 3, 2, 6, 7, 1)]
    for peer in far_first:
        remote(main_send.at[peer], main_in.at[me], sent, rs_got, member(peer)).start()

    fetch_c.wait()
    rows_c = slice(8, CY + 8)

    def send_tracers(i):
        part = slice(0, 2) if i == 0 else slice(2, NTR)

        @pl.when(me > 0)
        def _():
            remote(
                c.at[part, 0, rows_c], below.at[part], up_sent, up_got, member((me + ND - 1) % ND)
            ).start()

        @pl.when(me < ND - 1)
        def _():
            remote(
                c.at[part, 1, rows_c], above.at[part], down_sent, down_got, member((me + 1) % ND)
            ).start()

    send_tracers(0)

    chips = [(chip + k) % 4 for k in (2, 1, 3)]
    def pack_more(low, shift, east, west):
        old = state[1, 0, OWN + low : OWN + low + 8]
        east = jnp.where(between(lane8, shift + 24, shift + 32), roll(old, 40 + shift, 1), east)
        for p in range(2 * NTR):
            plane = c[p // 2, p % 2, 8 + low : 16 + low]
            west = jnp.where(lane8 == shift + 48 + p, roll(plane, shift + 48 + p, 1), west)
            east = jnp.where(lane8 == shift + 49 + p, roll(plane, shift + 50 + p, 1), east)
        return east, west

    pack_sides(1, late, pack_more)

    halo(1, side_pack.at[1, 0], side_in.at[1, 0], 1, 0)
    halo(1, side_pack.at[1, 1], side_in.at[1, 1], -1, 0)

    @pl.when(has_n)
    def _():
        halo(1, state.at[:, 0, END - 16 : END], state.at[:, 0, 0:OWN], 0, 1)
        halo(1, c.at[:, :, CY : CY + 8], c.at[:, :, 0:8], 0, 1)

    @pl.when(has_s)
    def _():
        halo(1, state.at[:, 0, OWN : OWN + 8], state.at[:, 0, END:HIGH], 0, -1)
        halo(1, c.at[:, :, 8:16], c.at[:, :, CY + 8 : CY + 16], 0, -1)

    @pl.when(me == 0)
    def _():
        above[...] = jnp.zeros_like(above)

    @pl.when(me == ND - 1)
    def _():
        below[...] = jnp.zeros_like(below)

    for ref in (x, state):
        for k in range(2):
            ref[:, k, HIGH:RX] = jnp.zeros((ref.shape[0], RX - HIGH, CX), F32)
    state[2, 1, 0:LOW] = jnp.zeros((LOW, CX), F32)
    state_b[2, :, 0:LOW] = jnp.zeros((2, LOW, CX), F32)

    def unpack_sides(phase, fields, extra=None):
        side = (lane8 < 8) | (lane8 >= CX - 8)
        for i in range(-1, 17):
            if i < 0:
                west, east, shift, ok = corner_in[0], corner_in[1], 56 * phase, side & has_s
            elif i == 16:
                west, east, shift, ok = corner_in[2], corner_in[3], 56 * phase, side & has_n
            else:
                j = 8 * (i % 8)
                west, east = side_in[phase, 0, j : j + 8], side_in[phase, 1, j : j + 8]
                shift, ok = 64 * (i // 8), side
            low = OWN + 8 * i
            for f, ref in enumerate(fields):
                start = shift + 8 * f + 8
                value = roll(jnp.where(between(lane8, start, start + 8), east, west), -start, 1)
                value = jnp.where(ok, value, 0.0)
                if extra is not None and f == 1 and 0 <= i < 16:
                    value = jnp.where(lane8 == CX - 9, roll(west, 88 - shift, 1), value)
                ref[low : low + 8] = value
            if extra is not None and 0 <= i < 16:
                extra(8 * i, shift, west, east)

    @pl.when(inner)
    def _():
        got(halo_got.at[0], 272)

    @pl.when(jnp.logical_not(inner))
    def _():
        got(halo_got.at[0], 200)

    unpack_sides(0, [x.at[f, 1] for f in range(7)])

    @pl.when(jnp.logical_not(has_s))
    def _():
        x[:, 0, LOW:OWN] = jnp.zeros((7, 8, CX), F32)

    @pl.when(jnp.logical_not(has_n))
    def _():
        x[:, 0, END:HIGH] = jnp.zeros((7, 8, CX), F32)

    def shifted(pair, steps):
        lane = lanes(pair[0].shape[0])
        edge = lane == (0 if steps > 0 else CX - 1)
        main, side = (roll(value, steps, 1) for value in pair)
        return jnp.where(edge, side, main), jnp.where(edge, main, side)

    def both(ref, low, size):
        return ref[0, low : low + size], ref[1, low : low + size]

    step = 24
    for low in range(LOW, HIGH, step):
        here = slice(low, low + step)
        count = both(x.at[6], low, step)
        count_e = shifted(count, -1)
        count_n = both(x.at[6], low + 1, step)
        thick = [both(x.at[l], low, step) for l in range(2)]
        thick_e = [shifted(thick[l], -1) for l in range(2)]
        for k in range(2):
            min_e = jnp.minimum(count[k], count_e[k])
            min_n = jnp.minimum(count[k], count_n[k])
            sums = [0.0] * 4
            for l in range(2):
                north = x[l, k, low + 1 : low + 1 + step]
                de = jnp.where(first + l < min_e, 0.5 * (thick[l][k] + thick_e[l][k]), 0.0)
                dn = jnp.where(first + l < min_n, 0.5 * (thick[l][k] + north), 0.0)
                face_e[l, k, here] = de
                face_n[l, k, here] = dn
                new = [de, dn, x[2 + l, k, here] * de, x[4 + l, k, here] * dn]
                sums = [a + b for a, b in zip(sums, new)]
            for f in range(4):
                local[f, k, here] = sums[f]

    def put_block(i, block):
        edge_send[i // EB, 8 * (i % EB) : 8 * (i % EB) + 8] = block

    for i in range(9):
        block = jnp.zeros((8, CX), F32)
        for j in range(2):
            low = LOW + 72 * j + 8 * i
            for f in range(4):
                start = 64 * j + 16 * f
                block = jnp.where(
                    lane8 == start, roll(local[f, 0, low : low + 8], start + 1, 1), block
                )
                block = jnp.where(
                    between(lane8, start + 1, start + 16),
                    roll(local[f, 1, low : low + 8], start + 9, 1),
                    block,
                )
        put_block(i, block)
    for f in range(4):
        put_block(9 + f, local[f, 0, END - 1 : END + 7])
        put_block(13 + f, local[f, 0, LOW:OWN])
    for i in range(17, NE * EB):
        put_block(i, jnp.zeros((8, CX), F32))

    owner = core == 0

    @pl.when(owner)
    def _():
        for q in chips:
            remote(edge_send.at[q], edge_in.at[me], edge_sent, edge_got, member(2 * q)).start()

    @pl.when(jnp.logical_not(owner))
    def _():
        for q in chips + [chip]:
            remote(edge_send.at[q], edge_in.at[me], edge_sent, edge_got, member(2 * q)).start()

    got(rs_got, 448)
    mine = main_send[me]
    for peer in peers:
        mine = mine + main_in[peer]
    main_all[chip, core] = mine
    piece = main_all.at[chip, core]
    for q in chips:
        remote(piece, piece, sent, ag_got, member(2 * q + core)).start()

    @pl.when(outer)
    def _():
        for i in range(4):
            low = OWN + 32 * i
            here = slice(low, low + 32)
            flux = both(local.at[2], low, 32)
            value = flux[0] - shifted(flux, 1)[0] + local[3, 0, here] - local[3, 0, low - 1 : low + 31]
            outer_send[i // 2, 32 * (i % 2) : 32 * (i % 2) + 32] = value
        for j in range(2):
            low = OWN + 64 * j
            outer_send[j, 64:128] = local[0, 0, low : low + 64]
            outer_send[j, 128:200] = local[1, 0, low - 8 : low + 64]
            block = jnp.zeros((8, CX), F32)
            for r in range(8):
                turned = roll(local[0, 1, low + 8 * r : low + 8 * r + 8], r + 1, 1)
                block = jnp.where(lane8 == r, turned, block)
            outer_send[j, 200:208] = block
        remote(outer_send, outer_pair, outer_sent, half_got, member(partner)).start()

    @pl.when(owner)
    def _():
        got(edge_got, 7 * 8 * EB)
        edge = edge_send[chip]
        for peer in peers:
            edge = edge + edge_in[peer]
        edge_all[chip] = edge
        for peer in far_first:
            remote(edge_all.at[chip], edge_all.at[chip], edge_sent, edge_all_got, member(peer)).start()

    @pl.when(outer)
    def _():
        got(half_got, 416)
        outer_sum[...] = outer_send[core] + outer_pair[core]
        middle_chip = jnp.where(upper, 2, ND - 4)
        remote(outer_sum, outer_in, outer_sent, outer_got, member(middle_chip + core)).start()

    send_tracers(1)

    @pl.when(inner)
    def _():
        got(halo_got.at[1], 392)
        left(sent_late, 392)

    @pl.when(jnp.logical_not(has_s))
    def _():
        got(halo_got.at[1], 248)
        left(sent_late, 272)

    @pl.when(jnp.logical_not(has_n))
    def _():
        got(halo_got.at[1], 272)
        left(sent_late, 248)


    def put_tracers(low, shift, west, east):
        for p in range(2 * NTR):
            value = jnp.where(lane8 <= shift + 48 + p, east, west)
            edge_c[p // 2, p % 2, low : low + 8] = roll(value, 79 - shift - p, 1)

    unpack_sides(1, [state.at[f, 1] for f in range(3)], put_tracers)

    @pl.when(jnp.logical_not(has_s))
    def _():
        state[:, 0, 0:OWN] = jnp.zeros((3, OWN, CX), F32)
        c[:, :, 0:8] = jnp.zeros((NTR, 2, 8, CX), F32)

    @pl.when(jnp.logical_not(has_n))
    def _():
        state[:, 0, END:HIGH] = jnp.zeros((3, 8, CX), F32)
        c[:, :, CY + 8 : CY + 16] = jnp.zeros((NTR, 2, 8, CX), F32)

    for low in range(LOW, HIGH, step):
        here = slice(low, low + step)
        is_wet = [jnp.where(value > 0.0, 1.0, 0.0) for value in both(x.at[6], low, step)]
        wet_e = shifted(is_wet, -1)
        wet_n = [jnp.where(value > 0.0, 1.0, 0.0) for value in both(x.at[6], low + 1, step)]
        for k in range(2):
            tw[k, here] = tau * is_wet[k]
            ae[k, here] = (1.0 - tau) * (is_wet[k] * wet_e[k])
            an[k, here] = (1.0 - tau) * (is_wet[k] * wet_n[k])
            wet_e_all[k, here] = (tau * coupling) * (is_wet[k] * wet_e[k])
            wet_n_all[k, here] = (tau * coupling) * (is_wet[k] * wet_n[k])

    got(ag_got, 192)
    half = main_all.at[:, core]
    remote(half, half, sent, forward_got, member(partner)).start()

    @pl.when(owner)
    def _():
        got(edge_all_got, 3 * 8 * EB)

    @pl.when(jnp.logical_not(owner))
    def _():
        got(edge_all_got, 4 * 8 * EB)

    got(forward_got, 256)

    def block_of(i):
        return edge_all[i // EB, 8 * (i % EB) : 8 * (i % EB) + 8]

    rim = (lane8 < 7) | (lane8 >= CX - 8)
    last_lane = lane8 == CX - 1
    row8 = rows_of(8)
    for i in range(18):
        block = block_of(i % 9)
        shift = 64 * (i // 9)
        here = slice(LOW + 8 * i, LOW + 8 * i + 8)
        sums = []
        for f in range(4):
            if i == 0:
                main = block_of(13 + f)
            elif i == 17:
                main = jnp.where(row8 == 7, 0.0, roll(block_of(9 + f), -1, 0))
            else:
                p, part_low = (i - 1) // 2, 16 * f + 8 * ((i - 1) % 2)
                main = main_all[p // 2, p % 2, part_low : part_low + 8]
                if i == 16:
                    main = jnp.where(row8 == 7, jnp.broadcast_to(block_of(9 + f)[0:1], (8, CX)), main)
            main = jnp.where(last_lane, roll(block, CX - 1 - 16 * f - shift, 1), main)
            side = jnp.where(rim, roll(block, -(9 + 16 * f + shift), 1), 0.0)
            total[f, 0, here] = main
            total[f, 1, here] = side
            sums.append((main, side))
        for k in range(2):
            east, north = wet_e_all[k, here], wet_n_all[k, here]
            be[k, here] = east * sums[0][k]
            bn[k, here] = north * sums[1][k]
            ce[k, here] = east * sums[2][k]
            cn[k, here] = north * sums[3][k]

    def substep(old, new):
        bottom_row = rows_of(step) == step - 1

        def rise(low):
            here = slice(low, low + step)
            east = both(old.at[1], low, step)
            west = shifted(east, 1)
            north = both(old.at[2], low, step)
            south = both(old.at[2], low - 1, step)
            level = []
            for k in range(2):
                value = old[0, k, here] - tw[k, here] * (east[k] - west[k] + north[k] - south[k])
                new[0, k, here] = value
                level.append(value)
            return level, east, north

        def move(low, held, beyond):
            here = slice(low, low + step)
            level, east, north = held
            level_e = shifted(level, -1)
            for k in range(2):
                level_n = roll(level[k], -1, 0)
                if beyond is not None:
                    first_row = jnp.broadcast_to(beyond[0][k][0:1], (step, CX))
                    level_n = jnp.where(bottom_row, first_row, level_n)
                new[1, k, here] = ae[k, here] * east[k] - be[k, here] * (level_e[k] - level[k]) + ce[k, here]
                new[2, k, here] = an[k, here] * north[k] - bn[k, here] * (level_n - level[k]) + cn[k, here]

        held = rise(LOW)
        for low in range(LOW, HIGH, step):
            coming = rise(low + step) if low + step < HIGH else None
            move(low, held, coming)
            held = coming

    def two(i, carry):
        substep(state, state_b)
        substep(state_b, state)
        return carry

    lax.fori_loop(0, NSUB // 2, two, 0)

    flow_rows = [(OWN - 8, 8)] + [(OWN + 32 * i, 32) for i in range(4)]
    for low, size in flow_rows:
        here = slice(low, low + size)
        shift_n = state[2, 0, here] - coupling * total[3, 0, here]
        for l in range(2):
            flow_n[l, here] = face_n[l, 0, here] * (x[4 + l, 0, here] + shift_n)
        prod_n[here] = shift_n

    for i in range(4):
        low = OWN + 32 * i
        here = slice(low, low + 32)
        mine = slice(32 * i, 32 * i + 32)
        shift_e = [state[1, k, here] - coupling * total[2, k, here] for k in range(2)]
        divs = []
        for l in range(2):
            flow = [face_e[l, k, here] * (x[2 + l, k, here] + shift_e[k]) for k in range(2)]
            west = shifted(flow, 1)[0]
            flow_e[l, 0, mine] = flow[0]
            flow_e[l, 1, mine] = west
            divs.append(flow[0] - west + flow_n[l, here] - flow_n[l, low - 1 : low + 31])
        div_1[mine] = divs[1]
        pair_send[mine] = divs[0] + divs[1]

    def divergence_of(parts, base):
        here = pl.ds(base, 64)
        shift_e = [state[1, k, here] - coupling * total[2, k, here] for k in range(2)]
        flow = parts[64:128] * shift_e[0]
        block = parts[200:208]
        column = jnp.concatenate([roll(block, -r, 1) for r in range(8)], axis=0)
        west = jnp.where(lanes(64) == 0, column * roll(shift_e[1], 1, 1), roll(flow, 1, 1))
        flow_t[0:72] = parts[128:200] * prod_n[pl.ds(base - 8, 72)]
        return parts[0:64] + flow - west + flow_t[8:72] - flow_t[7:71]

    @pl.when(jnp.logical_not(outer))
    def _():
        got(outer_got, 208)
        value = divergence_of(outer_in, pl.multiple_of(OWN + 64 * core, 8))
        outer_div[core] = value
        pair_send[CY : CY + 64] = value
        remote(pair_send, pair_div, sent, div_got, member(partner)).start()

    @pl.when(outer)
    def _():
        for j in range(2):
            pair_div[64 * j : 64 * j + 64] = divergence_of(outer_pair.at[j], OWN + 64 * j)
        outer_div[...] = jnp.zeros_like(outer_div)

    for low, size in flow_rows:
        here = slice(low, low + size)
        flow_w[here] = total[3, 0, here] + total[1, 0, here] * prod_n[here]

    for i in range(4):
        low = OWN + 32 * i
        here = slice(low, low + 32)
        mine = slice(32 * i, 32 * i + 32)
        shift_e = [state[1, k, here] - coupling * total[2, k, here] for k in range(2)]
        flow = [total[2, k, here] + total[0, k, here] * shift_e[k] for k in range(2)]
        whole_div[mine] = flow[0] - shifted(flow, 1)[0] + flow_w[here] - flow_w[low - 1 : low + 31]
        count = x[6, 0, here]
        for l in range(2):
            fe, fw = flow_e[l, 0, mine], flow_e[l, 1, mine]
            fn, fs = flow_n[l, here], flow_n[l, low - 1 : low + 31]
            gain = jnp.where(first + l < count, tracer_time / x[l, 0, here], 0.0)
            plus_e, minus_w = jnp.maximum(fe, 0.0), jnp.minimum(fw, 0.0)
            plus_n, minus_s = jnp.maximum(fn, 0.0), jnp.minimum(fs, 0.0)
            coef[l, 0, mine] = gain * (plus_e - fe)
            coef[l, 1, mine] = gain * (fw - minus_w)
            coef[l, 2, mine] = gain * (plus_n - fn)
            coef[l, 3, mine] = gain * (fs - minus_s)
            coef[l, 4, mine] = 1.0 - gain * (plus_e - minus_w + plus_n - minus_s)
            coef[l, 5, mine] = gain

    s_out[0] = state[0, 0, rows_own]
    e_out[0] = state[1, 0, rows_own]
    n_out[0] = state[2, 0, rows_own]

    lane32 = lanes(32)
    for l in range(2):
        for i in range(4):
            mine = slice(32 * i, 32 * i + 32)
            low = 8 + 32 * i
            a_e, a_w, a_n, a_s, a_c = (coef[l, j, mine] for j in range(5))
            for m in range(NTR):
                value = c[m, l, low : low + 32]
                edge = edge_c[m, l, mine]
                value_e = jnp.where(lane32 == CX - 1, edge, roll(value, -1, 1))
                value_w = jnp.where(lane32 == 0, edge, roll(value, 1, 1))
                part[m, l, mine] = (
                    a_c * value
                    + a_e * value_e
                    + a_w * value_w
                    + a_n * c[m, l, low + 1 : low + 33]
                    + a_s * c[m, l, low - 1 : low + 31]
                )

    halos_sent = [(inner, 272), (jnp.logical_not(inner), 200)]
    for where, rows in halos_sent:
        @pl.when(where & outer)
        def _(rows=rows):
            left(sent, rows + 896)

        @pl.when(where & jnp.logical_not(outer))
        def _(rows=rows):
            left(sent, rows + 1088)

    @pl.when(owner)
    def _():
        left(edge_sent, 10 * 8 * EB)

    @pl.when(jnp.logical_not(owner))
    def _():
        left(edge_sent, 4 * 8 * EB)

    @pl.when(outer)
    def _():
        left(outer_sent, 624)

    @pl.when(jnp.logical_not(outer))
    def _():
        got(div_got, 192)
        outer_div[other] = pair_div[CY : CY + 64]

    odd = core == 1
    for i in range(4):
        mine = slice(32 * i, 32 * i + 32)
        beyond = outer_div[i // 2, 32 * (i % 2) : 32 * (i % 2) + 32]
        near = pair_div[mine]
        here = pair_send[mine]
        deeper = jnp.where(
            upper,
            whole_div[mine] - here - beyond - jnp.where(odd, near, 0.0),
            beyond + jnp.where(odd, 0.0, near),
        )
        bottom = -deeper
        middle = -(div_1[mine] + deeper)
        top = jnp.where(me == 0, 0.0, -(here + deeper))
        for l in range(2):
            under_flow, over_flow = (middle, top) if l == 0 else (bottom, middle)
            gain = coef[l, 5, mine]
            lift[l, 0, mine] = gain * (jnp.minimum(under_flow, 0.0) - jnp.maximum(over_flow, 0.0))
            lift[l, 1, mine] = gain * jnp.maximum(under_flow, 0.0)
            lift[l, 2, mine] = -gain * jnp.minimum(over_flow, 0.0)

    @pl.when(me < ND - 1)
    def _():
        got(up_got, NTR * CY)
        left(down_sent, NTR * CY)

    @pl.when(me > 0)
    def _():
        got(down_got, NTR * CY)
        left(up_sent, NTR * CY)


def store(part, s_ref, e_ref, n_ref, c, below, above, lift, c_out, s_out, e_out, n_out, new_c, sem):
    copies = [
        pltpu.make_async_copy(source, target, sem.at[NTR + i])
        for i, (source, target) in enumerate([(s_ref, s_out), (e_ref, e_out), (n_ref, n_out)])
    ]
    for copy in copies:
        copy.start()
    for pair in range(0, NTR, 2):
        for l in range(2):
            for i in range(4):
                mine = slice(32 * i, 32 * i + 32)
                low = 8 + 32 * i
                a_c, a_b, a_a = (lift[l, j, mine] for j in range(3))
                for m in (pair, pair + 1):
                    under = c[m, 1, low : low + 32] if l == 0 else below[m, mine]
                    over = above[m, mine] if l == 0 else c[m, 0, low : low + 32]
                    new_c[m, l, mine] = (
                        part[m, l, mine] + a_c * c[m, l, low : low + 32] + a_b * under + a_a * over
                    )
        for m in (pair, pair + 1):
            copy = pltpu.make_async_copy(new_c.at[m], c_out.at[m, :, 0], sem.at[m])
            copy.start()
            copies.append(copy)
    for copy in copies:
        copy.wait()


def body(thickness, u_layer, v_layer, tracers, sea_level, u_column, v_column, wet_cells, levels):
    any_spec = pl.BlockSpec(memory_space=pl.ANY)
    near_spec = pl.BlockSpec(memory_space=pltpu.VMEM)

    def vmem(*shape):
        return pltpu.VMEM(shape, F32)

    plane = vmem(CY, CX)
    wide = vmem(2, RX, CX)
    wide2 = vmem(2, 2, RX, CX)
    column_c = vmem(NTR, CY, CX)
    flat = pltpu.VMEM((CY, CX), jnp.int32)
    halves = vmem(4, 2, 64, CX)
    edges = vmem(NE, 8 * EB, CX)
    dma = pltpu.SemaphoreType.DMA
    shapes = [tracers.shape] + [sea_level.shape] * 3
    results = pl.pallas_call(
        kernel,
        out_shape=(
            vmem(NTR, 2, CY, CX), *(pltpu.VMEM(shape, F32) for shape in shapes[1:]),
            vmem(NTR, 2, CY + 16, CX), column_c, column_c, vmem(2, 3, CY, CX),
        ),
        in_specs=[pl.BlockSpec(memory_space=pltpu.HBM)] * 9,
        out_specs=(near_spec,) * 8,
        scratch_shapes=[
            vmem(7, 2, RX, CX), vmem(3, 2, RX, CX), flat, flat,
            vmem(2, 2, 64, CX), vmem(2, 2, 64, CX), vmem(2, 2, 8, CX), vmem(4, 8, CX), vmem(11 * CY, CX),
            vmem(NTR, 2, CY, CX),
            vmem(ND, 64, CX), vmem(ND, 64, CX), halves,
            edges, vmem(ND, 8 * EB, CX), edges,
            wide2, wide2, vmem(4, 2, RX, CX), vmem(4, 2, RX, CX),
            wide, wide, wide, wide, wide, wide, wide, wide, wide, vmem(3, 2, RX, CX),
            vmem(2, 208, CX), vmem(2, 208, CX), vmem(208, CX), vmem(208, CX), vmem(2, 64, CX),
            vmem(2, RX, CX), vmem(RX, CX), vmem(RX, CX), vmem(2, 2, CY, CX), vmem(RX, CX), vmem(2, 6, CY, CX),
            plane, plane, vmem(CY + 64, CX), vmem(CY + 64, CX),
            dma((2,)), dma, dma, dma, dma, dma, dma,
            dma((2,)), dma, dma, dma, dma, dma, dma, dma,
            dma, dma, dma,
        ],
        compiler_params=pltpu.CompilerParams(
            collective_id=0, has_side_effects=True, vmem_limit_bytes=48 * 1024 * 1024
        ),
    )(*[
        pltpu.with_memory_space_constraint(x, pltpu.HBM)
        for x in (thickness, u_layer, v_layer, tracers, sea_level, u_column, v_column, wet_cells, levels)
    ])
    return pl.pallas_call(
        store,
        out_shape=tuple(jax.ShapeDtypeStruct(shape, F32) for shape in shapes),
        in_specs=[near_spec] * 8,
        out_specs=(any_spec,) * 4,
        scratch_shapes=[vmem(NTR, 2, CY, CX), dma((NTR + 3,))],
    )(*[pltpu.with_memory_space_constraint(x, pltpu.VMEM) for x in results])


def solution(mesh):
    return jax.shard_map(
        body,
        mesh=mesh,
        in_specs=(
            P("depth", "tiles", None, None),
            P("depth", "tiles", None, None),
            P("depth", "tiles", None, None),
            P(None, "depth", "tiles", None, None),
            P("tiles", None, None),
            P("tiles", None, None),
            P("tiles", None, None),
            P("tiles", None, None),
            P("tiles", None, None),
        ),
        out_specs=(
            P(None, "depth", "tiles", None, None),
            P("tiles", None, None),
            P("tiles", None, None),
            P("tiles", None, None),
        ),
        check_vma=False,
    )
```

```python
import functools

import jax
import jax.numpy as jnp
from jax import lax
from jax.experimental import pallas as pl
from jax.experimental.pallas import tpu as pltpu
from jax.sharding import PartitionSpec as P

TROWS = 8
NSUB = 8
NTR = 6
ND = 8
NE = 4
EB = 5
CY = 128
CX = 128
RX = CY + 32
OWN = 16
END = OWN + CY
LOW = OWN - 8
HIGH = END + 8

tau = 0.45
coupling = 1.0 / 16
tracer_time = 0.1

MESH = pl.DeviceIdType.MESH
F32 = jnp.float32


def roll(x, shift, axis):
    shift = shift % x.shape[axis]
    return x if shift == 0 else pltpu.roll(x, shift, axis)


def lanes(rows, width=CX):
    return lax.broadcasted_iota(jnp.int32, (rows, width), 1)


def rows_of(rows, width=CX):
    return lax.broadcasted_iota(jnp.int32, (rows, width), 0)


def between(x, low, high):
    return (x >= low) & (x < high)


def kernel(
    h_in, u_in, v_in, c_in, sea_in, uc_in, vc_in, wet_in, lev_in,
    part, s_out, e_out, n_out, c, below, above, lift,
    x, state, wet, lev,
    side_pack, side_in, corner_pack, corner_in, sizes,
    edge_c,
    main_send, pair_in, chip_sum, main_in, main_all,
    edge_send, edge_in, edge_all,
    face_e, face_n, local, total,
    tw, ae, an, be, bn, ce, cn, wet_e_all, wet_n_all, state_b,
    outer_send, outer_pair, outer_sum, outer_in, outer_next, outer_div,
    flow_n, flow_t, flow_w, flow_e, prod_n, coef, div_1, whole_div, pair_send, pair_div,
    loc_sem, sent, sent_late, edge_sent, outer_sent, up_sent, down_sent,
    halo_got, pair_got, rs_got, ag_got, forward_got, edge_got, edge_all_got, half_got, outer_got,
    up_got, down_got, div_got,
):
    me = lax.axis_index("depth")
    tile = lax.axis_index("tiles")
    tx = tile // TROWS
    ty = tile % TROWS
    chip = me // 2
    core = me % 2
    other = 1 - core
    partner = 2 * chip + other
    upper = me < ND // 2
    outer = (me < 2) | (me >= ND - 2)
    cols = 8

    def tile_at(dx, dy):
        return ((tx + dx + cols) % cols) * TROWS + (ty + dy + TROWS) % TROWS

    def member(which):
        return {"tiles": tile, "depth": which}

    def beside(dx, dy):
        return {"tiles": tile_at(dx, dy), "depth": me}

    def remote(source, target, send, recv, where):
        return pltpu.make_async_remote_copy(
            src_ref=source, dst_ref=target, send_sem=send, recv_sem=recv,
            device_id=where, device_id_type=MESH,
        )

    has_n = ty < TROWS - 1
    has_s = ty > 0
    inner = has_n & has_s

    rows_own = slice(OWN, END)

    def got(sem, rows):
        remote(sizes.at[0:rows], sizes.at[0:rows], sem, sem, member(partner)).wait_recv()

    def left(sem, rows):
        remote(sizes.at[0:rows], sizes.at[0:rows], sem, sem, member(partner)).wait_send()

    def fetch(source, target):
        pltpu.make_async_copy(source, target, loc_sem.at[0]).start()

    barrier = pltpu.get_barrier_semaphore()

    def greet(dy):
        for dx in (1, -1) if dy == 0 else (0, 1, -1):
            pl.semaphore_signal(barrier, inc=1, device_id=beside(dx, dy), device_id_type=MESH)

    greet(0)

    @pl.when(has_n)
    def _():
        greet(1)

    @pl.when(has_s)
    def _():
        greet(-1)

    fetch(h_in.at[:, 0], x.at[0:2, 0, rows_own])
    fetch(wet_in.at[0], wet)
    fetch(lev_in.at[0], lev)
    fetch(u_in.at[:, 0], x.at[2:4, 0, rows_own])
    fetch(v_in.at[:, 0], x.at[4:6, 0, rows_own])
    fetch(sea_in.at[0], state.at[0, 0, rows_own])
    fetch(uc_in.at[0], state.at[1, 0, rows_own])
    fetch(vc_in.at[0], state.at[2, 0, rows_own])
    peers = [(me + k) % ND for k in range(1, ND)]
    for peer in peers:
        pl.semaphore_signal(barrier, inc=1, device_id=member(peer), device_id_type=MESH)
    fetch_c = pltpu.make_async_copy(c_in.at[:, :, 0], c.at[:, :, 8 : CY + 8], loc_sem.at[1])
    fetch_c.start()

    fetched = 11 * CY
    pltpu.make_async_copy(sizes.at[0:fetched], sizes.at[0:fetched], loc_sem.at[0]).wait()

    lane8 = lanes(8)
    x[6, 0, rows_own] = (wet[...] * lev[...]).astype(F32)

    def pack_sides(phase, fields, extra=None):
        for i in range(8):
            east = west = jnp.zeros((8, CX), F32)
            for j in range(2):
                low = OWN + 64 * j + 8 * i
                for f, ref in enumerate(fields):
                    turned = roll(ref[low : low + 8], 8 * f + 8 + 64 * j, 1)
                    start = 64 * j + 8 * f
                    west = jnp.where(between(lane8, start + 8, start + 16), turned, west)
                    east = jnp.where(between(lane8, start, start + 8), turned, east)
                if extra is not None:
                    east, west = extra(64 * j + 8 * i, 64 * j, east, west)
            side_pack[phase, 0, 8 * i : 8 * i + 8] = east
            side_pack[phase, 1, 8 * i : 8 * i + 8] = west

    early = [x.at[f, 0] for f in range(7)]
    late = [state.at[f, 0] for f in range(3)]
    pack_sides(0, early)

    for j, low in enumerate((OWN, END - 8)):
        east = west = jnp.zeros((8, CX), F32)
        for f, ref in enumerate(early + late):
            turned = roll(ref[low : low + 8], 8 * f + 8, 1)
            west = jnp.where(between(lane8, 8 * f + 8, 8 * f + 16), turned, west)
            east = jnp.where(between(lane8, 8 * f, 8 * f + 8), turned, east)
        corner_pack[0, j] = east
        corner_pack[1, j] = west

    first = (2 * me).astype(F32)
    lane16 = lanes(16)
    row16 = rows_of(16)

    def next_row(ref, p):
        low = OWN + 16 * p
        if p < ND - 1:
            return ref[low + 1 : low + 17]
        return jnp.where(row16 == 15, 0.0, roll(ref[low : low + 16], -1, 0))

    for p in range(ND):
        low = OWN + 16 * p
        here = slice(low, low + 16)
        count = x[6, 0, here]
        count_e = jnp.minimum(count, jnp.where(lane16 == CX - 1, 0.0, roll(count, -1, 1)))
        count_n = jnp.minimum(count, next_row(x.at[6, 0], p))
        sums = [0.0] * 4
        for l in range(2):
            thick = x[l, 0, here]
            de = jnp.where(first + l < count_e, 0.5 * (thick + roll(thick, -1, 1)), 0.0)
            dn = jnp.where(first + l < count_n, 0.5 * (thick + next_row(x.at[l, 0], p)), 0.0)
            new = [de, dn, x[2 + l, 0, here] * de, x[4 + l, 0, here] * dn]
            sums = [a + b for a, b in zip(sums, new)]
        for f in range(4):
            main_send[p // 2, p % 2, 16 * f : 16 * f + 16] = sums[f]

    @pl.when(inner)
    def _():
        pl.semaphore_wait(barrier, 8 + ND - 1)

    @pl.when(jnp.logical_not(inner))
    def _():
        pl.semaphore_wait(barrier, 5 + ND - 1)

    def halo(phase, source, target, dx, dy):
        sem = sent if phase == 0 else sent_late
        remote(source, target, sem, halo_got.at[phase], beside(dx, dy)).start()

    halo(0, side_pack.at[0, 0], side_in.at[0, 0], 1, 0)
    halo(0, side_pack.at[0, 1], side_in.at[0, 1], -1, 0)

    @pl.when(has_n)
    def _():
        halo(0, corner_pack.at[0, 1], corner_in.at[0], 1, 1)
        halo(0, corner_pack.at[1, 1], corner_in.at[1], -1, 1)
        halo(0, x.at[:, 0, END - 8 : END], x.at[:, 0, LOW:OWN], 0, 1)

    @pl.when(has_s)
    def _():
        halo(0, corner_pack.at[0, 0], corner_in.at[2], 1, -1)
        halo(0, corner_pack.at[1, 0], corner_in.at[3], -1, -1)
        halo(0, x.at[:, 0, OWN : OWN + 8], x.at[:, 0, END:HIGH], 0, -1)

    remote(main_send.at[:, other], pair_in, sent, pair_got, member(partner)).start()

    fetch_c.wait()
    rows_c = slice(8, CY + 8)

    def send_tracers(i):
        part = slice(0, 2) if i == 0 else slice(2, NTR)

        @pl.when(me > 0)
        def _():
            remote(
                c.at[part, 0, rows_c], below.at[part], up_sent, up_got, member((me + ND - 1) % ND)
            ).start()

        @pl.when(me < ND - 1)
        def _():
            remote(
                c.at[part, 1, rows_c], above.at[part], down_sent, down_got, member((me + 1) % ND)
            ).start()

    send_tracers(0)

    got(pair_got, 256)
    chips = [(chip + k) % 4 for k in (2, 1, 3)]
    far_first = [(me + k) % ND for k in (4, 5, 3, 2, 6, 7, 1)]
    for q in range(4):
        chip_sum[q] = main_send[q, core] + pair_in[q]
    for q in chips:
        remote(chip_sum.at[q], main_in.at[chip], sent, rs_got, member(2 * q + core)).start()

    def pack_more(low, shift, east, west):
        old = state[1, 0, OWN + low : OWN + low + 8]
        east = jnp.where(between(lane8, shift + 24, shift + 32), roll(old, 40 + shift, 1), east)
        for p in range(2 * NTR):
            plane = c[p // 2, p % 2, 8 + low : 16 + low]
            west = jnp.where(lane8 == shift + 48 + p, roll(plane, shift + 48 + p, 1), west)
            east = jnp.where(lane8 == shift + 49 + p, roll(plane, shift + 50 + p, 1), east)
        return east, west

    pack_sides(1, late, pack_more)

    halo(1, side_pack.at[1, 0], side_in.at[1, 0], 1, 0)
    halo(1, side_pack.at[1, 1], side_in.at[1, 1], -1, 0)

    @pl.when(has_n)
    def _():
        halo(1, state.at[:, 0, END - 16 : END], state.at[:, 0, 0:OWN], 0, 1)
        halo(1, c.at[:, :, CY : CY + 8], c.at[:, :, 0:8], 0, 1)

    @pl.when(has_s)
    def _():
        halo(1, state.at[:, 0, OWN : OWN + 8], state.at[:, 0, END:HIGH], 0, -1)
        halo(1, c.at[:, :, 8:16], c.at[:, :, CY + 8 : CY + 16], 0, -1)

    @pl.when(me == 0)
    def _():
        above[...] = jnp.zeros_like(above)

    @pl.when(me == ND - 1)
    def _():
        below[...] = jnp.zeros_like(below)

    for ref in (x, state):
        for k in range(2):
            ref[:, k, HIGH:RX] = jnp.zeros((ref.shape[0], RX - HIGH, CX), F32)
    state[2, 1, 0:LOW] = jnp.zeros((LOW, CX), F32)
    state_b[2, :, 0:LOW] = jnp.zeros((2, LOW, CX), F32)

    def unpack_sides(phase, fields, extra=None):
        side = (lane8 < 8) | (lane8 >= CX - 8)
        for i in range(-1, 17):
            if i < 0:
                west, east, shift, ok = corner_in[0], corner_in[1], 56 * phase, side & has_s
            elif i == 16:
                west, east, shift, ok = corner_in[2], corner_in[3], 56 * phase, side & has_n
            else:
                j = 8 * (i % 8)
                west, east = side_in[phase, 0, j : j + 8], side_in[phase, 1, j : j + 8]
                shift, ok = 64 * (i // 8), side
            low = OWN + 8 * i
            for f, ref in enumerate(fields):
                start = shift + 8 * f + 8
                value = roll(jnp.where(between(lane8, start, start + 8), east, west), -start, 1)
                value = jnp.where(ok, value, 0.0)
                if extra is not None and f == 1 and 0 <= i < 16:
                    value = jnp.where(lane8 == CX - 9, roll(west, 88 - shift, 1), value)
                ref[low : low + 8] = value
            if extra is not None and 0 <= i < 16:
                extra(8 * i, shift, west, east)

    @pl.when(inner)
    def _():
        got(halo_got.at[0], 272)

    @pl.when(jnp.logical_not(inner))
    def _():
        got(halo_got.at[0], 200)

    unpack_sides(0, [x.at[f, 1] for f in range(7)])

    @pl.when(jnp.logical_not(has_s))
    def _():
        x[:, 0, LOW:OWN] = jnp.zeros((7, 8, CX), F32)

    @pl.when(jnp.logical_not(has_n))
    def _():
        x[:, 0, END:HIGH] = jnp.zeros((7, 8, CX), F32)

    def shifted(pair, steps):
        lane = lanes(pair[0].shape[0])
        edge = lane == (0 if steps > 0 else CX - 1)
        main, side = (roll(value, steps, 1) for value in pair)
        return jnp.where(edge, side, main), jnp.where(edge, main, side)

    def both(ref, low, size):
        return ref[0, low : low + size], ref[1, low : low + size]

    step = 24
    for low in range(LOW, HIGH, step):
        here = slice(low, low + step)
        count = both(x.at[6], low, step)
        count_e = shifted(count, -1)
        count_n = both(x.at[6], low + 1, step)
        thick = [both(x.at[l], low, step) for l in range(2)]
        thick_e = [shifted(thick[l], -1) for l in range(2)]
        for k in range(2):
            min_e = jnp.minimum(count[k], count_e[k])
            min_n = jnp.minimum(count[k], count_n[k])
            sums = [0.0] * 4
            for l in range(2):
                north = x[l, k, low + 1 : low + 1 + step]
                de = jnp.where(first + l < min_e, 0.5 * (thick[l][k] + thick_e[l][k]), 0.0)
                dn = jnp.where(first + l < min_n, 0.5 * (thick[l][k] + north), 0.0)
                face_e[l, k, here] = de
                face_n[l, k, here] = dn
                new = [de, dn, x[2 + l, k, here] * de, x[4 + l, k, here] * dn]
                sums = [a + b for a, b in zip(sums, new)]
            for f in range(4):
                local[f, k, here] = sums[f]

    def put_block(i, block):
        edge_send[i // EB, 8 * (i % EB) : 8 * (i % EB) + 8] = block

    for i in range(9):
        block = jnp.zeros((8, CX), F32)
        for j in range(2):
            low = LOW + 72 * j + 8 * i
            for f in range(4):
                start = 64 * j + 16 * f
                block = jnp.where(
                    lane8 == start, roll(local[f, 0, low : low + 8], start + 1, 1), block
                )
                block = jnp.where(
                    between(lane8, start + 1, start + 16),
                    roll(local[f, 1, low : low + 8], start + 9, 1),
                    block,
                )
        put_block(i, block)
    for f in range(4):
        put_block(9 + f, local[f, 0, END - 1 : END + 7])
        put_block(13 + f, local[f, 0, LOW:OWN])
    for i in range(17, NE * EB):
        put_block(i, jnp.zeros((8, CX), F32))

    owner = core == 0

    @pl.when(owner)
    def _():
        for q in chips:
            remote(edge_send.at[q], edge_in.at[me], edge_sent, edge_got, member(2 * q)).start()

    @pl.when(jnp.logical_not(owner))
    def _():
        for q in chips + [chip]:
            remote(edge_send.at[q], edge_in.at[me], edge_sent, edge_got, member(2 * q)).start()

    got(rs_got, 192)
    mine = chip_sum[chip]
    for q in chips:
        mine = mine + main_in[q]
    main_all[chip, core] = mine
    piece = main_all.at[chip, core]
    for q in chips:
        remote(piece, piece, sent, ag_got, member(2 * q + core)).start()

    for i in range(4):
        low = OWN + 32 * i
        here = slice(low, low + 32)
        flux = both(local.at[2], low, 32)
        value = flux[0] - shifted(flux, 1)[0] + local[3, 0, here] - local[3, 0, low - 1 : low + 31]
        outer_send[i // 2, 32 * (i % 2) : 32 * (i % 2) + 32] = value
    for j in range(2):
        low = OWN + 64 * j
        outer_send[j, 64:128] = local[0, 0, low : low + 64]
        outer_send[j, 128:200] = local[1, 0, low - 8 : low + 64]
        block = jnp.zeros((8, CX), F32)
        for r in range(8):
            turned = roll(local[0, 1, low + 8 * r : low + 8 * r + 8], r + 1, 1)
            block = jnp.where(lane8 == r, turned, block)
        outer_send[j, 200:208] = block
    remote(outer_send, outer_pair, outer_sent, half_got, member(partner)).start()

    @pl.when(owner)
    def _():
        got(edge_got, 7 * 8 * EB)
        edge = edge_send[chip]
        for peer in peers:
            edge = edge + edge_in[peer]
        edge_all[chip] = edge
        for peer in far_first:
            remote(edge_all.at[chip], edge_all.at[chip], edge_sent, edge_all_got, member(peer)).start()

    @pl.when(outer)
    def _():
        got(half_got, 416)
        outer_sum[...] = outer_send[core] + outer_pair[core]
        middle_chip = jnp.where(upper, 2, ND - 4)
        remote(outer_sum, outer_in, outer_sent, outer_got, member(middle_chip + core)).start()

    send_tracers(1)

    @pl.when(inner)
    def _():
        got(halo_got.at[1], 392)
        left(sent_late, 392)

    @pl.when(jnp.logical_not(has_s))
    def _():
        got(halo_got.at[1], 248)
        left(sent_late, 272)

    @pl.when(jnp.logical_not(has_n))
    def _():
        got(halo_got.at[1], 272)
        left(sent_late, 248)


    def put_tracers(low, shift, west, east):
        for p in range(2 * NTR):
            value = jnp.where(lane8 <= shift + 48 + p, east, west)
            edge_c[p // 2, p % 2, low : low + 8] = roll(value, 79 - shift - p, 1)

    unpack_sides(1, [state.at[f, 1] for f in range(3)], put_tracers)

    @pl.when(jnp.logical_not(has_s))
    def _():
        state[:, 0, 0:OWN] = jnp.zeros((3, OWN, CX), F32)
        c[:, :, 0:8] = jnp.zeros((NTR, 2, 8, CX), F32)

    @pl.when(jnp.logical_not(has_n))
    def _():
        state[:, 0, END:HIGH] = jnp.zeros((3, 8, CX), F32)
        c[:, :, CY + 8 : CY + 16] = jnp.zeros((NTR, 2, 8, CX), F32)

    for low in range(LOW, HIGH, step):
        here = slice(low, low + step)
        is_wet = [jnp.where(value > 0.0, 1.0, 0.0) for value in both(x.at[6], low, step)]
        wet_e = shifted(is_wet, -1)
        wet_n = [jnp.where(value > 0.0, 1.0, 0.0) for value in both(x.at[6], low + 1, step)]
        for k in range(2):
            tw[k, here] = tau * is_wet[k]
            ae[k, here] = (1.0 - tau) * (is_wet[k] * wet_e[k])
            an[k, here] = (1.0 - tau) * (is_wet[k] * wet_n[k])
            wet_e_all[k, here] = (tau * coupling) * (is_wet[k] * wet_e[k])
            wet_n_all[k, here] = (tau * coupling) * (is_wet[k] * wet_n[k])

    got(ag_got, 192)
    half = main_all.at[:, core]
    remote(half, half, sent, forward_got, member(partner)).start()

    @pl.when(owner)
    def _():
        got(edge_all_got, 3 * 8 * EB)

    @pl.when(jnp.logical_not(owner))
    def _():
        got(edge_all_got, 4 * 8 * EB)

    got(forward_got, 256)

    def block_of(i):
        return edge_all[i // EB, 8 * (i % EB) : 8 * (i % EB) + 8]

    rim = (lane8 < 7) | (lane8 >= CX - 8)
    last_lane = lane8 == CX - 1
    row8 = rows_of(8)
    for i in range(18):
        block = block_of(i % 9)
        shift = 64 * (i // 9)
        here = slice(LOW + 8 * i, LOW + 8 * i + 8)
        sums = []
        for f in range(4):
            if i == 0:
                main = block_of(13 + f)
            elif i == 17:
                main = jnp.where(row8 == 7, 0.0, roll(block_of(9 + f), -1, 0))
            else:
                p, part_low = (i - 1) // 2, 16 * f + 8 * ((i - 1) % 2)
                main = main_all[p // 2, p % 2, part_low : part_low + 8]
                if i == 16:
                    main = jnp.where(row8 == 7, jnp.broadcast_to(block_of(9 + f)[0:1], (8, CX)), main)
            main = jnp.where(last_lane, roll(block, CX - 1 - 16 * f - shift, 1), main)
            side = jnp.where(rim, roll(block, -(9 + 16 * f + shift), 1), 0.0)
            total[f, 0, here] = main
            total[f, 1, here] = side
            sums.append((main, side))
        for k in range(2):
            east, north = wet_e_all[k, here], wet_n_all[k, here]
            be[k, here] = east * sums[0][k]
            bn[k, here] = north * sums[1][k]
            ce[k, here] = east * sums[2][k]
            cn[k, here] = north * sums[3][k]

    def substep(old, new):
        bottom_row = rows_of(step) == step - 1

        def rise(low):
            here = slice(low, low + step)
            east = both(old.at[1], low, step)
            west = shifted(east, 1)
            north = both(old.at[2], low, step)
            south = both(old.at[2], low - 1, step)
            level = []
            for k in range(2):
                value = old[0, k, here] - tw[k, here] * (east[k] - west[k] + north[k] - south[k])
                new[0, k, here] = value
                level.append(value)
            return level, east, north

        def move(low, held, beyond):
            here = slice(low, low + step)
            level, east, north = held
            level_e = shifted(level, -1)
            for k in range(2):
                level_n = roll(level[k], -1, 0)
                if beyond is not None:
                    first_row = jnp.broadcast_to(beyond[0][k][0:1], (step, CX))
                    level_n = jnp.where(bottom_row, first_row, level_n)
                new[1, k, here] = ae[k, here] * east[k] - be[k, here] * (level_e[k] - level[k]) + ce[k, here]
                new[2, k, here] = an[k, here] * north[k] - bn[k, here] * (level_n - level[k]) + cn[k, here]

        held = rise(LOW)
        for low in range(LOW, HIGH, step):
            coming = rise(low + step) if low + step < HIGH else None
            move(low, held, coming)
            held = coming

    def two(i, carry):
        substep(state, state_b)
        substep(state_b, state)
        return carry

    lax.fori_loop(0, NSUB // 2 - 1, two, 0)

    @pl.when(jnp.logical_not(outer))
    def _():
        got(outer_got, 208)
        remote(outer_in, outer_next, sent, div_got, member(partner)).start()

    two(0, 0)

    flow_rows = [(OWN - 8, 8)] + [(OWN + 32 * i, 32) for i in range(4)]
    for low, size in flow_rows:
        here = slice(low, low + size)
        shift_n = state[2, 0, here] - coupling * total[3, 0, here]
        for l in range(2):
            flow_n[l, here] = face_n[l, 0, here] * (x[4 + l, 0, here] + shift_n)
        prod_n[here] = shift_n

    for i in range(4):
        low = OWN + 32 * i
        here = slice(low, low + 32)
        mine = slice(32 * i, 32 * i + 32)
        shift_e = [state[1, k, here] - coupling * total[2, k, here] for k in range(2)]
        divs = []
        for l in range(2):
            flow = [face_e[l, k, here] * (x[2 + l, k, here] + shift_e[k]) for k in range(2)]
            west = shifted(flow, 1)[0]
            flow_e[l, 0, mine] = flow[0]
            flow_e[l, 1, mine] = west
            divs.append(flow[0] - west + flow_n[l, here] - flow_n[l, low - 1 : low + 31])
        div_1[mine] = divs[1]
        pair_send[mine] = divs[0] + divs[1]

    def divergence_of(parts, base):
        here = pl.ds(base, 64)
        shift_e = [state[1, k, here] - coupling * total[2, k, here] for k in range(2)]
        flow = parts[64:128] * shift_e[0]
        block = parts[200:208]
        column = jnp.concatenate([roll(block, -r, 1) for r in range(8)], axis=0)
        west = jnp.where(lanes(64) == 0, column * roll(shift_e[1], 1, 1), roll(flow, 1, 1))
        flow_t[0:72] = parts[128:200] * prod_n[pl.ds(base - 8, 72)]
        return parts[0:64] + flow - west + flow_t[8:72] - flow_t[7:71]

    @pl.when(jnp.logical_not(outer))
    def _():
        got(half_got, 416)
        outer_div[core] = divergence_of(outer_in, pl.multiple_of(OWN + 64 * core, 8))

    @pl.when(outer)
    def _():
        outer_div[...] = jnp.zeros_like(outer_div)

    for j in range(2):
        pair_div[64 * j : 64 * j + 64] = divergence_of(outer_pair.at[j], OWN + 64 * j)

    for low, size in flow_rows:
        here = slice(low, low + size)
        flow_w[here] = total[3, 0, here] + total[1, 0, here] * prod_n[here]

    for i in range(4):
        low = OWN + 32 * i
        here = slice(low, low + 32)
        mine = slice(32 * i, 32 * i + 32)
        shift_e = [state[1, k, here] - coupling * total[2, k, here] for k in range(2)]
        flow = [total[2, k, here] + total[0, k, here] * shift_e[k] for k in range(2)]
        whole_div[mine] = flow[0] - shifted(flow, 1)[0] + flow_w[here] - flow_w[low - 1 : low + 31]
        count = x[6, 0, here]
        for l in range(2):
            fe, fw = flow_e[l, 0, mine], flow_e[l, 1, mine]
            fn, fs = flow_n[l, here], flow_n[l, low - 1 : low + 31]
            gain = jnp.where(first + l < count, tracer_time / x[l, 0, here], 0.0)
            plus_e, minus_w = jnp.maximum(fe, 0.0), jnp.minimum(fw, 0.0)
            plus_n, minus_s = jnp.maximum(fn, 0.0), jnp.minimum(fs, 0.0)
            coef[l, 0, mine] = gain * (plus_e - fe)
            coef[l, 1, mine] = gain * (fw - minus_w)
            coef[l, 2, mine] = gain * (plus_n - fn)
            coef[l, 3, mine] = gain * (fs - minus_s)
            coef[l, 4, mine] = 1.0 - gain * (plus_e - minus_w + plus_n - minus_s)
            coef[l, 5, mine] = gain

    s_out[0] = state[0, 0, rows_own]
    e_out[0] = state[1, 0, rows_own]
    n_out[0] = state[2, 0, rows_own]

    lane32 = lanes(32)
    for l in range(2):
        for i in range(4):
            mine = slice(32 * i, 32 * i + 32)
            low = 8 + 32 * i
            a_e, a_w, a_n, a_s, a_c = (coef[l, j, mine] for j in range(5))
            for m in range(NTR):
                value = c[m, l, low : low + 32]
                edge = edge_c[m, l, mine]
                value_e = jnp.where(lane32 == CX - 1, edge, roll(value, -1, 1))
                value_w = jnp.where(lane32 == 0, edge, roll(value, 1, 1))
                part[m, l, mine] = (
                    a_c * value
                    + a_e * value_e
                    + a_w * value_w
                    + a_n * c[m, l, low + 1 : low + 33]
                    + a_s * c[m, l, low - 1 : low + 31]
                )

    halos_sent = [(inner, 272), (jnp.logical_not(inner), 200)]
    for where, rows in halos_sent:
        @pl.when(where & outer)
        def _(rows=rows):
            left(sent, rows + 896)

        @pl.when(where & jnp.logical_not(outer))
        def _(rows=rows):
            left(sent, rows + 1104)

    @pl.when(owner)
    def _():
        left(edge_sent, 10 * 8 * EB)

    @pl.when(jnp.logical_not(owner))
    def _():
        left(edge_sent, 4 * 8 * EB)

    @pl.when(outer)
    def _():
        left(outer_sent, 624)

    @pl.when(jnp.logical_not(outer))
    def _():
        left(outer_sent, 416)
        got(div_got, 208)
        outer_div[other] = divergence_of(outer_next, pl.multiple_of(OWN + 64 * other, 8))

    odd = core == 1
    for i in range(4):
        mine = slice(32 * i, 32 * i + 32)
        beyond = outer_div[i // 2, 32 * (i % 2) : 32 * (i % 2) + 32]
        near = pair_div[mine]
        here = pair_send[mine]
        deeper = jnp.where(
            upper,
            whole_div[mine] - here - beyond - jnp.where(odd, near, 0.0),
            beyond + jnp.where(odd, 0.0, near),
        )
        bottom = -deeper
        middle = -(div_1[mine] + deeper)
        top = jnp.where(me == 0, 0.0, -(here + deeper))
        for l in range(2):
            under_flow, over_flow = (middle, top) if l == 0 else (bottom, middle)
            gain = coef[l, 5, mine]
            lift[l, 0, mine] = gain * (jnp.minimum(under_flow, 0.0) - jnp.maximum(over_flow, 0.0))
            lift[l, 1, mine] = gain * jnp.maximum(under_flow, 0.0)
            lift[l, 2, mine] = -gain * jnp.minimum(over_flow, 0.0)

    @pl.when(me < ND - 1)
    def _():
        got(up_got, NTR * CY)
        left(down_sent, NTR * CY)

    @pl.when(me > 0)
    def _():
        got(down_got, NTR * CY)
        left(up_sent, NTR * CY)


def store(part, s_ref, e_ref, n_ref, c, below, above, lift, c_out, s_out, e_out, n_out, new_c, sem):
    copies = [
        pltpu.make_async_copy(source, target, sem.at[NTR + i])
        for i, (source, target) in enumerate([(s_ref, s_out), (e_ref, e_out), (n_ref, n_out)])
    ]
    for copy in copies:
        copy.start()
    for pair in range(0, NTR, 2):
        for l in range(2):
            for i in range(4):
                mine = slice(32 * i, 32 * i + 32)
                low = 8 + 32 * i
                a_c, a_b, a_a = (lift[l, j, mine] for j in range(3))
                for m in (pair, pair + 1):
                    under = c[m, 1, low : low + 32] if l == 0 else below[m, mine]
                    over = above[m, mine] if l == 0 else c[m, 0, low : low + 32]
                    new_c[m, l, mine] = (
                        part[m, l, mine] + a_c * c[m, l, low : low + 32] + a_b * under + a_a * over
                    )
        for m in (pair, pair + 1):
            copy = pltpu.make_async_copy(new_c.at[m], c_out.at[m, :, 0], sem.at[m])
            copy.start()
            copies.append(copy)
    for copy in copies:
        copy.wait()


def body(thickness, u_layer, v_layer, tracers, sea_level, u_column, v_column, wet_cells, levels):
    any_spec = pl.BlockSpec(memory_space=pl.ANY)
    near_spec = pl.BlockSpec(memory_space=pltpu.VMEM)

    def vmem(*shape):
        return pltpu.VMEM(shape, F32)

    plane = vmem(CY, CX)
    wide = vmem(2, RX, CX)
    wide2 = vmem(2, 2, RX, CX)
    column_c = vmem(NTR, CY, CX)
    flat = pltpu.VMEM((CY, CX), jnp.int32)
    quarter = vmem(4, 64, CX)
    halves = vmem(4, 2, 64, CX)
    edges = vmem(NE, 8 * EB, CX)
    dma = pltpu.SemaphoreType.DMA
    shapes = [tracers.shape] + [sea_level.shape] * 3
    results = pl.pallas_call(
        kernel,
        out_shape=(
            vmem(NTR, 2, CY, CX), *(pltpu.VMEM(shape, F32) for shape in shapes[1:]),
            vmem(NTR, 2, CY + 16, CX), column_c, column_c, vmem(2, 3, CY, CX),
        ),
        in_specs=[pl.BlockSpec(memory_space=pltpu.HBM)] * 9,
        out_specs=(near_spec,) * 8,
        scratch_shapes=[
            vmem(7, 2, RX, CX), vmem(3, 2, RX, CX), flat, flat,
            vmem(2, 2, 64, CX), vmem(2, 2, 64, CX), vmem(2, 2, 8, CX), vmem(4, 8, CX), vmem(11 * CY, CX),
            vmem(NTR, 2, CY, CX),
            halves, quarter, quarter, quarter, halves,
            edges, vmem(ND, 8 * EB, CX), edges,
            wide2, wide2, vmem(4, 2, RX, CX), vmem(4, 2, RX, CX),
            wide, wide, wide, wide, wide, wide, wide, wide, wide, vmem(3, 2, RX, CX),
            vmem(2, 208, CX), vmem(2, 208, CX), vmem(208, CX), vmem(208, CX), vmem(208, CX), vmem(2, 64, CX),
            vmem(2, RX, CX), vmem(RX, CX), vmem(RX, CX), vmem(2, 2, CY, CX), vmem(RX, CX), vmem(2, 6, CY, CX),
            plane, plane, plane, plane,
            dma((2,)), dma, dma, dma, dma, dma, dma,
            dma((2,)), dma, dma, dma, dma, dma, dma, dma, dma,
            dma, dma, dma,
        ],
        compiler_params=pltpu.CompilerParams(
            collective_id=0, has_side_effects=True, vmem_limit_bytes=48 * 1024 * 1024
        ),
    )(*[
        pltpu.with_memory_space_constraint(x, pltpu.HBM)
        for x in (thickness, u_layer, v_layer, tracers, sea_level, u_column, v_column, wet_cells, levels)
    ])
    return pl.pallas_call(
        store,
        out_shape=tuple(jax.ShapeDtypeStruct(shape, F32) for shape in shapes),
        in_specs=[near_spec] * 8,
        out_specs=(any_spec,) * 4,
        scratch_shapes=[vmem(NTR, 2, CY, CX), dma((NTR + 3,))],
    )(*[pltpu.with_memory_space_constraint(x, pltpu.VMEM) for x in results])


def solution(mesh):
    return jax.shard_map(
        body,
        mesh=mesh,
        in_specs=(
            P("depth", "tiles", None, None),
            P("depth", "tiles", None, None),
            P("depth", "tiles", None, None),
            P(None, "depth", "tiles", None, None),
            P("tiles", None, None),
            P("tiles", None, None),
            P("tiles", None, None),
            P("tiles", None, None),
            P("tiles", None, None),
        ),
        out_specs=(
            P(None, "depth", "tiles", None, None),
            P("tiles", None, None),
            P("tiles", None, None),
            P("tiles", None, None),
        ),
        check_vma=False,
    )
```

```python
import functools

import jax
import jax.numpy as jnp
from jax import lax
from jax.experimental import pallas as pl
from jax.experimental.pallas import tpu as pltpu
from jax.sharding import PartitionSpec as P

TROWS = 8
NSUB = 8
NTR = 6
ND = 8
NE = 4
EB = 5
CY = 128
CX = 128
RX = CY + 32
OWN = 16
END = OWN + CY
LOW = OWN - 8
HIGH = END + 8

tau = 0.45
coupling = 1.0 / 16
tracer_time = 0.1

MESH = pl.DeviceIdType.MESH
F32 = jnp.float32


def roll(x, shift, axis):
    shift = shift % x.shape[axis]
    return x if shift == 0 else pltpu.roll(x, shift, axis)


def lanes(rows, width=CX):
    return lax.broadcasted_iota(jnp.int32, (rows, width), 1)


def rows_of(rows, width=CX):
    return lax.broadcasted_iota(jnp.int32, (rows, width), 0)


def between(x, low, high):
    return (x >= low) & (x < high)


def kernel(
    h_in, u_in, v_in, c_in, sea_in, uc_in, vc_in, wet_in, lev_in,
    part, s_out, e_out, n_out, c, below, above, lift,
    x, state, wet, lev,
    side_pack, side_in, corner_pack, corner_in, sizes,
    edge_c,
    main_send, pair_in, chip_sum, main_in, main_all,
    edge_send, edge_in, edge_all,
    face_e, face_n, local, total,
    tw, ae, an, be, bn, ce, cn, wet_e_all, wet_n_all, state_b,
    outer_send, outer_pair, outer_sum, outer_in, outer_next, outer_div,
    flow_n, flow_t, flow_w, flow_e, prod_n, coef, div_1, whole_div, pair_send, pair_div,
    loc_sem, sent, sent_late, edge_sent, outer_sent, up_sent, down_sent,
    halo_got, pair_got, rs_got, ag_got, forward_got, edge_got, edge_all_got, half_got, outer_got,
    up_got, down_got, div_got,
):
    me = lax.axis_index("depth")
    tile = lax.axis_index("tiles")
    tx = tile // TROWS
    ty = tile % TROWS
    chip = me // 2
    core = me % 2
    other = 1 - core
    partner = 2 * chip + other
    upper = me < ND // 2
    outer = (me < 2) | (me >= ND - 2)
    cols = 8

    def tile_at(dx, dy):
        return ((tx + dx + cols) % cols) * TROWS + (ty + dy + TROWS) % TROWS

    def member(which):
        return {"tiles": tile, "depth": which}

    def beside(dx, dy):
        return {"tiles": tile_at(dx, dy), "depth": me}

    def remote(source, target, send, recv, where):
        return pltpu.make_async_remote_copy(
            src_ref=source, dst_ref=target, send_sem=send, recv_sem=recv,
            device_id=where, device_id_type=MESH,
        )

    has_n = ty < TROWS - 1
    has_s = ty > 0
    inner = has_n & has_s

    rows_own = slice(OWN, END)

    def got(sem, rows):
        remote(sizes.at[0:rows], sizes.at[0:rows], sem, sem, member(partner)).wait_recv()

    def left(sem, rows):
        remote(sizes.at[0:rows], sizes.at[0:rows], sem, sem, member(partner)).wait_send()

    def fetch(source, target):
        pltpu.make_async_copy(source, target, loc_sem.at[0]).start()

    barrier = pltpu.get_barrier_semaphore()

    def greet(dy):
        for dx in (1, -1) if dy == 0 else (0, 1, -1):
            pl.semaphore_signal(barrier, inc=1, device_id=beside(dx, dy), device_id_type=MESH)

    greet(0)

    @pl.when(has_n)
    def _():
        greet(1)

    @pl.when(has_s)
    def _():
        greet(-1)

    fetch(h_in.at[:, 0], x.at[0:2, 0, rows_own])
    fetch(wet_in.at[0], wet)
    fetch(lev_in.at[0], lev)
    fetch(u_in.at[:, 0], x.at[2:4, 0, rows_own])
    fetch(v_in.at[:, 0], x.at[4:6, 0, rows_own])
    fetch(sea_in.at[0], state.at[0, 0, rows_own])
    fetch(uc_in.at[0], state.at[1, 0, rows_own])
    fetch(vc_in.at[0], state.at[2, 0, rows_own])
    peers = [(me + k) % ND for k in range(1, ND)]
    for peer in peers:
        pl.semaphore_signal(barrier, inc=1, device_id=member(peer), device_id_type=MESH)
    fetch_c = pltpu.make_async_copy(c_in.at[:, :, 0], c.at[:, :, 8 : CY + 8], loc_sem.at[1])
    fetch_c.start()

    fetched = 11 * CY
    pltpu.make_async_copy(sizes.at[0:fetched], sizes.at[0:fetched], loc_sem.at[0]).wait()

    lane8 = lanes(8)
    x[6, 0, rows_own] = (wet[...] * lev[...]).astype(F32)

    def pack_sides(phase, fields, extra=None):
        for i in range(8):
            east = west = jnp.zeros((8, CX), F32)
            for j in range(2):
                low = OWN + 64 * j + 8 * i
                for f, ref in enumerate(fields):
                    turned = roll(ref[low : low + 8], 8 * f + 8 + 64 * j, 1)
                    start = 64 * j + 8 * f
                    west = jnp.where(between(lane8, start + 8, start + 16), turned, west)
                    east = jnp.where(between(lane8, start, start + 8), turned, east)
                if extra is not None:
                    east, west = extra(64 * j + 8 * i, 64 * j, east, west)
            side_pack[phase, 0, 8 * i : 8 * i + 8] = east
            side_pack[phase, 1, 8 * i : 8 * i + 8] = west

    early = [x.at[f, 0] for f in range(7)]
    late = [state.at[f, 0] for f in range(3)]
    pack_sides(0, early)

    for j, low in enumerate((OWN, END - 8)):
        east = west = jnp.zeros((8, CX), F32)
        for f, ref in enumerate(early + late):
            turned = roll(ref[low : low + 8], 8 * f + 8, 1)
            west = jnp.where(between(lane8, 8 * f + 8, 8 * f + 16), turned, west)
            east = jnp.where(between(lane8, 8 * f, 8 * f + 8), turned, east)
        corner_pack[0, j] = east
        corner_pack[1, j] = west

    first = (2 * me).astype(F32)
    lane16 = lanes(16)
    row16 = rows_of(16)

    def next_row(ref, p):
        low = OWN + 16 * p
        if p < ND - 1:
            return ref[low + 1 : low + 17]
        return jnp.where(row16 == 15, 0.0, roll(ref[low : low + 16], -1, 0))

    for p in range(ND):
        low = OWN + 16 * p
        here = slice(low, low + 16)
        count = x[6, 0, here]
        count_e = jnp.minimum(count, jnp.where(lane16 == CX - 1, 0.0, roll(count, -1, 1)))
        count_n = jnp.minimum(count, next_row(x.at[6, 0], p))
        sums = [0.0] * 4
        for l in range(2):
            thick = x[l, 0, here]
            de = jnp.where(first + l < count_e, 0.5 * (thick + roll(thick, -1, 1)), 0.0)
            dn = jnp.where(first + l < count_n, 0.5 * (thick + next_row(x.at[l, 0], p)), 0.0)
            new = [de, dn, x[2 + l, 0, here] * de, x[4 + l, 0, here] * dn]
            sums = [a + b for a, b in zip(sums, new)]
        for f in range(4):
            main_send[p // 2, p % 2, 16 * f : 16 * f + 16] = sums[f]

    @pl.when(inner)
    def _():
        pl.semaphore_wait(barrier, 8 + ND - 1)

    @pl.when(jnp.logical_not(inner))
    def _():
        pl.semaphore_wait(barrier, 5 + ND - 1)

    def halo(phase, source, target, dx, dy):
        sem = sent if phase == 0 else sent_late
        remote(source, target, sem, halo_got.at[phase], beside(dx, dy)).start()

    halo(0, side_pack.at[0, 0], side_in.at[0, 0], 1, 0)
    halo(0, side_pack.at[0, 1], side_in.at[0, 1], -1, 0)

    @pl.when(has_n)
    def _():
        halo(0, corner_pack.at[0, 1], corner_in.at[0], 1, 1)
        halo(0, corner_pack.at[1, 1], corner_in.at[1], -1, 1)
        halo(0, x.at[:, 0, END - 8 : END], x.at[:, 0, LOW:OWN], 0, 1)

    @pl.when(has_s)
    def _():
        halo(0, corner_pack.at[0, 0], corner_in.at[2], 1, -1)
        halo(0, corner_pack.at[1, 0], corner_in.at[3], -1, -1)
        halo(0, x.at[:, 0, OWN : OWN + 8], x.at[:, 0, END:HIGH], 0, -1)

    remote(main_send.at[:, other], pair_in, sent, pair_got, member(partner)).start()

    fetch_c.wait()
    rows_c = slice(8, CY + 8)

    def send_tracers(i):
        part = (slice(0, 3), slice(3, 4), slice(4, NTR))[i]

        @pl.when(me > 0)
        def _():
            remote(
                c.at[part, 0, rows_c], below.at[part], up_sent, up_got, member((me + ND - 1) % ND)
            ).start()

        @pl.when(me < ND - 1)
        def _():
            remote(
                c.at[part, 1, rows_c], above.at[part], down_sent, down_got, member((me + 1) % ND)
            ).start()

    send_tracers(0)

    got(pair_got, 256)
    chips = [(chip + k) % 4 for k in (2, 1, 3)]
    far_first = [(me + k) % ND for k in (4, 5, 3, 2, 6, 7, 1)]
    for q in range(4):
        chip_sum[q] = main_send[q, core] + pair_in[q]
    for q in chips:
        remote(chip_sum.at[q], main_in.at[chip], sent, rs_got, member(2 * q + core)).start()

    send_tracers(1)

    def pack_more(low, shift, east, west):
        old = state[1, 0, OWN + low : OWN + low + 8]
        east = jnp.where(between(lane8, shift + 24, shift + 32), roll(old, 40 + shift, 1), east)
        for p in range(2 * NTR):
            plane = c[p // 2, p % 2, 8 + low : 16 + low]
            west = jnp.where(lane8 == shift + 48 + p, roll(plane, shift + 48 + p, 1), west)
            east = jnp.where(lane8 == shift + 49 + p, roll(plane, shift + 50 + p, 1), east)
        return east, west

    pack_sides(1, late, pack_more)

    halo(1, side_pack.at[1, 0], side_in.at[1, 0], 1, 0)
    halo(1, side_pack.at[1, 1], side_in.at[1, 1], -1, 0)

    @pl.when(has_n)
    def _():
        halo(1, state.at[:, 0, END - 16 : END], state.at[:, 0, 0:OWN], 0, 1)
        halo(1, c.at[:, :, CY : CY + 8], c.at[:, :, 0:8], 0, 1)

    @pl.when(has_s)
    def _():
        halo(1, state.at[:, 0, OWN : OWN + 8], state.at[:, 0, END:HIGH], 0, -1)
        halo(1, c.at[:, :, 8:16], c.at[:, :, CY + 8 : CY + 16], 0, -1)

    @pl.when(me == 0)
    def _():
        above[...] = jnp.zeros_like(above)

    @pl.when(me == ND - 1)
    def _():
        below[...] = jnp.zeros_like(below)

    for ref in (x, state):
        for k in range(2):
            ref[:, k, HIGH:RX] = jnp.zeros((ref.shape[0], RX - HIGH, CX), F32)
    state[2, 1, 0:LOW] = jnp.zeros((LOW, CX), F32)
    state_b[2, :, 0:LOW] = jnp.zeros((2, LOW, CX), F32)

    def unpack_sides(phase, fields, extra=None):
        side = (lane8 < 8) | (lane8 >= CX - 8)
        for i in range(-1, 17):
            if i < 0:
                west, east, shift, ok = corner_in[0], corner_in[1], 56 * phase, side & has_s
            elif i == 16:
                west, east, shift, ok = corner_in[2], corner_in[3], 56 * phase, side & has_n
            else:
                j = 8 * (i % 8)
                west, east = side_in[phase, 0, j : j + 8], side_in[phase, 1, j : j + 8]
                shift, ok = 64 * (i // 8), side
            low = OWN + 8 * i
            for f, ref in enumerate(fields):
                start = shift + 8 * f + 8
                value = roll(jnp.where(between(lane8, start, start + 8), east, west), -start, 1)
                value = jnp.where(ok, value, 0.0)
                if extra is not None and f == 1 and 0 <= i < 16:
                    value = jnp.where(lane8 == CX - 9, roll(west, 88 - shift, 1), value)
                ref[low : low + 8] = value
            if extra is not None and 0 <= i < 16:
                extra(8 * i, shift, west, east)

    @pl.when(inner)
    def _():
        got(halo_got.at[0], 272)

    @pl.when(jnp.logical_not(inner))
    def _():
        got(halo_got.at[0], 200)

    unpack_sides(0, [x.at[f, 1] for f in range(7)])

    @pl.when(jnp.logical_not(has_s))
    def _():
        x[:, 0, LOW:OWN] = jnp.zeros((7, 8, CX), F32)

    @pl.when(jnp.logical_not(has_n))
    def _():
        x[:, 0, END:HIGH] = jnp.zeros((7, 8, CX), F32)

    def shifted(pair, steps):
        lane = lanes(pair[0].shape[0])
        edge = lane == (0 if steps > 0 else CX - 1)
        main, side = (roll(value, steps, 1) for value in pair)
        return jnp.where(edge, side, main), jnp.where(edge, main, side)

    def both(ref, low, size):
        return ref[0, low : low + size], ref[1, low : low + size]

    step = 24
    for low in range(LOW, HIGH, step):
        here = slice(low, low + step)
        count = both(x.at[6], low, step)
        count_e = shifted(count, -1)
        count_n = both(x.at[6], low + 1, step)
        thick = [both(x.at[l], low, step) for l in range(2)]
        thick_e = [shifted(thick[l], -1) for l in range(2)]
        for k in range(2):
            min_e = jnp.minimum(count[k], count_e[k])
            min_n = jnp.minimum(count[k], count_n[k])
            sums = [0.0] * 4
            for l in range(2):
                north = x[l, k, low + 1 : low + 1 + step]
                de = jnp.where(first + l < min_e, 0.5 * (thick[l][k] + thick_e[l][k]), 0.0)
                dn = jnp.where(first + l < min_n, 0.5 * (thick[l][k] + north), 0.0)
                face_e[l, k, here] = de
                face_n[l, k, here] = dn
                new = [de, dn, x[2 + l, k, here] * de, x[4 + l, k, here] * dn]
                sums = [a + b for a, b in zip(sums, new)]
            for f in range(4):
                local[f, k, here] = sums[f]

    def put_block(i, block):
        edge_send[i // EB, 8 * (i % EB) : 8 * (i % EB) + 8] = block

    for i in range(9):
        block = jnp.zeros((8, CX), F32)
        for j in range(2):
            low = LOW + 72 * j + 8 * i
            for f in range(4):
                start = 64 * j + 16 * f
                block = jnp.where(
                    lane8 == start, roll(local[f, 0, low : low + 8], start + 1, 1), block
                )
                block = jnp.where(
                    between(lane8, start + 1, start + 16),
                    roll(local[f, 1, low : low + 8], start + 9, 1),
                    block,
                )
        put_block(i, block)
    for f in range(4):
        put_block(9 + f, local[f, 0, END - 1 : END + 7])
        put_block(13 + f, local[f, 0, LOW:OWN])
    for i in range(17, NE * EB):
        put_block(i, jnp.zeros((8, CX), F32))

    owner = core == 0

    @pl.when(owner)
    def _():
        for q in chips:
            remote(edge_send.at[q], edge_in.at[me], edge_sent, edge_got, member(2 * q)).start()

    @pl.when(jnp.logical_not(owner))
    def _():
        for q in chips + [chip]:
            remote(edge_send.at[q], edge_in.at[me], edge_sent, edge_got, member(2 * q)).start()

    got(rs_got, 192)
    mine = chip_sum[chip]
    for q in chips:
        mine = mine + main_in[q]
    main_all[chip, core] = mine
    piece = main_all.at[chip, core]
    for q in chips:
        remote(piece, piece, sent, ag_got, member(2 * q + core)).start()

    for i in range(4):
        low = OWN + 32 * i
        here = slice(low, low + 32)
        flux = both(local.at[2], low, 32)
        value = flux[0] - shifted(flux, 1)[0] + local[3, 0, here] - local[3, 0, low - 1 : low + 31]
        outer_send[i // 2, 32 * (i % 2) : 32 * (i % 2) + 32] = value
    for j in range(2):
        low = OWN + 64 * j
        outer_send[j, 64:128] = local[0, 0, low : low + 64]
        outer_send[j, 128:200] = local[1, 0, low - 8 : low + 64]
        block = jnp.zeros((8, CX), F32)
        for r in range(8):
            turned = roll(local[0, 1, low + 8 * r : low + 8 * r + 8], r + 1, 1)
            block = jnp.where(lane8 == r, turned, block)
        outer_send[j, 200:208] = block
    remote(outer_send, outer_pair, outer_sent, half_got, member(partner)).start()

    @pl.when(owner)
    def _():
        got(edge_got, 7 * 8 * EB)
        edge = edge_send[chip]
        for peer in peers:
            edge = edge + edge_in[peer]
        edge_all[chip] = edge
        for peer in far_first:
            remote(edge_all.at[chip], edge_all.at[chip], edge_sent, edge_all_got, member(peer)).start()

    @pl.when(outer)
    def _():
        got(half_got, 416)
        outer_sum[...] = outer_send[core] + outer_pair[core]
        middle_chip = jnp.where(upper, 2, ND - 4)
        remote(outer_sum, outer_in, outer_sent, outer_got, member(middle_chip + core)).start()

    send_tracers(2)

    @pl.when(inner)
    def _():
        got(halo_got.at[1], 392)
        left(sent_late, 392)

    @pl.when(jnp.logical_not(has_s))
    def _():
        got(halo_got.at[1], 248)
        left(sent_late, 272)

    @pl.when(jnp.logical_not(has_n))
    def _():
        got(halo_got.at[1], 272)
        left(sent_late, 248)


    def put_tracers(low, shift, west, east):
        for p in range(2 * NTR):
            value = jnp.where(lane8 <= shift + 48 + p, east, west)
            edge_c[p // 2, p % 2, low : low + 8] = roll(value, 79 - shift - p, 1)

    unpack_sides(1, [state.at[f, 1] for f in range(3)], put_tracers)

    @pl.when(jnp.logical_not(has_s))
    def _():
        state[:, 0, 0:OWN] = jnp.zeros((3, OWN, CX), F32)
        c[:, :, 0:8] = jnp.zeros((NTR, 2, 8, CX), F32)

    @pl.when(jnp.logical_not(has_n))
    def _():
        state[:, 0, END:HIGH] = jnp.zeros((3, 8, CX), F32)
        c[:, :, CY + 8 : CY + 16] = jnp.zeros((NTR, 2, 8, CX), F32)

    for low in range(LOW, HIGH, step):
        here = slice(low, low + step)
        is_wet = [jnp.where(value > 0.0, 1.0, 0.0) for value in both(x.at[6], low, step)]
        wet_e = shifted(is_wet, -1)
        wet_n = [jnp.where(value > 0.0, 1.0, 0.0) for value in both(x.at[6], low + 1, step)]
        for k in range(2):
            tw[k, here] = tau * is_wet[k]
            ae[k, here] = (1.0 - tau) * (is_wet[k] * wet_e[k])
            an[k, here] = (1.0 - tau) * (is_wet[k] * wet_n[k])
            wet_e_all[k, here] = (tau * coupling) * (is_wet[k] * wet_e[k])
            wet_n_all[k, here] = (tau * coupling) * (is_wet[k] * wet_n[k])

    got(ag_got, 192)
    half = main_all.at[:, core]
    remote(half, half, sent, forward_got, member(partner)).start()

    @pl.when(owner)
    def _():
        got(edge_all_got, 3 * 8 * EB)

    @pl.when(jnp.logical_not(owner))
    def _():
        got(edge_all_got, 4 * 8 * EB)

    got(forward_got, 256)

    def block_of(i):
        return edge_all[i // EB, 8 * (i % EB) : 8 * (i % EB) + 8]

    rim = (lane8 < 7) | (lane8 >= CX - 8)
    last_lane = lane8 == CX - 1
    row8 = rows_of(8)
    for i in range(18):
        block = block_of(i % 9)
        shift = 64 * (i // 9)
        here = slice(LOW + 8 * i, LOW + 8 * i + 8)
        sums = []
        for f in range(4):
            if i == 0:
                main = block_of(13 + f)
            elif i == 17:
                main = jnp.where(row8 == 7, 0.0, roll(block_of(9 + f), -1, 0))
            else:
                p, part_low = (i - 1) // 2, 16 * f + 8 * ((i - 1) % 2)
                main = main_all[p // 2, p % 2, part_low : part_low + 8]
                if i == 16:
                    main = jnp.where(row8 == 7, jnp.broadcast_to(block_of(9 + f)[0:1], (8, CX)), main)
            main = jnp.where(last_lane, roll(block, CX - 1 - 16 * f - shift, 1), main)
            side = jnp.where(rim, roll(block, -(9 + 16 * f + shift), 1), 0.0)
            total[f, 0, here] = main
            total[f, 1, here] = side
            sums.append((main, side))
        for k in range(2):
            east, north = wet_e_all[k, here], wet_n_all[k, here]
            be[k, here] = east * sums[0][k]
            bn[k, here] = north * sums[1][k]
            ce[k, here] = east * sums[2][k]
            cn[k, here] = north * sums[3][k]

    def substep(old, new):
        bottom_row = rows_of(step) == step - 1

        def rise(low):
            here = slice(low, low + step)
            east = both(old.at[1], low, step)
            west = shifted(east, 1)
            north = both(old.at[2], low, step)
            south = both(old.at[2], low - 1, step)
            level = []
            for k in range(2):
                value = old[0, k, here] - tw[k, here] * (east[k] - west[k] + north[k] - south[k])
                new[0, k, here] = value
                level.append(value)
            return level, east, north

        def move(low, held, beyond):
            here = slice(low, low + step)
            level, east, north = held
            level_e = shifted(level, -1)
            for k in range(2):
                level_n = roll(level[k], -1, 0)
                if beyond is not None:
                    first_row = jnp.broadcast_to(beyond[0][k][0:1], (step, CX))
                    level_n = jnp.where(bottom_row, first_row, level_n)
                new[1, k, here] = ae[k, here] * east[k] - be[k, here] * (level_e[k] - level[k]) + ce[k, here]
                new[2, k, here] = an[k, here] * north[k] - bn[k, here] * (level_n - level[k]) + cn[k, here]

        held = rise(LOW)
        for low in range(LOW, HIGH, step):
            coming = rise(low + step) if low + step < HIGH else None
            move(low, held, coming)
            held = coming

    def two(i, carry):
        substep(state, state_b)
        substep(state_b, state)
        return carry

    lax.fori_loop(0, NSUB // 2 - 1, two, 0)

    @pl.when(jnp.logical_not(outer))
    def _():
        got(outer_got, 208)
        remote(outer_in, outer_next, sent, div_got, member(partner)).start()

    two(0, 0)

    flow_rows = [(OWN - 8, 8)] + [(OWN + 32 * i, 32) for i in range(4)]
    for low, size in flow_rows:
        here = slice(low, low + size)
        shift_n = state[2, 0, here] - coupling * total[3, 0, here]
        for l in range(2):
            flow_n[l, here] = face_n[l, 0, here] * (x[4 + l, 0, here] + shift_n)
        prod_n[here] = shift_n

    for i in range(4):
        low = OWN + 32 * i
        here = slice(low, low + 32)
        mine = slice(32 * i, 32 * i + 32)
        shift_e = [state[1, k, here] - coupling * total[2, k, here] for k in range(2)]
        divs = []
        for l in range(2):
            flow = [face_e[l, k, here] * (x[2 + l, k, here] + shift_e[k]) for k in range(2)]
            west = shifted(flow, 1)[0]
            flow_e[l, 0, mine] = flow[0]
            flow_e[l, 1, mine] = west
            divs.append(flow[0] - west + flow_n[l, here] - flow_n[l, low - 1 : low + 31])
        div_1[mine] = divs[1]
        pair_send[mine] = divs[0] + divs[1]

    def divergence_of(parts, base):
        here = pl.ds(base, 64)
        shift_e = [state[1, k, here] - coupling * total[2, k, here] for k in range(2)]
        flow = parts[64:128] * shift_e[0]
        block = parts[200:208]
        column = jnp.concatenate([roll(block, -r, 1) for r in range(8)], axis=0)
        west = jnp.where(lanes(64) == 0, column * roll(shift_e[1], 1, 1), roll(flow, 1, 1))
        flow_t[0:72] = parts[128:200] * prod_n[pl.ds(base - 8, 72)]
        return parts[0:64] + flow - west + flow_t[8:72] - flow_t[7:71]

    @pl.when(jnp.logical_not(outer))
    def _():
        got(half_got, 416)
        outer_div[core] = divergence_of(outer_in, pl.multiple_of(OWN + 64 * core, 8))

    @pl.when(outer)
    def _():
        outer_div[...] = jnp.zeros_like(outer_div)

    for j in range(2):
        pair_div[64 * j : 64 * j + 64] = divergence_of(outer_pair.at[j], OWN + 64 * j)

    for low, size in flow_rows:
        here = slice(low, low + size)
        flow_w[here] = total[3, 0, here] + total[1, 0, here] * prod_n[here]

    for i in range(4):
        low = OWN + 32 * i
        here = slice(low, low + 32)
        mine = slice(32 * i, 32 * i + 32)
        shift_e = [state[1, k, here] - coupling * total[2, k, here] for k in range(2)]
        flow = [total[2, k, here] + total[0, k, here] * shift_e[k] for k in range(2)]
        whole_div[mine] = flow[0] - shifted(flow, 1)[0] + flow_w[here] - flow_w[low - 1 : low + 31]
        count = x[6, 0, here]
        for l in range(2):
            fe, fw = flow_e[l, 0, mine], flow_e[l, 1, mine]
            fn, fs = flow_n[l, here], flow_n[l, low - 1 : low + 31]
            gain = jnp.where(first + l < count, tracer_time / x[l, 0, here], 0.0)
            plus_e, minus_w = jnp.maximum(fe, 0.0), jnp.minimum(fw, 0.0)
            plus_n, minus_s = jnp.maximum(fn, 0.0), jnp.minimum(fs, 0.0)
            coef[l, 0, mine] = gain * (plus_e - fe)
            coef[l, 1, mine] = gain * (fw - minus_w)
            coef[l, 2, mine] = gain * (plus_n - fn)
            coef[l, 3, mine] = gain * (fs - minus_s)
            coef[l, 4, mine] = 1.0 - gain * (plus_e - minus_w + plus_n - minus_s)
            coef[l, 5, mine] = gain

    s_out[0] = state[0, 0, rows_own]
    e_out[0] = state[1, 0, rows_own]
    n_out[0] = state[2, 0, rows_own]

    lane32 = lanes(32)
    for l in range(2):
        for i in range(4):
            mine = slice(32 * i, 32 * i + 32)
            low = 8 + 32 * i
            a_e, a_w, a_n, a_s, a_c = (coef[l, j, mine] for j in range(5))
            for m in range(NTR):
                value = c[m, l, low : low + 32]
                edge = edge_c[m, l, mine]
                value_e = jnp.where(lane32 == CX - 1, edge, roll(value, -1, 1))
                value_w = jnp.where(lane32 == 0, edge, roll(value, 1, 1))
                part[m, l, mine] = (
                    a_c * value
                    + a_e * value_e
                    + a_w * value_w
                    + a_n * c[m, l, low + 1 : low + 33]
                    + a_s * c[m, l, low - 1 : low + 31]
                )

    halos_sent = [(inner, 272), (jnp.logical_not(inner), 200)]
    for where, rows in halos_sent:
        @pl.when(where & outer)
        def _(rows=rows):
            left(sent, rows + 896)

        @pl.when(where & jnp.logical_not(outer))
        def _(rows=rows):
            left(sent, rows + 1104)

    @pl.when(owner)
    def _():
        left(edge_sent, 10 * 8 * EB)

    @pl.when(jnp.logical_not(owner))
    def _():
        left(edge_sent, 4 * 8 * EB)

    @pl.when(outer)
    def _():
        left(outer_sent, 624)

    @pl.when(jnp.logical_not(outer))
    def _():
        left(outer_sent, 416)
        got(div_got, 208)
        outer_div[other] = divergence_of(outer_next, pl.multiple_of(OWN + 64 * other, 8))

    odd = core == 1
    for i in range(4):
        mine = slice(32 * i, 32 * i + 32)
        beyond = outer_div[i // 2, 32 * (i % 2) : 32 * (i % 2) + 32]
        near = pair_div[mine]
        here = pair_send[mine]
        deeper = jnp.where(
            upper,
            whole_div[mine] - here - beyond - jnp.where(odd, near, 0.0),
            beyond + jnp.where(odd, 0.0, near),
        )
        bottom = -deeper
        middle = -(div_1[mine] + deeper)
        top = jnp.where(me == 0, 0.0, -(here + deeper))
        for l in range(2):
            under_flow, over_flow = (middle, top) if l == 0 else (bottom, middle)
            gain = coef[l, 5, mine]
            lift[l, 0, mine] = gain * (jnp.minimum(under_flow, 0.0) - jnp.maximum(over_flow, 0.0))
            lift[l, 1, mine] = gain * jnp.maximum(under_flow, 0.0)
            lift[l, 2, mine] = -gain * jnp.minimum(over_flow, 0.0)

    @pl.when(me < ND - 1)
    def _():
        got(up_got, NTR * CY)
        left(down_sent, NTR * CY)

    @pl.when(me > 0)
    def _():
        got(down_got, NTR * CY)
        left(up_sent, NTR * CY)


def store(part, s_ref, e_ref, n_ref, c, below, above, lift, c_out, s_out, e_out, n_out, new_c, sem):
    copies = [
        pltpu.make_async_copy(source, target, sem.at[NTR + i])
        for i, (source, target) in enumerate([(s_ref, s_out), (e_ref, e_out), (n_ref, n_out)])
    ]
    for copy in copies:
        copy.start()
    for pair in range(0, NTR, 2):
        for l in range(2):
            for i in range(4):
                mine = slice(32 * i, 32 * i + 32)
                low = 8 + 32 * i
                a_c, a_b, a_a = (lift[l, j, mine] for j in range(3))
                for m in (pair, pair + 1):
                    under = c[m, 1, low : low + 32] if l == 0 else below[m, mine]
                    over = above[m, mine] if l == 0 else c[m, 0, low : low + 32]
                    new_c[m, l, mine] = (
                        part[m, l, mine] + a_c * c[m, l, low : low + 32] + a_b * under + a_a * over
                    )
        for m in (pair, pair + 1):
            copy = pltpu.make_async_copy(new_c.at[m], c_out.at[m, :, 0], sem.at[m])
            copy.start()
            copies.append(copy)
    for copy in copies:
        copy.wait()


def body(thickness, u_layer, v_layer, tracers, sea_level, u_column, v_column, wet_cells, levels):
    any_spec = pl.BlockSpec(memory_space=pl.ANY)
    near_spec = pl.BlockSpec(memory_space=pltpu.VMEM)

    def vmem(*shape):
        return pltpu.VMEM(shape, F32)

    plane = vmem(CY, CX)
    wide = vmem(2, RX, CX)
    wide2 = vmem(2, 2, RX, CX)
    column_c = vmem(NTR, CY, CX)
    flat = pltpu.VMEM((CY, CX), jnp.int32)
    quarter = vmem(4, 64, CX)
    halves = vmem(4, 2, 64, CX)
    edges = vmem(NE, 8 * EB, CX)
    dma = pltpu.SemaphoreType.DMA
    shapes = [tracers.shape] + [sea_level.shape] * 3
    results = pl.pallas_call(
        kernel,
        out_shape=(
            vmem(NTR, 2, CY, CX), *(pltpu.VMEM(shape, F32) for shape in shapes[1:]),
            vmem(NTR, 2, CY + 16, CX), column_c, column_c, vmem(2, 3, CY, CX),
        ),
        in_specs=[pl.BlockSpec(memory_space=pltpu.HBM)] * 9,
        out_specs=(near_spec,) * 8,
        scratch_shapes=[
            vmem(7, 2, RX, CX), vmem(3, 2, RX, CX), flat, flat,
            vmem(2, 2, 64, CX), vmem(2, 2, 64, CX), vmem(2, 2, 8, CX), vmem(4, 8, CX), vmem(11 * CY, CX),
            vmem(NTR, 2, CY, CX),
            halves, quarter, quarter, quarter, halves,
            edges, vmem(ND, 8 * EB, CX), edges,
            wide2, wide2, vmem(4, 2, RX, CX), vmem(4, 2, RX, CX),
            wide, wide, wide, wide, wide, wide, wide, wide, wide, vmem(3, 2, RX, CX),
            vmem(2, 208, CX), vmem(2, 208, CX), vmem(208, CX), vmem(208, CX), vmem(208, CX), vmem(2, 64, CX),
            vmem(2, RX, CX), vmem(RX, CX), vmem(RX, CX), vmem(2, 2, CY, CX), vmem(RX, CX), vmem(2, 6, CY, CX),
            plane, plane, plane, plane,
            dma((2,)), dma, dma, dma, dma, dma, dma,
            dma((2,)), dma, dma, dma, dma, dma, dma, dma, dma,
            dma, dma, dma,
        ],
        compiler_params=pltpu.CompilerParams(
            collective_id=0, has_side_effects=True, vmem_limit_bytes=48 * 1024 * 1024
        ),
    )(*[
        pltpu.with_memory_space_constraint(x, pltpu.HBM)
        for x in (thickness, u_layer, v_layer, tracers, sea_level, u_column, v_column, wet_cells, levels)
    ])
    return pl.pallas_call(
        store,
        out_shape=tuple(jax.ShapeDtypeStruct(shape, F32) for shape in shapes),
        in_specs=[near_spec] * 8,
        out_specs=(any_spec,) * 4,
        scratch_shapes=[vmem(NTR, 2, CY, CX), dma((NTR + 3,))],
    )(*[pltpu.with_memory_space_constraint(x, pltpu.VMEM) for x in results])


def solution(mesh):
    return jax.shard_map(
        body,
        mesh=mesh,
        in_specs=(
            P("depth", "tiles", None, None),
            P("depth", "tiles", None, None),
            P("depth", "tiles", None, None),
            P(None, "depth", "tiles", None, None),
            P("tiles", None, None),
            P("tiles", None, None),
            P("tiles", None, None),
            P("tiles", None, None),
            P("tiles", None, None),
        ),
        out_specs=(
            P(None, "depth", "tiles", None, None),
            P("tiles", None, None),
            P("tiles", None, None),
            P("tiles", None, None),
        ),
        check_vma=False,
    )
```

```python
import functools

import jax
import jax.numpy as jnp
from jax import lax
from jax.experimental import pallas as pl
from jax.experimental.pallas import tpu as pltpu
from jax.sharding import PartitionSpec as P

TROWS = 8
NSUB = 8
NTR = 6
ND = 8
NE = 4
EB = 5
CY = 128
CX = 128
RX = CY + 32
OWN = 16
END = OWN + CY
LOW = OWN - 8
HIGH = END + 8

tau = 0.45
coupling = 1.0 / 16
tracer_time = 0.1

MESH = pl.DeviceIdType.MESH
F32 = jnp.float32


def roll(x, shift, axis):
    shift = shift % x.shape[axis]
    return x if shift == 0 else pltpu.roll(x, shift, axis)


def lanes(rows, width=CX):
    return lax.broadcasted_iota(jnp.int32, (rows, width), 1)


def rows_of(rows, width=CX):
    return lax.broadcasted_iota(jnp.int32, (rows, width), 0)


def between(x, low, high):
    return (x >= low) & (x < high)


def kernel(
    h_in, u_in, v_in, c_in, sea_in, uc_in, vc_in, wet_in, lev_in,
    part, s_out, e_out, n_out, c, below, above, lift,
    x, state, wet, lev,
    side_pack, side_in, corner_pack, corner_in, sizes,
    edge_c,
    main_send, pair_in, chip_sum, main_in, main_all,
    edge_send, edge_in, edge_all,
    face_e, face_n, local, total,
    tw, ae, an, be, bn, ce, cn, wet_e_all, wet_n_all, state_b,
    outer_send, outer_pair, outer_sum, outer_in, outer_next, outer_div,
    flow_n, flow_t, flow_w, flow_e, prod_n, coef, div_1, whole_div, pair_send, pair_div,
    loc_sem, sent, sent_late, edge_sent, outer_sent, up_sent, down_sent,
    halo_got, pair_got, rs_got, ag_got, forward_got, edge_got, edge_all_got, half_got, outer_got,
    up_got, down_got, div_got,
):
    me = lax.axis_index("depth")
    tile = lax.axis_index("tiles")
    tx = tile // TROWS
    ty = tile % TROWS
    chip = me // 2
    core = me % 2
    other = 1 - core
    partner = 2 * chip + other
    upper = me < ND // 2
    outer = (me < 2) | (me >= ND - 2)
    cols = 8

    def tile_at(dx, dy):
        return ((tx + dx + cols) % cols) * TROWS + (ty + dy + TROWS) % TROWS

    def member(which):
        return {"tiles": tile, "depth": which}

    def beside(dx, dy):
        return {"tiles": tile_at(dx, dy), "depth": me}

    def remote(source, target, send, recv, where):
        return pltpu.make_async_remote_copy(
            src_ref=source, dst_ref=target, send_sem=send, recv_sem=recv,
            device_id=where, device_id_type=MESH,
        )

    has_n = ty < TROWS - 1
    has_s = ty > 0
    inner = has_n & has_s

    rows_own = slice(OWN, END)

    def got(sem, rows):
        remote(sizes.at[0:rows], sizes.at[0:rows], sem, sem, member(partner)).wait_recv()

    def left(sem, rows):
        remote(sizes.at[0:rows], sizes.at[0:rows], sem, sem, member(partner)).wait_send()

    def fetch(source, target):
        pltpu.make_async_copy(source, target, loc_sem.at[0]).start()

    barrier = pltpu.get_barrier_semaphore()

    def greet(dy):
        for dx in (1, -1) if dy == 0 else (0, 1, -1):
            pl.semaphore_signal(barrier, inc=1, device_id=beside(dx, dy), device_id_type=MESH)

    greet(0)

    @pl.when(has_n)
    def _():
        greet(1)

    @pl.when(has_s)
    def _():
        greet(-1)

    fetch(h_in.at[:, 0], x.at[0:2, 0, rows_own])
    fetch(wet_in.at[0], wet)
    fetch(lev_in.at[0], lev)
    fetch(u_in.at[:, 0], x.at[2:4, 0, rows_own])
    fetch(v_in.at[:, 0], x.at[4:6, 0, rows_own])
    fetch(sea_in.at[0], state.at[0, 0, rows_own])
    fetch(uc_in.at[0], state.at[1, 0, rows_own])
    fetch(vc_in.at[0], state.at[2, 0, rows_own])
    peers = [(me + k) % ND for k in range(1, ND)]
    for peer in peers:
        pl.semaphore_signal(barrier, inc=1, device_id=member(peer), device_id_type=MESH)
    fetch_c = pltpu.make_async_copy(c_in.at[:, :, 0], c.at[:, :, 8 : CY + 8], loc_sem.at[1])
    fetch_c.start()

    fetched = 11 * CY
    pltpu.make_async_copy(sizes.at[0:fetched], sizes.at[0:fetched], loc_sem.at[0]).wait()

    lane8 = lanes(8)
    x[6, 0, rows_own] = (wet[...] * lev[...]).astype(F32)

    def pack_sides(phase, fields, extra=None):
        for i in range(8):
            east = west = jnp.zeros((8, CX), F32)
            for j in range(2):
                low = OWN + 64 * j + 8 * i
                for f, ref in enumerate(fields):
                    turned = roll(ref[low : low + 8], 8 * f + 8 + 64 * j, 1)
                    start = 64 * j + 8 * f
                    west = jnp.where(between(lane8, start + 8, start + 16), turned, west)
                    east = jnp.where(between(lane8, start, start + 8), turned, east)
                if extra is not None:
                    east, west = extra(64 * j + 8 * i, 64 * j, east, west)
            side_pack[phase, 0, 8 * i : 8 * i + 8] = east
            side_pack[phase, 1, 8 * i : 8 * i + 8] = west

    early = [x.at[f, 0] for f in range(7)]
    late = [state.at[f, 0] for f in range(3)]
    pack_sides(0, early)

    for j, low in enumerate((OWN, END - 8)):
        east = west = jnp.zeros((8, CX), F32)
        for f, ref in enumerate(early + late):
            turned = roll(ref[low : low + 8], 8 * f + 8, 1)
            west = jnp.where(between(lane8, 8 * f + 8, 8 * f + 16), turned, west)
            east = jnp.where(between(lane8, 8 * f, 8 * f + 8), turned, east)
        corner_pack[0, j] = east
        corner_pack[1, j] = west

    first = (2 * me).astype(F32)
    lane16 = lanes(16)
    row16 = rows_of(16)

    def next_row(ref, p):
        low = OWN + 16 * p
        if p < ND - 1:
            return ref[low + 1 : low + 17]
        return jnp.where(row16 == 15, 0.0, roll(ref[low : low + 16], -1, 0))

    for p in range(ND):
        low = OWN + 16 * p
        here = slice(low, low + 16)
        count = x[6, 0, here]
        count_e = jnp.minimum(count, jnp.where(lane16 == CX - 1, 0.0, roll(count, -1, 1)))
        count_n = jnp.minimum(count, next_row(x.at[6, 0], p))
        sums = [0.0] * 4
        for l in range(2):
            thick = x[l, 0, here]
            de = jnp.where(first + l < count_e, 0.5 * (thick + roll(thick, -1, 1)), 0.0)
            dn = jnp.where(first + l < count_n, 0.5 * (thick + next_row(x.at[l, 0], p)), 0.0)
            new = [de, dn, x[2 + l, 0, here] * de, x[4 + l, 0, here] * dn]
            sums = [a + b for a, b in zip(sums, new)]
        for f in range(4):
            main_send[p // 2, p % 2, 16 * f : 16 * f + 16] = sums[f]

    @pl.when(inner)
    def _():
        pl.semaphore_wait(barrier, 8 + ND - 1)

    @pl.when(jnp.logical_not(inner))
    def _():
        pl.semaphore_wait(barrier, 5 + ND - 1)

    def halo(phase, source, target, dx, dy):
        sem = sent if phase == 0 else sent_late
        remote(source, target, sem, halo_got.at[phase], beside(dx, dy)).start()

    halo(0, side_pack.at[0, 0], side_in.at[0, 0], 1, 0)
    halo(0, side_pack.at[0, 1], side_in.at[0, 1], -1, 0)

    @pl.when(has_n)
    def _():
        halo(0, corner_pack.at[0, 1], corner_in.at[0], 1, 1)
        halo(0, corner_pack.at[1, 1], corner_in.at[1], -1, 1)
        halo(0, x.at[:, 0, END - 8 : END], x.at[:, 0, LOW:OWN], 0, 1)

    @pl.when(has_s)
    def _():
        halo(0, corner_pack.at[0, 0], corner_in.at[2], 1, -1)
        halo(0, corner_pack.at[1, 0], corner_in.at[3], -1, -1)
        halo(0, x.at[:, 0, OWN : OWN + 8], x.at[:, 0, END:HIGH], 0, -1)

    remote(main_send.at[:, other], pair_in, sent, pair_got, member(partner)).start()

    fetch_c.wait()
    rows_c = slice(8, CY + 8)

    def send_tracers(i):
        part = (slice(0, 3), slice(3, 4), slice(4, NTR))[i]

        @pl.when(me > 0)
        def _():
            remote(
                c.at[part, 0, rows_c], below.at[part], up_sent, up_got, member((me + ND - 1) % ND)
            ).start()

        @pl.when(me < ND - 1)
        def _():
            remote(
                c.at[part, 1, rows_c], above.at[part], down_sent, down_got, member((me + 1) % ND)
            ).start()

    send_tracers(0)

    got(pair_got, 256)
    chips = [(chip + k) % 4 for k in (2, 1, 3)]
    far_first = [(me + k) % ND for k in (4, 5, 3, 2, 6, 7, 1)]
    for q in range(4):
        chip_sum[q] = main_send[q, core] + pair_in[q]
    for q in chips:
        remote(chip_sum.at[q], main_in.at[chip], sent, rs_got, member(2 * q + core)).start()

    send_tracers(1)

    def pack_more(low, shift, east, west):
        old = state[1, 0, OWN + low : OWN + low + 8]
        east = jnp.where(between(lane8, shift + 24, shift + 32), roll(old, 40 + shift, 1), east)
        for p in range(2 * NTR):
            plane = c[p // 2, p % 2, 8 + low : 16 + low]
            west = jnp.where(lane8 == shift + 48 + p, roll(plane, shift + 48 + p, 1), west)
            east = jnp.where(lane8 == shift + 49 + p, roll(plane, shift + 50 + p, 1), east)
        return east, west

    pack_sides(1, late, pack_more)

    halo(1, side_pack.at[1, 0], side_in.at[1, 0], 1, 0)
    halo(1, side_pack.at[1, 1], side_in.at[1, 1], -1, 0)

    @pl.when(has_n)
    def _():
        halo(1, state.at[:, 0, END - 16 : END], state.at[:, 0, 0:OWN], 0, 1)
        halo(1, c.at[:, :, CY : CY + 8], c.at[:, :, 0:8], 0, 1)

    @pl.when(has_s)
    def _():
        halo(1, state.at[:, 0, OWN : OWN + 8], state.at[:, 0, END:HIGH], 0, -1)
        halo(1, c.at[:, :, 8:16], c.at[:, :, CY + 8 : CY + 16], 0, -1)

    @pl.when(me == 0)
    def _():
        above[...] = jnp.zeros_like(above)

    @pl.when(me == ND - 1)
    def _():
        below[...] = jnp.zeros_like(below)

    for ref in (x, state):
        for k in range(2):
            ref[:, k, HIGH:RX] = jnp.zeros((ref.shape[0], RX - HIGH, CX), F32)
    state[2, 1, 0:LOW] = jnp.zeros((LOW, CX), F32)
    state_b[2, :, 0:LOW] = jnp.zeros((2, LOW, CX), F32)

    def unpack_sides(phase, fields, extra=None):
        side = (lane8 < 8) | (lane8 >= CX - 8)
        for i in range(-1, 17):
            if i < 0:
                west, east, shift, ok = corner_in[0], corner_in[1], 56 * phase, side & has_s
            elif i == 16:
                west, east, shift, ok = corner_in[2], corner_in[3], 56 * phase, side & has_n
            else:
                j = 8 * (i % 8)
                west, east = side_in[phase, 0, j : j + 8], side_in[phase, 1, j : j + 8]
                shift, ok = 64 * (i // 8), side
            low = OWN + 8 * i
            for f, ref in enumerate(fields):
                start = shift + 8 * f + 8
                value = roll(jnp.where(between(lane8, start, start + 8), east, west), -start, 1)
                value = jnp.where(ok, value, 0.0)
                if extra is not None and f == 1 and 0 <= i < 16:
                    value = jnp.where(lane8 == CX - 9, roll(west, 88 - shift, 1), value)
                ref[low : low + 8] = value
            if extra is not None and 0 <= i < 16:
                extra(8 * i, shift, west, east)

    @pl.when(inner)
    def _():
        got(halo_got.at[0], 272)

    @pl.when(jnp.logical_not(inner))
    def _():
        got(halo_got.at[0], 200)

    unpack_sides(0, [x.at[f, 1] for f in range(7)])

    @pl.when(jnp.logical_not(has_s))
    def _():
        x[:, 0, LOW:OWN] = jnp.zeros((7, 8, CX), F32)

    @pl.when(jnp.logical_not(has_n))
    def _():
        x[:, 0, END:HIGH] = jnp.zeros((7, 8, CX), F32)

    def shifted(pair, steps):
        lane = lanes(pair[0].shape[0])
        edge = lane == (0 if steps > 0 else CX - 1)
        main, side = (roll(value, steps, 1) for value in pair)
        return jnp.where(edge, side, main), jnp.where(edge, main, side)

    def both(ref, low, size):
        return ref[0, low : low + size], ref[1, low : low + size]

    step = 24
    for low in range(LOW, HIGH, step):
        here = slice(low, low + step)
        count = both(x.at[6], low, step)
        count_e = shifted(count, -1)
        count_n = both(x.at[6], low + 1, step)
        thick = [both(x.at[l], low, step) for l in range(2)]
        thick_e = [shifted(thick[l], -1) for l in range(2)]
        for k in range(2):
            min_e = jnp.minimum(count[k], count_e[k])
            min_n = jnp.minimum(count[k], count_n[k])
            sums = [0.0] * 4
            for l in range(2):
                north = x[l, k, low + 1 : low + 1 + step]
                de = jnp.where(first + l < min_e, 0.5 * (thick[l][k] + thick_e[l][k]), 0.0)
                dn = jnp.where(first + l < min_n, 0.5 * (thick[l][k] + north), 0.0)
                face_e[l, k, here] = de
                face_n[l, k, here] = dn
                new = [de, dn, x[2 + l, k, here] * de, x[4 + l, k, here] * dn]
                sums = [a + b for a, b in zip(sums, new)]
            for f in range(4):
                local[f, k, here] = sums[f]

    def put_block(i, block):
        edge_send[i // EB, 8 * (i % EB) : 8 * (i % EB) + 8] = block

    for i in range(9):
        block = jnp.zeros((8, CX), F32)
        for j in range(2):
            low = LOW + 72 * j + 8 * i
            for f in range(4):
                start = 64 * j + 16 * f
                block = jnp.where(
                    lane8 == start, roll(local[f, 0, low : low + 8], start + 1, 1), block
                )
                block = jnp.where(
                    between(lane8, start + 1, start + 16),
                    roll(local[f, 1, low : low + 8], start + 9, 1),
                    block,
                )
        put_block(i, block)
    for f in range(4):
        put_block(9 + f, local[f, 0, END - 1 : END + 7])
        put_block(13 + f, local[f, 0, LOW:OWN])
    for i in range(17, NE * EB):
        put_block(i, jnp.zeros((8, CX), F32))

    owner = core == 0

    @pl.when(owner)
    def _():
        for q in chips:
            remote(edge_send.at[q], edge_in.at[me], edge_sent, edge_got, member(2 * q)).start()

    @pl.when(jnp.logical_not(owner))
    def _():
        for q in chips + [chip]:
            remote(edge_send.at[q], edge_in.at[me], edge_sent, edge_got, member(2 * q)).start()

    got(rs_got, 192)
    mine = chip_sum[chip]
    for q in chips:
        mine = mine + main_in[q]
    main_all[chip, core] = mine
    piece = main_all.at[chip, core]
    for q in chips:
        remote(piece, piece, sent, ag_got, member(2 * q + core)).start()

    for i in range(4):
        low = OWN + 32 * i
        here = slice(low, low + 32)
        flux = both(local.at[2], low, 32)
        value = flux[0] - shifted(flux, 1)[0] + local[3, 0, here] - local[3, 0, low - 1 : low + 31]
        outer_send[i // 2, 32 * (i % 2) : 32 * (i % 2) + 32] = value
    for j in range(2):
        low = OWN + 64 * j
        outer_send[j, 64:128] = local[0, 0, low : low + 64]
        outer_send[j, 128:200] = local[1, 0, low - 8 : low + 64]
        block = jnp.zeros((8, CX), F32)
        for r in range(8):
            turned = roll(local[0, 1, low + 8 * r : low + 8 * r + 8], r + 1, 1)
            block = jnp.where(lane8 == r, turned, block)
        outer_send[j, 200:208] = block
    remote(outer_send, outer_pair, outer_sent, half_got, member(partner)).start()

    @pl.when(inner)
    def _():
        got(halo_got.at[1], 392)
        left(sent_late, 392)

    @pl.when(jnp.logical_not(has_s))
    def _():
        got(halo_got.at[1], 248)
        left(sent_late, 272)

    @pl.when(jnp.logical_not(has_n))
    def _():
        got(halo_got.at[1], 272)
        left(sent_late, 248)


    def put_tracers(low, shift, west, east):
        for p in range(2 * NTR):
            value = jnp.where(lane8 <= shift + 48 + p, east, west)
            edge_c[p // 2, p % 2, low : low + 8] = roll(value, 79 - shift - p, 1)

    unpack_sides(1, [state.at[f, 1] for f in range(3)], put_tracers)

    @pl.when(jnp.logical_not(has_s))
    def _():
        state[:, 0, 0:OWN] = jnp.zeros((3, OWN, CX), F32)
        c[:, :, 0:8] = jnp.zeros((NTR, 2, 8, CX), F32)

    @pl.when(jnp.logical_not(has_n))
    def _():
        state[:, 0, END:HIGH] = jnp.zeros((3, 8, CX), F32)
        c[:, :, CY + 8 : CY + 16] = jnp.zeros((NTR, 2, 8, CX), F32)

    for low in range(LOW, HIGH, step):
        here = slice(low, low + step)
        is_wet = [jnp.where(value > 0.0, 1.0, 0.0) for value in both(x.at[6], low, step)]
        wet_e = shifted(is_wet, -1)
        wet_n = [jnp.where(value > 0.0, 1.0, 0.0) for value in both(x.at[6], low + 1, step)]
        for k in range(2):
            tw[k, here] = tau * is_wet[k]
            ae[k, here] = (1.0 - tau) * (is_wet[k] * wet_e[k])
            an[k, here] = (1.0 - tau) * (is_wet[k] * wet_n[k])
            wet_e_all[k, here] = (tau * coupling) * (is_wet[k] * wet_e[k])
            wet_n_all[k, here] = (tau * coupling) * (is_wet[k] * wet_n[k])

    @pl.when(owner)
    def _():
        got(edge_got, 7 * 8 * EB)
        edge = edge_send[chip]
        for peer in peers:
            edge = edge + edge_in[peer]
        edge_all[chip] = edge
        for peer in far_first:
            remote(edge_all.at[chip], edge_all.at[chip], edge_sent, edge_all_got, member(peer)).start()

    @pl.when(outer)
    def _():
        got(half_got, 416)
        outer_sum[...] = outer_send[core] + outer_pair[core]
        middle_chip = jnp.where(upper, 2, ND - 4)
        remote(outer_sum, outer_in, outer_sent, outer_got, member(middle_chip + core)).start()

    send_tracers(2)

    got(ag_got, 192)
    half = main_all.at[:, core]
    remote(half, half, sent, forward_got, member(partner)).start()

    @pl.when(owner)
    def _():
        got(edge_all_got, 3 * 8 * EB)

    @pl.when(jnp.logical_not(owner))
    def _():
        got(edge_all_got, 4 * 8 * EB)

    got(forward_got, 256)

    def block_of(i):
        return edge_all[i // EB, 8 * (i % EB) : 8 * (i % EB) + 8]

    rim = (lane8 < 7) | (lane8 >= CX - 8)
    last_lane = lane8 == CX - 1
    row8 = rows_of(8)
    for i in range(18):
        block = block_of(i % 9)
        shift = 64 * (i // 9)
        here = slice(LOW + 8 * i, LOW + 8 * i + 8)
        sums = []
        for f in range(4):
            if i == 0:
                main = block_of(13 + f)
            elif i == 17:
                main = jnp.where(row8 == 7, 0.0, roll(block_of(9 + f), -1, 0))
            else:
                p, part_low = (i - 1) // 2, 16 * f + 8 * ((i - 1) % 2)
                main = main_all[p // 2, p % 2, part_low : part_low + 8]
                if i == 16:
                    main = jnp.where(row8 == 7, jnp.broadcast_to(block_of(9 + f)[0:1], (8, CX)), main)
            main = jnp.where(last_lane, roll(block, CX - 1 - 16 * f - shift, 1), main)
            side = jnp.where(rim, roll(block, -(9 + 16 * f + shift), 1), 0.0)
            total[f, 0, here] = main
            total[f, 1, here] = side
            sums.append((main, side))
        for k in range(2):
            east, north = wet_e_all[k, here], wet_n_all[k, here]
            be[k, here] = east * sums[0][k]
            bn[k, here] = north * sums[1][k]
            ce[k, here] = east * sums[2][k]
            cn[k, here] = north * sums[3][k]

    def substep(old, new):
        bottom_row = rows_of(step) == step - 1

        def rise(low):
            here = slice(low, low + step)
            east = both(old.at[1], low, step)
            west = shifted(east, 1)
            north = both(old.at[2], low, step)
            south = both(old.at[2], low - 1, step)
            level = []
            for k in range(2):
                value = old[0, k, here] - tw[k, here] * (east[k] - west[k] + north[k] - south[k])
                new[0, k, here] = value
                level.append(value)
            return level, east, north

        def move(low, held, beyond):
            here = slice(low, low + step)
            level, east, north = held
            level_e = shifted(level, -1)
            for k in range(2):
                level_n = roll(level[k], -1, 0)
                if beyond is not None:
                    first_row = jnp.broadcast_to(beyond[0][k][0:1], (step, CX))
                    level_n = jnp.where(bottom_row, first_row, level_n)
                new[1, k, here] = ae[k, here] * east[k] - be[k, here] * (level_e[k] - level[k]) + ce[k, here]
                new[2, k, here] = an[k, here] * north[k] - bn[k, here] * (level_n - level[k]) + cn[k, here]

        held = rise(LOW)
        for low in range(LOW, HIGH, step):
            coming = rise(low + step) if low + step < HIGH else None
            move(low, held, coming)
            held = coming

    def two(i, carry):
        substep(state, state_b)
        substep(state_b, state)
        return carry

    lax.fori_loop(0, NSUB // 2 - 1, two, 0)

    @pl.when(jnp.logical_not(outer))
    def _():
        got(outer_got, 208)
        remote(outer_in, outer_next, sent, div_got, member(partner)).start()

    two(0, 0)

    flow_rows = [(OWN - 8, 8)] + [(OWN + 32 * i, 32) for i in range(4)]
    for low, size in flow_rows:
        here = slice(low, low + size)
        shift_n = state[2, 0, here] - coupling * total[3, 0, here]
        for l in range(2):
            flow_n[l, here] = face_n[l, 0, here] * (x[4 + l, 0, here] + shift_n)
        prod_n[here] = shift_n

    for i in range(4):
        low = OWN + 32 * i
        here = slice(low, low + 32)
        mine = slice(32 * i, 32 * i + 32)
        shift_e = [state[1, k, here] - coupling * total[2, k, here] for k in range(2)]
        divs = []
        for l in range(2):
            flow = [face_e[l, k, here] * (x[2 + l, k, here] + shift_e[k]) for k in range(2)]
            west = shifted(flow, 1)[0]
            flow_e[l, 0, mine] = flow[0]
            flow_e[l, 1, mine] = west
            divs.append(flow[0] - west + flow_n[l, here] - flow_n[l, low - 1 : low + 31])
        div_1[mine] = divs[1]
        pair_send[mine] = divs[0] + divs[1]

    def divergence_of(parts, base):
        here = pl.ds(base, 64)
        shift_e = [state[1, k, here] - coupling * total[2, k, here] for k in range(2)]
        flow = parts[64:128] * shift_e[0]
        block = parts[200:208]
        column = jnp.concatenate([roll(block, -r, 1) for r in range(8)], axis=0)
        west = jnp.where(lanes(64) == 0, column * roll(shift_e[1], 1, 1), roll(flow, 1, 1))
        flow_t[0:72] = parts[128:200] * prod_n[pl.ds(base - 8, 72)]
        return parts[0:64] + flow - west + flow_t[8:72] - flow_t[7:71]

    @pl.when(jnp.logical_not(outer))
    def _():
        got(half_got, 416)
        outer_div[core] = divergence_of(outer_in, pl.multiple_of(OWN + 64 * core, 8))

    @pl.when(outer)
    def _():
        outer_div[...] = jnp.zeros_like(outer_div)

    for j in range(2):
        pair_div[64 * j : 64 * j + 64] = divergence_of(outer_pair.at[j], OWN + 64 * j)

    for low, size in flow_rows:
        here = slice(low, low + size)
        flow_w[here] = total[3, 0, here] + total[1, 0, here] * prod_n[here]

    for i in range(4):
        low = OWN + 32 * i
        here = slice(low, low + 32)
        mine = slice(32 * i, 32 * i + 32)
        shift_e = [state[1, k, here] - coupling * total[2, k, here] for k in range(2)]
        flow = [total[2, k, here] + total[0, k, here] * shift_e[k] for k in range(2)]
        whole_div[mine] = flow[0] - shifted(flow, 1)[0] + flow_w[here] - flow_w[low - 1 : low + 31]
        count = x[6, 0, here]
        for l in range(2):
            fe, fw = flow_e[l, 0, mine], flow_e[l, 1, mine]
            fn, fs = flow_n[l, here], flow_n[l, low - 1 : low + 31]
            gain = jnp.where(first + l < count, tracer_time / x[l, 0, here], 0.0)
            plus_e, minus_w = jnp.maximum(fe, 0.0), jnp.minimum(fw, 0.0)
            plus_n, minus_s = jnp.maximum(fn, 0.0), jnp.minimum(fs, 0.0)
            coef[l, 0, mine] = gain * (plus_e - fe)
            coef[l, 1, mine] = gain * (fw - minus_w)
            coef[l, 2, mine] = gain * (plus_n - fn)
            coef[l, 3, mine] = gain * (fs - minus_s)
            coef[l, 4, mine] = 1.0 - gain * (plus_e - minus_w + plus_n - minus_s)
            coef[l, 5, mine] = gain

    s_out[0] = state[0, 0, rows_own]
    e_out[0] = state[1, 0, rows_own]
    n_out[0] = state[2, 0, rows_own]

    lane32 = lanes(32)
    for l in range(2):
        for i in range(4):
            mine = slice(32 * i, 32 * i + 32)
            low = 8 + 32 * i
            a_e, a_w, a_n, a_s, a_c = (coef[l, j, mine] for j in range(5))
            for m in range(NTR):
                value = c[m, l, low : low + 32]
                edge = edge_c[m, l, mine]
                value_e = jnp.where(lane32 == CX - 1, edge, roll(value, -1, 1))
                value_w = jnp.where(lane32 == 0, edge, roll(value, 1, 1))
                part[m, l, mine] = (
                    a_c * value
                    + a_e * value_e
                    + a_w * value_w
                    + a_n * c[m, l, low + 1 : low + 33]
                    + a_s * c[m, l, low - 1 : low + 31]
                )

    halos_sent = [(inner, 272), (jnp.logical_not(inner), 200)]
    for where, rows in halos_sent:
        @pl.when(where & outer)
        def _(rows=rows):
            left(sent, rows + 896)

        @pl.when(where & jnp.logical_not(outer))
        def _(rows=rows):
            left(sent, rows + 1104)

    @pl.when(owner)
    def _():
        left(edge_sent, 10 * 8 * EB)

    @pl.when(jnp.logical_not(owner))
    def _():
        left(edge_sent, 4 * 8 * EB)

    @pl.when(outer)
    def _():
        left(outer_sent, 624)

    @pl.when(jnp.logical_not(outer))
    def _():
        left(outer_sent, 416)
        got(div_got, 208)
        outer_div[other] = divergence_of(outer_next, pl.multiple_of(OWN + 64 * other, 8))

    odd = core == 1
    for i in range(4):
        mine = slice(32 * i, 32 * i + 32)
        beyond = outer_div[i // 2, 32 * (i % 2) : 32 * (i % 2) + 32]
        near = pair_div[mine]
        here = pair_send[mine]
        deeper = jnp.where(
            upper,
            whole_div[mine] - here - beyond - jnp.where(odd, near, 0.0),
            beyond + jnp.where(odd, 0.0, near),
        )
        bottom = -deeper
        middle = -(div_1[mine] + deeper)
        top = jnp.where(me == 0, 0.0, -(here + deeper))
        for l in range(2):
            under_flow, over_flow = (middle, top) if l == 0 else (bottom, middle)
            gain = coef[l, 5, mine]
            lift[l, 0, mine] = gain * (jnp.minimum(under_flow, 0.0) - jnp.maximum(over_flow, 0.0))
            lift[l, 1, mine] = gain * jnp.maximum(under_flow, 0.0)
            lift[l, 2, mine] = -gain * jnp.minimum(over_flow, 0.0)

    @pl.when(me < ND - 1)
    def _():
        got(up_got, NTR * CY)
        left(down_sent, NTR * CY)

    @pl.when(me > 0)
    def _():
        got(down_got, NTR * CY)
        left(up_sent, NTR * CY)


def store(part, s_ref, e_ref, n_ref, c, below, above, lift, c_out, s_out, e_out, n_out, new_c, sem):
    copies = [
        pltpu.make_async_copy(source, target, sem.at[NTR + i])
        for i, (source, target) in enumerate([(s_ref, s_out), (e_ref, e_out), (n_ref, n_out)])
    ]
    for copy in copies:
        copy.start()
    for pair in range(0, NTR, 2):
        for l in range(2):
            for i in range(4):
                mine = slice(32 * i, 32 * i + 32)
                low = 8 + 32 * i
                a_c, a_b, a_a = (lift[l, j, mine] for j in range(3))
                for m in (pair, pair + 1):
                    under = c[m, 1, low : low + 32] if l == 0 else below[m, mine]
                    over = above[m, mine] if l == 0 else c[m, 0, low : low + 32]
                    new_c[m, l, mine] = (
                        part[m, l, mine] + a_c * c[m, l, low : low + 32] + a_b * under + a_a * over
                    )
        for m in (pair, pair + 1):
            copy = pltpu.make_async_copy(new_c.at[m], c_out.at[m, :, 0], sem.at[m])
            copy.start()
            copies.append(copy)
    for copy in copies:
        copy.wait()


def body(thickness, u_layer, v_layer, tracers, sea_level, u_column, v_column, wet_cells, levels):
    any_spec = pl.BlockSpec(memory_space=pl.ANY)
    near_spec = pl.BlockSpec(memory_space=pltpu.VMEM)

    def vmem(*shape):
        return pltpu.VMEM(shape, F32)

    plane = vmem(CY, CX)
    wide = vmem(2, RX, CX)
    wide2 = vmem(2, 2, RX, CX)
    column_c = vmem(NTR, CY, CX)
    flat = pltpu.VMEM((CY, CX), jnp.int32)
    quarter = vmem(4, 64, CX)
    halves = vmem(4, 2, 64, CX)
    edges = vmem(NE, 8 * EB, CX)
    dma = pltpu.SemaphoreType.DMA
    shapes = [tracers.shape] + [sea_level.shape] * 3
    results = pl.pallas_call(
        kernel,
        out_shape=(
            vmem(NTR, 2, CY, CX), *(pltpu.VMEM(shape, F32) for shape in shapes[1:]),
            vmem(NTR, 2, CY + 16, CX), column_c, column_c, vmem(2, 3, CY, CX),
        ),
        in_specs=[pl.BlockSpec(memory_space=pltpu.HBM)] * 9,
        out_specs=(near_spec,) * 8,
        scratch_shapes=[
            vmem(7, 2, RX, CX), vmem(3, 2, RX, CX), flat, flat,
            vmem(2, 2, 64, CX), vmem(2, 2, 64, CX), vmem(2, 2, 8, CX), vmem(4, 8, CX), vmem(11 * CY, CX),
            vmem(NTR, 2, CY, CX),
            halves, quarter, quarter, quarter, halves,
            edges, vmem(ND, 8 * EB, CX), edges,
            wide2, wide2, vmem(4, 2, RX, CX), vmem(4, 2, RX, CX),
            wide, wide, wide, wide, wide, wide, wide, wide, wide, vmem(3, 2, RX, CX),
            vmem(2, 208, CX), vmem(2, 208, CX), vmem(208, CX), vmem(208, CX), vmem(208, CX), vmem(2, 64, CX),
            vmem(2, RX, CX), vmem(RX, CX), vmem(RX, CX), vmem(2, 2, CY, CX), vmem(RX, CX), vmem(2, 6, CY, CX),
            plane, plane, plane, plane,
            dma((2,)), dma, dma, dma, dma, dma, dma,
            dma((2,)), dma, dma, dma, dma, dma, dma, dma, dma,
            dma, dma, dma,
        ],
        compiler_params=pltpu.CompilerParams(
            collective_id=0, has_side_effects=True, vmem_limit_bytes=48 * 1024 * 1024
        ),
    )(*[
        pltpu.with_memory_space_constraint(x, pltpu.HBM)
        for x in (thickness, u_layer, v_layer, tracers, sea_level, u_column, v_column, wet_cells, levels)
    ])
    return pl.pallas_call(
        store,
        out_shape=tuple(jax.ShapeDtypeStruct(shape, F32) for shape in shapes),
        in_specs=[near_spec] * 8,
        out_specs=(any_spec,) * 4,
        scratch_shapes=[vmem(NTR, 2, CY, CX), dma((NTR + 3,))],
    )(*[pltpu.with_memory_space_constraint(x, pltpu.VMEM) for x in results])


def solution(mesh):
    return jax.shard_map(
        body,
        mesh=mesh,
        in_specs=(
            P("depth", "tiles", None, None),
            P("depth", "tiles", None, None),
            P("depth", "tiles", None, None),
            P(None, "depth", "tiles", None, None),
            P("tiles", None, None),
            P("tiles", None, None),
            P("tiles", None, None),
            P("tiles", None, None),
            P("tiles", None, None),
        ),
        out_specs=(
            P(None, "depth", "tiles", None, None),
            P("tiles", None, None),
            P("tiles", None, None),
            P("tiles", None, None),
        ),
        check_vma=False,
    )
```
